128 devices in a mesh: dp: 8 (over y_hi, z), mp: 16 (over x, y_lo, core).
Axes of the slice: x: 4, y: 4 (y_hi: 2, y_lo: 2; y = y_hi * 2 + y_lo), z: 4, core: 2. Of those that a mesh axis runs over, the one named last changes fastest.
Arguments:
- z_a: float32 [1024, 16384], P('dp', 'mp'), may hold values from -60 to 60
- z_b: float32 [1024, 16384], P('dp', 'mp'), may hold values from -60 to 60
Outputs:
- dz_a: float32 [1024, 16384], P('dp', 'mp')
- dz_b: float32 [1024, 16384], P('dp', 'mp')
The draws below stay inside these ranges and needn't reach their ends.
All inputs are finite; a program needn't handle non-finite values.
Results may differ from the reference program's by a relative error of at most 0.0054.
Values may be sent and summed in bfloat16 or wider, within the bound.
A program may use at most 192 MiB of HBM per device.

```python
import math
import jax
import jax.numpy as jnp
from jax import lax

F = 16384
ROWS = 1024
N_MP = 16


def common_field(key):
    key_rows, key_cols, key_offset, key_normal = jax.random.split(key, 4)
    position = jnp.arange(ROWS, dtype=jnp.float32) / max(ROWS - 1, 1)
    row_drift = jnp.exp(math.log(3.0) * (position - 0.5))
    row_scale = row_drift * jnp.exp(jax.random.uniform(key_rows, (ROWS,), jnp.float32, math.log(0.5), math.log(2.0)))
    col_scale = jnp.exp(jax.random.uniform(key_cols, (F,), jnp.float32, math.log(0.3), math.log(3.0)))
    offset = 0.5 * col_scale * jax.random.truncated_normal(key_offset, -4.0, 4.0, (F,), jnp.float32)
    normal_part = jax.random.truncated_normal(key_normal, -4.0, 4.0, (ROWS, F), jnp.float32)
    base_noise = normal_part
    return (offset, row_scale, col_scale, base_noise)


def draw_z_a(key, part):
    offset, row_scale, col_scale, base_noise = common_field(key)
    return offset[None, :] + row_scale[:, None] * col_scale[None, :] * base_noise


def draw_z_b(key, part):
    offset, row_scale, col_scale, base_noise = common_field(key)
    key = jax.random.fold_in(key, 12)
    extra_noise = jax.random.truncated_normal(key, -4.0, 4.0, (ROWS, F), jnp.float32)
    return offset[None, :] + row_scale[:, None] * col_scale[None, :] * (base_noise + 0.1 * extra_noise)


def setup_inputs(seed: int = 0) -> dict:
    streams_of = jax.random.split(jax.random.key(seed), 3)
    z_a = draw_z_a(jax.random.fold_in(streams_of[2], 71), 0)
    z_b = draw_z_b(jax.random.fold_in(streams_of[2], 71), 0)
    return {"z_a": z_a, "z_b": z_b}


INVARIANCE_WEIGHT = 25.0
VARIANCE_WEIGHT = 25.0
DEVIATION_FLOOR = 0.0001
HUBER_EDGE = 0.05

def view_terms(projected):
    row_total = projected.shape[0]
    column_average = lax.optimization_barrier(jnp.sum(projected, axis=0)) / row_total
    centered = projected - column_average
    spread_squared = lax.optimization_barrier(jnp.sum(centered * centered, axis=0)) / (row_total - 1)
    spread = jnp.sqrt(spread_squared + DEVIATION_FLOOR)
    var_term = jnp.where(spread < 1.0, -(VARIANCE_WEIGHT * row_total / (2.0 * (row_total - 1))) / spread, 0.0) * centered
    centered_bf = centered.astype(jnp.bfloat16)
    widened = lax.optimization_barrier(centered_bf).astype(jnp.float32)
    block_cols = F // N_MP
    scaling = 2.0 * row_total / (row_total - 1.0)

    def one_block(block_index):
        col_start = (block_index * block_cols).astype(jnp.int32)
        column_part = lax.dynamic_slice_in_dim(widened, col_start, block_cols, 1)
        gram_block = jnp.dot(widened.T, column_part, preferred_element_type=jnp.float32)
        row_ids = jnp.arange(F, dtype=jnp.int32)[:, None]
        col_ids = col_start + jnp.arange(block_cols, dtype=jnp.int32)[None, :]
        clipped = jnp.clip(gram_block / (row_total - 1.0), -HUBER_EDGE, HUBER_EDGE)
        clipped = jnp.where(row_ids == col_ids, 0.0, clipped)
        weight_q = (scaling * clipped).astype(jnp.bfloat16)
        weight_wide = lax.optimization_barrier(weight_q).astype(jnp.float32)
        return jnp.dot(widened, weight_wide, preferred_element_type=jnp.float32)
    pieces = lax.map(one_block, jnp.arange(N_MP, dtype=jnp.int32))
    covariance_term = jnp.transpose(pieces, (1, 0, 2)).reshape(row_total, F)
    return var_term + covariance_term

def reference(z_a, z_b):
    difference = INVARIANCE_WEIGHT * (z_a - z_b)
    dz_a = difference + view_terms(z_a)
    dz_b = view_terms(z_b) - difference
    return (dz_a, dz_b)
```

```python
import jax
import jax.numpy as jnp
from jax import lax
from jax.experimental import pallas as pl
from jax.experimental.pallas import tpu as pltpu
from jax.sharding import PartitionSpec as P

INVARIANCE_WEIGHT = 25.0
VARIANCE_WEIGHT = 25.0
DEVIATION_FLOOR = 0.0001
HUBER_EDGE = 0.05

MESH = pl.DeviceIdType.MESH
F32 = jnp.float32
BF16 = jnp.bfloat16
N_COPIES = 120


def kernel(za, zb, out_a, out_b, stats, zi, stage, jt, wt, part_out, part_in, own, rows_out, rows_in, ss, rs):
    dp = lax.axis_index("dp")
    mp = lax.axis_index("mp")
    yh, z = dp // 4, dp % 4
    x, yl, c = mp // 4, (mp // 2) % 2, mp % 2
    local_rows, cols = za.shape
    chunk = cols // 4
    n_rows = local_rows * 8

    def dev(yh_=None, z_=None, x_=None, yl_=None, c_=None):
        yh_ = yh if yh_ is None else yh_
        z_ = z if z_ is None else z_
        x_ = x if x_ is None else x_
        yl_ = yl if yl_ is None else yl_
        c_ = c if c_ is None else c_
        return (yh_ * 4 + z_, x_ * 4 + yl_ * 2 + c_)

    def plus(v, k):
        return (v + (k % 4)) % 4

    sent = []

    def copy(src, dst, device):
        i = len(sent)
        cp = pltpu.make_async_remote_copy(
            src_ref=src, dst_ref=dst, send_sem=ss.at[i], recv_sem=rs.at[i], device_id=device, device_id_type=MESH
        )
        cp.start()
        sent.append(cp)
        return cp

    zl, zr, xl, xr = plus(z, -1), plus(z, 1), plus(x, -1), plus(x, 1)
    oyh, oyl, oc = 1 - yh, 1 - yl, 1 - c
    dp_peers = [(a, b) for a in range(2) for b in range(4) if a or b]

    def peer(a, b):
        return oyh if a else yh, plus(z, b)

    partners = [dev(yh_=peer(a, b)[0], z_=peer(a, b)[1]) for a, b in dp_peers]
    partners += [dev(yl_=oyl), dev(yh_=oyh, yl_=oyl), dev(x_=xl), dev(x_=xr), dev(c_=oc)]
    barrier = pltpu.get_barrier_semaphore()
    for partner in partners:
        pl.semaphore_signal(barrier, inc=1, device_id=partner, device_id_type=MESH)

    for v, ref in enumerate((za, zb)):
        total = jnp.sum(ref[...], axis=0, keepdims=True)
        shifted = ref[...] - total * (1.0 / local_rows)
        stats[dp, v : v + 1, :] = total
        stats[dp, v + 2 : v + 3, :] = jnp.sum(shifted * shifted, axis=0, keepdims=True)
    pl.semaphore_wait(barrier, len(partners))
    cps = [copy(stats.at[dp], stats.at[dp], dev(yh_=peer(a, b)[0], z_=peer(a, b)[1])) for a, b in dp_peers]
    for cp in cps:
        cp.wait_recv()

    totals = jnp.zeros((2, cols), F32)
    for d in range(8):
        totals = totals + stats[d, 0:2, :]
    mean = totals * (1.0 / n_rows)
    squares = jnp.zeros((2, cols), F32)
    for d in range(8):
        gap = stats[d, 0:2, :] * (1.0 / local_rows) - mean
        squares = squares + (stats[d, 2:4, :] + local_rows * (gap * gap))
    spread = jnp.sqrt(squares / (n_rows - 1) + DEVIATION_FLOOR)
    pull = jnp.where(spread < 1.0, -(VARIANCE_WEIGHT * n_rows / (2.0 * (n_rows - 1))) / spread, 0.0)

    first = yh == 0
    for f in range(4):
        cut = slice(f * chunk, (f + 1) * chunk)
        ca = (za[:, cut] - mean[0:1, cut]).astype(BF16)
        cb = (zb[:, cut] - mean[1:2, cut]).astype(BF16)
        zi[f, c, yl, z, yh] = jnp.where(first, ca, cb)
        stage[f] = jnp.where(first, cb, ca)

    order = [plus(z, 1), plus(z, -1), plus(z, 2), z]
    y_copies = []
    for f in order:
        here = zi.at[f, c, yl, z, yh]
        y_copies.append(
            [
                copy(here, here, dev(yl_=oyl)),
                copy(stage.at[f], here, dev(yh_=oyh, yl_=oyl)),
                copy(stage.at[f], here, dev(yh_=oyh)),
            ]
        )

    def shard_send(f, to):
        a = copy(zi.at[f, c, yl, z], zi.at[f, c, yl, z], dev(z_=to))
        b = copy(zi.at[f, c, oyl, z], zi.at[f, c, oyl, z], dev(z_=to))
        return a, b

    shares = []

    def share(ref):
        shares.append(copy(ref, ref, dev(c_=oc)))

    right, left = {}, {}
    right_f = [plus(z, k) for k in (1, 2, 3, 0)]
    left_f = [plus(z, k) for k in (-1, 2, 0, 1)]

    from_left_f = [plus(z, k) for k in (0, 1, 2, 3)]
    from_right_f = [plus(z, k) for k in (0, 3, 1, 2)]

    def wait_y(j):
        for cp in y_copies[j]:
            cp.wait_recv()
        share(zi.at[order[j], c, :, z])

    wait_y(0)
    right[0] = shard_send(right_f[0], zr)
    wait_y(1)
    left[0] = shard_send(left_f[0], zl)
    wait_y(2)
    right[1] = shard_send(right_f[1], zr)
    left[1] = shard_send(left_f[1], zl)
    wait_y(3)

    half = chunk // 2
    j_copies = {}

    def slab_send(q):
        zq = plus(z, q)
        block = zi[z, c, yl, zq].reshape(2 * local_rows, chunk)
        jt[zq, x] = block.T
        j_copies[q] = [copy(jt.at[zq, x], jt.at[zq, x], dev(x_=xr)), copy(jt.at[zq, x], jt.at[zq, x], dev(x_=xl))]

    j_fwd = []

    def slab_forward(q):
        zq = plus(z, q)
        for cp in j_copies[q]:
            cp.wait_recv()
        lo, hi = pl.ds(0, half), pl.ds(half, half)
        j_fwd.append(copy(jt.at[zq, xl, lo], jt.at[zq, xl, lo], dev(x_=xr)))
        j_fwd.append(copy(jt.at[zq, xr, hi], jt.at[zq, xr, hi], dev(x_=xl)))

    slab_send(0)

    difference = INVARIANCE_WEIGHT * (za[...] - zb[...])
    out_a[...] = difference + pull[0:1, :] * (za[...] - mean[0:1, :])
    out_b[...] = pull[1:2, :] * (zb[...] - mean[1:2, :]) - difference

    def forward_right(f):
        ref = zi.at[f, c, yl, zl, 0]
        return copy(ref, ref, dev(z_=zr))

    def forward_left(f):
        ref = zi.at[f, c, yl, zr, 1]
        return copy(ref, ref, dev(z_=zl))

    fr, fl = {}, {}
    z2 = plus(z, 2)

    right[0][0].wait_recv()
    fr[3] = forward_right(from_left_f[0])
    slab_send(-1)
    left[0][0].wait_recv()
    fl[1] = forward_left(from_right_f[0])
    slab_send(1)
    slab_forward(0)
    right[0][1].wait_recv()
    share(zi.at[from_left_f[0], c, :, zl])
    left[0][1].wait_recv()
    share(zi.at[from_right_f[0], c, :, zr])

    right[1][0].wait_recv()
    fr[0] = forward_right(from_left_f[1])
    right[2] = shard_send(right_f[2], zr)
    left[1][0].wait_recv()
    fl[0] = forward_left(from_right_f[1])
    left[2] = shard_send(left_f[2], zl)
    right[1][1].wait_recv()
    share(zi.at[from_left_f[1], c, :, zl])
    left[1][1].wait_recv()
    share(zi.at[from_right_f[1], c, :, zr])
    slab_forward(-1)
    slab_forward(1)

    across = {}

    def opposite(q):
        fr[q].wait_recv()
        fl[q].wait_recv()
        ref = zi.at[plus(z, q), c, yl, z2]
        across[q] = copy(ref, ref, dev(yl_=oyl))
        share(ref)

    def across_done(q):
        across[q].wait_recv()
        share(zi.at[plus(z, q), c, oyl, z2])

    opposite(0)
    slab_send(2)
    right[3] = shard_send(right_f[3], zr)
    left[3] = shard_send(left_f[3], zl)
    across_done(0)

    right[2][0].wait_recv()
    fr[1] = forward_right(from_left_f[2])
    left[2][0].wait_recv()
    fl[2] = forward_left(from_right_f[2])
    slab_forward(2)
    right[2][1].wait_recv()
    share(zi.at[from_left_f[2], c, :, zl])
    left[2][1].wait_recv()
    share(zi.at[from_right_f[2], c, :, zr])

    scale = 2.0 * n_rows / (n_rows - 1.0)
    slope = scale / (n_rows - 1.0)
    edge = HUBER_EDGE * scale

    def gram(f, cc, yy, first_part, parts):
        size = parts * chunk
        g = jnp.zeros((size, chunk), F32)
        for q in range(4):
            lhs = jt[q, pl.ds(first_part, parts)].reshape(size, chunk)
            rhs = zi[f, cc, yy, q].reshape(2 * local_rows, chunk)
            g = g + jnp.dot(lhs, rhs, preferred_element_type=F32)
        w = jnp.clip(g * slope, -edge, edge).astype(BF16)
        wt[f, cc, yy, pl.ds(first_part, parts)] = w.reshape(parts, chunk, chunk)

    def gram_blocks(f, yy):
        def body(i, carry):
            gram(f, i // 2, yy, (i % 2) * 2, 2)
            return carry

        lax.fori_loop(0, 4, body, 0)

    def gram_part(f, yy, part):
        def body(cc, carry):
            gram(f, cc, yy, part, 1)
            return carry

        lax.fori_loop(0, 2, body, 0)

    opposite(1)
    across_done(1)

    shared = iter(shares)

    n_seen = [0]

    def sibling(n):
        while n_seen[0] < n:
            next(shared).wait_recv()
            n_seen[0] += 1

    for cp in j_fwd:
        cp.wait_recv()
    sibling(10)
    gram_blocks(z, yl)
    gram_blocks(z, oyl)
    row_id = lax.broadcasted_iota(jnp.int32, (chunk, chunk), 0)
    col_id = lax.broadcasted_iota(jnp.int32, (chunk, chunk), 1)
    wt[z, c, yl, x] = jnp.where(row_id == col_id, jnp.zeros((), BF16), wt[z, c, yl, x])

    right[3][0].wait_recv()
    fr[2] = forward_right(from_left_f[3])
    left[3][0].wait_recv()
    fl[3] = forward_left(from_right_f[3])
    sibling(14)
    gram_blocks(plus(z, 1), yl)
    gram_blocks(plus(z, 1), oyl)
    right[3][1].wait_recv()
    share(zi.at[from_left_f[3], c, :, zl])
    left[3][1].wait_recv()
    share(zi.at[from_right_f[3], c, :, zr])
    opposite(2)
    opposite(3)
    sibling(18)
    gram_blocks(plus(z, 2), yl)
    gram_blocks(plus(z, 3), yl)
    across_done(2)
    across_done(3)
    sibling(20)
    x2 = plus(x, 2)
    gram_part(plus(z, 2), oyl, x2)
    gram_part(plus(z, 3), oyl, x2)

    def product(part, h):
        acc = jnp.zeros((4 * local_rows, chunk), F32)
        for f in range(4):
            for cc in range(2):
                for yy in range(2):
                    lhs = zi[f, cc, yy, 2 * h : 2 * h + 2].reshape(4 * local_rows, chunk)
                    acc = acc + lax.dot_general(
                        lhs, wt[f, cc, yy, part], (((1,), (1,)), ((), ())), preferred_element_type=F32
                    )
        return acc

    def send_part(slot, to, land):
        return copy(part_out.at[slot], part_in.at[land], dev(x_=to))

    part_out[0] = product(x2, 0).astype(BF16)
    r0 = send_part(0, xr, 0)
    part_out[1] = product(x2, 1).astype(BF16)
    l0 = send_part(1, xl, 3)
    for part in (xr, xl, x):
        gram_part(plus(z, 2), oyl, part)
        gram_part(plus(z, 3), oyl, part)
    part_out[2] = product(xr, 1).astype(BF16)
    r1 = send_part(2, xr, 1)
    part_out[3] = product(xl, 0).astype(BF16)
    l1 = send_part(3, xl, 4)
    acc = product(xr, 0)
    r0.wait_recv()
    part_out[4] = (acc + part_in[0].astype(F32)).astype(BF16)
    r2 = send_part(4, xr, 2)
    acc = product(xl, 1)
    l0.wait_recv()
    part_out[5] = (acc + part_in[3].astype(F32)).astype(BF16)
    l2 = send_part(5, xl, 5)
    own[0] = product(x, 0)
    own[1] = product(x, 1)
    r1.wait_recv()
    l1.wait_recv()
    own[0] = own[0] + part_in[4].astype(F32)
    own[1] = own[1] + part_in[1].astype(F32)
    r2.wait_recv()
    rows_out[0:2] = (own[0] + part_in[2].astype(F32)).astype(BF16).reshape(2, 2, local_rows, chunk)
    l2.wait_recv()
    rows_out[2:4] = (own[1] + part_in[5].astype(F32)).astype(BF16).reshape(2, 2, local_rows, chunk)

    back = []
    for a, b in dp_peers:
        pyh, pz = peer(a, b)
        back.append(copy(rows_out.at[pz, pyh], rows_in.at[yh, z], dev(yh_=pyh, z_=pz)))
    rows_in[yh, z] = rows_out[z, yh]
    for cp in back:
        cp.wait_recv()
    for f in range(4):
        cut = slice(f * chunk, (f + 1) * chunk)
        out_a[:, cut] = out_a[:, cut] + rows_in[0, f].astype(F32)
        out_b[:, cut] = out_b[:, cut] + rows_in[1, f].astype(F32)
    for cp in sent:
        cp.wait_send()


def on_device(z_a, z_b):
    rows, cols = z_a.shape
    chunk = cols // 4
    vmem = pl.BlockSpec(memory_space=pltpu.VMEM)
    return pl.pallas_call(
        kernel,
        out_shape=[jax.ShapeDtypeStruct((rows, cols), F32)] * 2,
        in_specs=[vmem, vmem],
        out_specs=[vmem, vmem],
        scratch_shapes=[
            pltpu.VMEM((8, 4, cols), F32),
            pltpu.VMEM((4, 2, 2, 4, 2, rows, chunk), BF16),
            pltpu.VMEM((4, rows, chunk), BF16),
            pltpu.VMEM((4, 4, chunk, 2 * rows), BF16),
            pltpu.VMEM((4, 2, 2, 4, chunk, chunk), BF16),
            pltpu.VMEM((6, 4 * rows, chunk), BF16),
            pltpu.VMEM((6, 4 * rows, chunk), BF16),
            pltpu.VMEM((2, 4 * rows, chunk), F32),
            pltpu.VMEM((4, 2, rows, chunk), BF16),
            pltpu.VMEM((2, 4, rows, chunk), BF16),
            pltpu.SemaphoreType.DMA((N_COPIES,)),
            pltpu.SemaphoreType.DMA((N_COPIES,)),
        ],
        compiler_params=pltpu.CompilerParams(collective_id=0, has_side_effects=True, vmem_limit_bytes=56 * 1024 * 1024),
        name="vicreg",
    )(z_a, z_b)


def solution(mesh):
    specs = (P("dp", "mp"), P("dp", "mp"))
    return jax.shard_map(on_device, mesh=mesh, in_specs=specs, out_specs=specs, check_vma=False)
```

```python
import jax
import jax.numpy as jnp
from jax import lax
from jax.experimental import pallas as pl
from jax.experimental.pallas import tpu as pltpu
from jax.sharding import PartitionSpec as P

INVARIANCE_WEIGHT = 25.0
VARIANCE_WEIGHT = 25.0
DEVIATION_FLOOR = 0.0001
HUBER_EDGE = 0.05

MESH = pl.DeviceIdType.MESH
F32 = jnp.float32
BF16 = jnp.bfloat16
N_COPIES = 128


def kernel(za_hbm, zb_hbm, cov, coefs, za, zb, stats, zi, stage, jt, wt, part_out, part_in, rows_out, rows_in, ls, ss, rs):
    dp = lax.axis_index("dp")
    mp = lax.axis_index("mp")
    yh, z = dp // 4, dp % 4
    x, yl, c = mp // 4, (mp // 2) % 2, mp % 2
    local_rows, cols = za.shape
    chunk = cols // 4
    n_rows = local_rows * 8
    pair = 2 * local_rows

    def dev(yh_=None, z_=None, x_=None, yl_=None, c_=None):
        yh_ = yh if yh_ is None else yh_
        z_ = z if z_ is None else z_
        x_ = x if x_ is None else x_
        yl_ = yl if yl_ is None else yl_
        c_ = c if c_ is None else c_
        return (yh_ * 4 + z_, x_ * 4 + yl_ * 2 + c_)

    def plus(v, k):
        return (v + (k % 4)) % 4

    sent = []

    def copy(src, dst, device):
        i = len(sent)
        cp = pltpu.make_async_remote_copy(
            src_ref=src, dst_ref=dst, send_sem=ss.at[i], recv_sem=rs.at[i], device_id=device, device_id_type=MESH
        )
        cp.start()
        sent.append(cp)
        return cp

    zl, zr, z2 = plus(z, -1), plus(z, 1), plus(z, 2)
    xl, xr, x2 = plus(x, -1), plus(x, 1), plus(x, 2)
    oyh, oyl, oc = 1 - yh, 1 - yl, 1 - c
    dp_peers = [(a, b) for a in range(2) for b in range(4) if a or b]

    def peer(a, b):
        return oyh if a else yh, plus(z, b)

    partners = [dev(yh_=peer(a, b)[0], z_=peer(a, b)[1]) for a, b in dp_peers]
    partners += [dev(yl_=oyl), dev(yh_=oyh, yl_=oyl), dev(x_=xl), dev(x_=xr), dev(c_=oc)]
    barrier = pltpu.get_barrier_semaphore()
    for partner in partners:
        pl.semaphore_signal(barrier, inc=1, device_id=partner, device_id_type=MESH)

    loads = [pltpu.make_async_copy(za_hbm, za, ls.at[0]), pltpu.make_async_copy(zb_hbm, zb, ls.at[1])]
    for load in loads:
        load.start()

    for v, ref in enumerate((za, zb)):
        loads[v].wait()
        total = jnp.sum(ref[...], axis=0, keepdims=True)
        shifted = ref[...] - total * (1.0 / local_rows)
        stats[dp, v : v + 1, :] = total
        stats[dp, v + 2 : v + 3, :] = jnp.sum(shifted * shifted, axis=0, keepdims=True)
    pl.semaphore_wait(barrier, len(partners))
    cps = [copy(stats.at[dp], stats.at[dp], dev(yh_=peer(a, b)[0], z_=peer(a, b)[1])) for a, b in dp_peers]
    for cp in cps:
        cp.wait_recv()

    totals = jnp.zeros((2, cols), F32)
    for d in range(8):
        totals = totals + stats[d, 0:2, :]
    mean = totals * (1.0 / n_rows)

    first = yh == 0
    for f in range(4):
        cut = slice(f * chunk, (f + 1) * chunk)
        ca = (za[:, cut] - mean[0:1, cut]).astype(BF16)
        cb = (zb[:, cut] - mean[1:2, cut]).astype(BF16)
        zi[f, c, yl, z, yh] = jnp.where(first, ca, cb)
        stage[f] = jnp.where(first, cb, ca)

    right_f = [plus(z, k) for k in (1, 2, 3, 0)]
    left_f = [plus(z, k) for k in (-1, 2, 0, 1)]
    from_left_f = [plus(z, k) for k in (0, 1, 2, 3)]
    from_right_f = [plus(z, k) for k in (0, 3, 1, 2)]

    def mine(f, to):
        return copy(zi.at[f, c, yl, z, yh], zi.at[f, c, yl, z, yh], dev(z_=to))

    def others(f, to):
        return copy(zi.at[f, c, yl, z, oyh], zi.at[f, c, yl, z, oyh], dev(z_=to))

    y1, y02 = {}, {}
    for k in (1, 3, 0, 2):
        f = plus(z, k)
        y1[k] = copy(stage.at[f], zi.at[f, c, yl, z, yh], dev(yh_=oyh))
    ra, rb, la, lb = {}, {}, {}, {}
    for s in range(2):
        ra[s] = mine(right_f[s], zr)
        la[s] = mine(left_f[s], zl)
    for k in (1, 3, 2, 0):
        f = plus(z, k)
        here = zi.at[f, c, yl, z, yh]
        y02[k] = [copy(here, here, dev(yl_=oyl)), copy(stage.at[f], here, dev(yh_=oyh, yl_=oyl))]

    half = chunk // 2
    slab, slab_fwd = {}, []

    def slab_send(q):
        zq = plus(z, q)
        jt[zq, x] = zi[z, c, yl, zq].reshape(pair, chunk).T
        slab[q] = [copy(jt.at[zq, x], jt.at[zq, x], dev(x_=xr)), copy(jt.at[zq, x], jt.at[zq, x], dev(x_=xl))]

    def slab_forward(q):
        zq = plus(z, q)
        for cp in slab[q]:
            cp.wait_recv()
        lo, hi = pl.ds(0, half), pl.ds(half, half)
        slab_fwd.append(copy(jt.at[zq, xl, lo], jt.at[zq, xl, lo], dev(x_=xr)))
        slab_fwd.append(copy(jt.at[zq, xr, hi], jt.at[zq, xr, hi], dev(x_=xl)))

    def forward_right(f):
        ref = zi.at[f, c, yl, zl, yh]
        return copy(ref, ref, dev(z_=zr))

    def forward_left(f):
        ref = zi.at[f, c, yl, zr, oyh]
        return copy(ref, ref, dev(z_=zl))

    fr, fl = {}, {}
    shared = {}

    def share(key, ref):
        shared[key] = copy(ref, ref, dev(c_=oc))

    y1[1].wait_recv()
    rb[0] = others(right_f[0], zr)
    y1[3].wait_recv()
    lb[0] = others(left_f[0], zl)
    y1[0].wait_recv()
    slab_send(0)
    y1[2].wait_recv()
    rb[1] = others(right_f[1], zr)
    lb[1] = others(left_f[1], zl)
    ra[2] = mine(right_f[2], zr)
    la[2] = mine(left_f[2], zl)

    squares = jnp.zeros((2, cols), F32)
    for d in range(8):
        gap = stats[d, 0:2, :] * (1.0 / local_rows) - mean
        squares = squares + (stats[d, 2:4, :] + local_rows * (gap * gap))
    spread = jnp.sqrt(squares / (n_rows - 1) + DEVIATION_FLOOR)
    coefs[0:2, :] = mean
    coefs[2:4, :] = jnp.where(spread < 1.0, -(VARIANCE_WEIGHT * n_rows / (2.0 * (n_rows - 1))) / spread, 0.0)

    ra[0].wait_recv()
    rb[0].wait_recv()
    slab_send(-1)
    la[0].wait_recv()
    lb[0].wait_recv()
    slab_send(1)
    ra[1].wait_recv()
    fr[0] = forward_right(from_left_f[1])
    lb[1].wait_recv()
    fl[0] = forward_left(from_right_f[1])
    rb[2] = others(right_f[2], zr)
    lb[2] = others(left_f[2], zl)
    slab_forward(0)
    ra[3] = mine(right_f[3], zr)
    la[3] = mine(left_f[3], zl)
    fr[3] = forward_right(from_left_f[0])
    fl[1] = forward_left(from_right_f[0])
    rb[3] = others(right_f[3], zr)
    lb[3] = others(left_f[3], zl)
    rb[1].wait_recv()
    la[1].wait_recv()
    ra[2].wait_recv()
    fr[1] = forward_right(from_left_f[2])
    lb[2].wait_recv()
    fl[2] = forward_left(from_right_f[2])
    rb[2].wait_recv()
    la[2].wait_recv()

    across = {}

    def opposite(q):
        fr[q].wait_recv()
        fl[q].wait_recv()
        f = plus(z, q)
        across[q] = copy(zi.at[f, c, yl, z2], zi.at[f, c, yl, z2], dev(yl_=oyl))

    opposite(0)
    slab_send(2)
    share(("same", 0), zi.at[z, c, yl])
    slab_forward(-1)
    slab_forward(1)

    rc, lc = {}, {}
    right_c = [plus(z, k) for k in (1, 2, 3, 0)]
    left_c = [plus(z, k) for k in (3, 0, 1, 2)]
    for k in (1, 3, 2, 0):
        for cp in y02[k]:
            cp.wait_recv()
        share(("own", k), zi.at[plus(z, k), c, oyl, z])

    def direct(q):
        rc[q] = copy(zi.at[right_c[q], c, oyl, z], zi.at[right_c[q], c, oyl, z], dev(z_=zr))
        lc[q] = copy(zi.at[left_c[q], c, oyl, z], zi.at[left_c[q], c, oyl, z], dev(z_=zl))

    direct(0)
    ra[3].wait_recv()
    fr[2] = forward_right(from_left_f[3])
    lb[3].wait_recv()
    fl[3] = forward_left(from_right_f[3])
    direct(1)
    rb[3].wait_recv()
    la[3].wait_recv()
    for q in (1, 2, 3):
        opposite(q)
        share(("same", q), zi.at[plus(z, q), c, yl])
        if q == 1:
            slab_forward(2)
    direct(2)
    direct(3)

    scale = 2.0 * n_rows / (n_rows - 1.0)
    slope = scale / (n_rows - 1.0)
    edge = HUBER_EDGE * scale

    def gram(f, cc, yy, first_part, parts):
        size = parts * chunk
        g = jnp.zeros((size, chunk), F32)
        for q in range(4):
            lhs = jt[q, pl.ds(first_part, parts)].reshape(size, chunk)
            rhs = zi[f, cc, yy, q].reshape(pair, chunk)
            g = g + jnp.dot(lhs, rhs, preferred_element_type=F32)
        w = jnp.clip(g * slope, -edge, edge).astype(BF16)
        wt[f, cc, yy, pl.ds(first_part, parts)] = w.reshape(parts, chunk, chunk)

    def gram_part(cc, part):
        def body(q, carry):
            gram((z + q) % 4, cc, yl, part, 1)
            return carry

        lax.fori_loop(0, 4, body, 0)

    def gram_block(f, cc, yy):
        def body(i, carry):
            gram(f, cc, yy, 2 * i, 2)
            return carry

        lax.fori_loop(0, 2, body, 0)

    gram_part(c, x)
    for q in range(4):
        shared["same", q].wait_recv()
    gram_part(oc, x)
    row_id = lax.broadcasted_iota(jnp.int32, (chunk, chunk), 0)
    col_id = lax.broadcasted_iota(jnp.int32, (chunk, chunk), 1)
    wt[z, c, yl, x] = jnp.where(row_id == col_id, jnp.zeros((), BF16), wt[z, c, yl, x])
    for part in (xl, xr):
        gram_part(c, part)
        gram_part(oc, part)
    for cp in slab_fwd:
        cp.wait_recv()
    gram_part(c, x2)
    gram_part(oc, x2)

    def arrive(q):
        f = plus(z, q)
        rc[q].wait_recv()
        share(("left", q), zi.at[f, c, oyl, zl])
        lc[q].wait_recv()
        share(("right", q), zi.at[f, c, oyl, zr])
        across[q].wait_recv()
        share(("across", q), zi.at[f, c, oyl, z2])

    def sibling(q):
        for name in ("own", "left", "right", "across"):
            shared[name, q].wait_recv()

    for q in range(3):
        arrive(q)
        gram_block(plus(z, q), c, oyl)
        sibling(q)
        gram_block(plus(z, q), oc, oyl)
    arrive(3)
    gram(zl, c, oyl, x2, 1)
    sibling(3)
    gram(zl, oc, oyl, x2, 1)

    def product(part, k):
        zq = plus(z, k)
        acc = jnp.zeros((pair, chunk), F32)
        for f in range(4):
            for cc in range(2):
                for yy in range(2):
                    lhs = zi[f, cc, yy, zq].reshape(pair, chunk)
                    acc = acc + lax.dot_general(
                        lhs, wt[f, cc, yy, part], (((1,), (1,)), ((), ())), preferred_element_type=F32
                    )
        return acc

    def send_part(slot, value, to):
        part_out[slot] = value.astype(BF16)
        return copy(part_out.at[slot], part_in.at[slot], dev(x_=to))

    r, l = {}, {}
    r[0] = send_part(0, product(x2, 2), xr)
    l[0] = send_part(1, product(x2, 0), xl)
    r[1] = send_part(2, product(x2, 1), xr)
    l[1] = send_part(3, product(x2, 3), xl)
    for part in (xr, xl):
        gram(zl, c, oyl, part, 1)
        gram(zl, oc, oyl, part, 1)
    r[2] = send_part(4, product(xr, 0), xr)
    l[2] = send_part(5, product(xl, 2), xl)
    r[3] = send_part(6, product(xr, 3), xr)
    l[3] = send_part(7, product(xl, 1), xl)
    acc = product(xr, 2)
    r[0].wait_recv()
    r[4] = send_part(8, acc + part_in[0].astype(F32), xr)
    acc = product(xl, 0)
    l[0].wait_recv()
    l[4] = send_part(9, acc + part_in[1].astype(F32), xl)
    acc = product(xr, 1)
    r[1].wait_recv()
    r[5] = send_part(10, acc + part_in[2].astype(F32), xr)
    acc = product(xl, 3)
    l[1].wait_recv()
    l[5] = send_part(11, acc + part_in[3].astype(F32), xl)
    gram(zl, c, oyl, x, 1)
    gram(zl, oc, oyl, x, 1)

    back = []

    def give(k, total):
        zq = plus(z, k)
        rows_out[zq] = total.astype(BF16).reshape(2, local_rows, chunk)
        back.append(copy(rows_out.at[zq, oyh], rows_in.at[yh, z], dev(yh_=oyh, z_=zq)))
        if k == 0:
            rows_in[yh, z] = rows_out[z, yh]
        else:
            back.append(copy(rows_out.at[zq, yh], rows_in.at[yh, z], dev(z_=zq)))

    acc = product(x, 2)
    l[2].wait_recv()
    acc = acc + part_in[5].astype(F32)
    r[4].wait_recv()
    give(2, acc + part_in[8].astype(F32))
    acc = product(x, 0)
    r[2].wait_recv()
    acc = acc + part_in[4].astype(F32)
    l[4].wait_recv()
    give(0, acc + part_in[9].astype(F32))
    acc = product(x, 1)
    l[3].wait_recv()
    acc = acc + part_in[7].astype(F32)
    r[5].wait_recv()
    give(1, acc + part_in[10].astype(F32))
    acc = product(x, 3)
    r[3].wait_recv()
    acc = acc + part_in[6].astype(F32)
    l[5].wait_recv()
    give(3, acc + part_in[11].astype(F32))
    for cp in back:
        cp.wait_recv()
    for v in range(2):
        for f in range(4):
            cov[v, :, f * chunk : (f + 1) * chunk] = rows_in[v, f]
    for cp in sent:
        cp.wait_send()


def on_device(z_a, z_b):
    rows, cols = z_a.shape
    chunk = cols // 4
    vmem = pl.BlockSpec(memory_space=pltpu.VMEM)
    hbm = pl.BlockSpec(memory_space=pl.ANY)
    cov, coefs = pl.pallas_call(
        kernel,
        out_shape=[jax.ShapeDtypeStruct((2, rows, cols), BF16), jax.ShapeDtypeStruct((4, cols), F32)],
        in_specs=[hbm, hbm],
        out_specs=[vmem, vmem],
        scratch_shapes=[
            pltpu.VMEM((rows, cols), F32),
            pltpu.VMEM((rows, cols), F32),
            pltpu.VMEM((8, 4, cols), F32),
            pltpu.VMEM((4, 2, 2, 4, 2, rows, chunk), BF16),
            pltpu.VMEM((4, rows, chunk), BF16),
            pltpu.VMEM((4, 4, chunk, 2 * rows), BF16),
            pltpu.VMEM((4, 2, 2, 4, chunk, chunk), BF16),
            pltpu.VMEM((12, 2 * rows, chunk), BF16),
            pltpu.VMEM((12, 2 * rows, chunk), BF16),
            pltpu.VMEM((4, 2, rows, chunk), BF16),
            pltpu.VMEM((2, 4, rows, chunk), BF16),
            pltpu.SemaphoreType.DMA((2,)),
            pltpu.SemaphoreType.DMA((N_COPIES,)),
            pltpu.SemaphoreType.DMA((N_COPIES,)),
        ],
        compiler_params=pltpu.CompilerParams(collective_id=0, has_side_effects=True, vmem_limit_bytes=56 * 1024 * 1024),
        name="vicreg",
    )(z_a, z_b)
    difference = INVARIANCE_WEIGHT * (z_a - z_b)
    dz_a = difference + coefs[2:3] * (z_a - coefs[0:1]) + cov[0].astype(F32)
    dz_b = coefs[3:4] * (z_b - coefs[1:2]) - difference + cov[1].astype(F32)
    return dz_a, dz_b


def solution(mesh):
    specs = (P("dp", "mp"), P("dp", "mp"))
    return jax.shard_map(on_device, mesh=mesh, in_specs=specs, out_specs=specs, check_vma=False)
```

```python
import jax
import jax.numpy as jnp
from jax import lax
from jax.experimental import pallas as pl
from jax.experimental.pallas import tpu as pltpu
from jax.sharding import PartitionSpec as P

INVARIANCE_WEIGHT = 25.0
VARIANCE_WEIGHT = 25.0
DEVIATION_FLOOR = 0.0001
HUBER_EDGE = 0.05

MESH = pl.DeviceIdType.MESH
F32 = jnp.float32
BF16 = jnp.bfloat16
N_COPIES = 128


def kernel(za_hbm, zb_hbm, cov, mean_a, mean_b, pull_a, pull_b, za, zb, sums, squares, zi, stage, jt, wt, part_out, part_in, rows_out, rows_in, ls, ss, rs):
    dp = lax.axis_index("dp")
    mp = lax.axis_index("mp")
    yh, z = dp // 4, dp % 4
    x, yl, c = mp // 4, (mp // 2) % 2, mp % 2
    local_rows, cols = za.shape
    chunk = cols // 4
    n_rows = local_rows * 8
    pair = 2 * local_rows

    def dev(yh_=None, z_=None, x_=None, yl_=None, c_=None):
        yh_ = yh if yh_ is None else yh_
        z_ = z if z_ is None else z_
        x_ = x if x_ is None else x_
        yl_ = yl if yl_ is None else yl_
        c_ = c if c_ is None else c_
        return (yh_ * 4 + z_, x_ * 4 + yl_ * 2 + c_)

    def plus(v, k):
        return (v + (k % 4)) % 4

    sent = []

    def copy(src, dst, device):
        i = len(sent)
        cp = pltpu.make_async_remote_copy(
            src_ref=src, dst_ref=dst, send_sem=ss.at[i], recv_sem=rs.at[i], device_id=device, device_id_type=MESH
        )
        cp.start()
        sent.append(cp)
        return cp

    zl, zr, z2 = plus(z, -1), plus(z, 1), plus(z, 2)
    xl, xr, x2 = plus(x, -1), plus(x, 1), plus(x, 2)
    oyh, oyl, oc = 1 - yh, 1 - yl, 1 - c
    dp_peers = [(a, b) for a in range(2) for b in range(4) if a or b]

    def peer(a, b):
        return oyh if a else yh, plus(z, b)

    partners = [dev(yh_=peer(a, b)[0], z_=peer(a, b)[1]) for a, b in dp_peers]
    partners += [dev(yl_=oyl), dev(yh_=oyh, yl_=oyl), dev(x_=xl), dev(x_=xr), dev(c_=oc)]
    barrier = pltpu.get_barrier_semaphore()
    for partner in partners:
        pl.semaphore_signal(barrier, inc=1, device_id=partner, device_id_type=MESH)

    loads = [pltpu.make_async_copy(za_hbm, za, ls.at[0]), pltpu.make_async_copy(zb_hbm, zb, ls.at[1])]
    for load in loads:
        load.start()

    for v, ref in enumerate((za, zb)):
        loads[v].wait()
        sums[dp, v : v + 1, :] = jnp.sum(ref[...], axis=0, keepdims=True)
    pl.semaphore_wait(barrier, len(partners))
    def to_peers(ref):
        return [copy(ref, ref, dev(yh_=peer(a, b)[0], z_=peer(a, b)[1])) for a, b in dp_peers]

    for cp in to_peers(sums.at[dp]):
        cp.wait_recv()

    totals = jnp.zeros((2, cols), F32)
    for d in range(8):
        totals = totals + sums[d]
    mean = totals * (1.0 / n_rows)

    first = yh == 0
    for f in range(4):
        cut = slice(f * chunk, (f + 1) * chunk)
        ca = (za[:, cut] - mean[0:1, cut]).astype(BF16)
        cb = (zb[:, cut] - mean[1:2, cut]).astype(BF16)
        zi[f, c, yl, z, yh] = jnp.where(first, ca, cb)
        stage[f] = jnp.where(first, cb, ca)

    right_f = [plus(z, k) for k in (1, 2, 3, 0)]
    left_f = [plus(z, k) for k in (-1, 2, 0, 1)]
    from_left_f = [plus(z, k) for k in (0, 1, 2, 3)]
    from_right_f = [plus(z, k) for k in (0, 3, 1, 2)]

    def mine(f, to):
        return copy(zi.at[f, c, yl, z, yh], zi.at[f, c, yl, z, yh], dev(z_=to))

    def others(f, to):
        return copy(zi.at[f, c, yl, z, oyh], zi.at[f, c, yl, z, oyh], dev(z_=to))

    y1, y02 = {}, {}
    for k in (1, 3, 0, 2):
        f = plus(z, k)
        y1[k] = copy(stage.at[f], zi.at[f, c, yl, z, yh], dev(yh_=oyh))
    ra, rb, la, lb = {}, {}, {}, {}
    for s in range(2):
        ra[s] = mine(right_f[s], zr)
        la[s] = mine(left_f[s], zl)
    for k in (1, 3, 2, 0):
        f = plus(z, k)
        here = zi.at[f, c, yl, z, yh]
        y02[k] = [copy(here, here, dev(yl_=oyl)), copy(stage.at[f], here, dev(yh_=oyh, yl_=oyl))]

    half = chunk // 2
    slab, slab_fwd = {}, []

    def slab_send(q):
        zq = plus(z, q)
        jt[zq, x] = zi[z, c, yl, zq].reshape(pair, chunk).T
        slab[q] = [copy(jt.at[zq, x], jt.at[zq, x], dev(x_=xr)), copy(jt.at[zq, x], jt.at[zq, x], dev(x_=xl))]

    def slab_forward(q):
        zq = plus(z, q)
        for cp in slab[q]:
            cp.wait_recv()
        lo, hi = pl.ds(0, half), pl.ds(half, half)
        slab_fwd.append(copy(jt.at[zq, xl, lo], jt.at[zq, xl, lo], dev(x_=xr)))
        slab_fwd.append(copy(jt.at[zq, xr, hi], jt.at[zq, xr, hi], dev(x_=xl)))

    def forward_right(f):
        ref = zi.at[f, c, yl, zl, yh]
        return copy(ref, ref, dev(z_=zr))

    def forward_left(f):
        ref = zi.at[f, c, yl, zr, oyh]
        return copy(ref, ref, dev(z_=zl))

    fr, fl = {}, {}
    shared = {}

    def share(key, ref):
        shared[key] = copy(ref, ref, dev(c_=oc))

    y1[1].wait_recv()
    rb[0] = others(right_f[0], zr)
    y1[3].wait_recv()
    lb[0] = others(left_f[0], zl)
    y1[0].wait_recv()
    slab_send(0)
    y1[2].wait_recv()
    rb[1] = others(right_f[1], zr)
    lb[1] = others(left_f[1], zl)
    ra[2] = mine(right_f[2], zr)
    la[2] = mine(left_f[2], zl)

    for v, ref in enumerate((za, zb)):
        centered = ref[...] - mean[v : v + 1, :]
        squares[dp, v : v + 1, :] = jnp.sum(centered * centered, axis=0, keepdims=True)
    square_copies = to_peers(squares.at[dp])

    ra[0].wait_recv()
    rb[0].wait_recv()
    slab_send(-1)
    la[0].wait_recv()
    lb[0].wait_recv()
    slab_send(1)
    ra[1].wait_recv()
    fr[0] = forward_right(from_left_f[1])
    lb[1].wait_recv()
    fl[0] = forward_left(from_right_f[1])
    rb[2] = others(right_f[2], zr)
    lb[2] = others(left_f[2], zl)
    slab_forward(0)
    ra[3] = mine(right_f[3], zr)
    la[3] = mine(left_f[3], zl)
    fr[3] = forward_right(from_left_f[0])
    fl[1] = forward_left(from_right_f[0])
    rb[3] = others(right_f[3], zr)
    lb[3] = others(left_f[3], zl)
    rb[1].wait_recv()
    la[1].wait_recv()
    ra[2].wait_recv()
    fr[1] = forward_right(from_left_f[2])
    lb[2].wait_recv()
    fl[2] = forward_left(from_right_f[2])
    rb[2].wait_recv()
    la[2].wait_recv()

    across = {}

    def opposite(q):
        fr[q].wait_recv()
        fl[q].wait_recv()
        f = plus(z, q)
        across[q] = copy(zi.at[f, c, yl, z2], zi.at[f, c, yl, z2], dev(yl_=oyl))

    opposite(0)
    slab_send(2)
    share(("same", 0), zi.at[z, c, yl])

    rc, lc = {}, {}
    right_c = [plus(z, k) for k in (1, 2, 3, 0)]
    left_c = [plus(z, k) for k in (3, 0, 1, 2)]

    def direct(q):
        rc[q] = copy(zi.at[right_c[q], c, oyl, z], zi.at[right_c[q], c, oyl, z], dev(z_=zr))
        lc[q] = copy(zi.at[left_c[q], c, oyl, z], zi.at[left_c[q], c, oyl, z], dev(z_=zl))

    scale = 2.0 * n_rows / (n_rows - 1.0)
    slope = scale / (n_rows - 1.0)
    edge = HUBER_EDGE * scale

    def gram(f, cc, yy, part):
        g = jnp.zeros((chunk, chunk), F32)
        for q in range(4):
            g = g + jnp.dot(jt[q, part], zi[f, cc, yy, q].reshape(pair, chunk), preferred_element_type=F32)
        wt[f, cc, yy, part] = jnp.clip(g * slope, -edge, edge).astype(BF16)

    def gram_part(cc, part):
        for q in range(4):
            gram(plus(z, q), cc, yl, part)

    def gram_block(f):
        for cc in (c, oc):
            for part in range(4):
                gram(f, cc, oyl, part)

    for k in (1, 3):
        for cp in y02[k]:
            cp.wait_recv()
        share(("own", k), zi.at[plus(z, k), c, oyl, z])
    direct(0)
    slab_forward(-1)
    slab_forward(1)
    ra[3].wait_recv()
    fr[2] = forward_right(from_left_f[3])
    lb[3].wait_recv()
    fl[3] = forward_left(from_right_f[3])
    for k in (2, 0):
        for cp in y02[k]:
            cp.wait_recv()
        share(("own", k), zi.at[plus(z, k), c, oyl, z])
    direct(1)
    rb[3].wait_recv()
    la[3].wait_recv()
    gram(z, c, yl, x)
    opposite(1)
    share(("same", 1), zi.at[plus(z, 1), c, yl])
    slab_forward(2)
    direct(2)
    opposite(2)
    share(("same", 2), zi.at[plus(z, 2), c, yl])
    opposite(3)
    share(("same", 3), zi.at[plus(z, 3), c, yl])
    direct(3)

    def arrive(q):
        f = plus(z, q)
        rc[q].wait_recv()
        share(("left", q), zi.at[f, c, oyl, zl])
        lc[q].wait_recv()
        share(("right", q), zi.at[f, c, oyl, zr])
        across[q].wait_recv()
        share(("across", q), zi.at[f, c, oyl, z2])

    def sibling(q):
        for name in ("own", "left", "right", "across"):
            shared[name, q].wait_recv()

    for q in (1, 2, 3):
        gram(plus(z, q), c, yl, x)
    gram_part(c, xl)
    gram_part(c, xr)
    arrive(0)
    for q in range(4):
        shared["same", q].wait_recv()
    gram_part(oc, x)
    gram_part(oc, xl)
    gram_part(oc, xr)
    row_id = lax.broadcasted_iota(jnp.int32, (chunk, chunk), 0)
    col_id = lax.broadcasted_iota(jnp.int32, (chunk, chunk), 1)
    wt[z, c, yl, x] = jnp.where(row_id == col_id, jnp.zeros((), BF16), wt[z, c, yl, x])
    arrive(1)
    for cp in slab_fwd:
        cp.wait_recv()
    gram_part(c, x2)
    gram_part(oc, x2)
    sibling(0)
    gram_block(z)
    arrive(2)
    sibling(1)
    gram_block(zr)
    arrive(3)
    sibling(2)
    gram_block(z2)
    gram(zl, c, oyl, x2)
    sibling(3)
    gram(zl, oc, oyl, x2)

    for cp in square_copies:
        cp.wait_recv()
    variance = jnp.zeros((2, cols), F32)
    for d in range(8):
        variance = variance + squares[d]
    spread = jnp.sqrt(variance / (n_rows - 1) + DEVIATION_FLOOR)
    pull = jnp.where(spread < 1.0, -(VARIANCE_WEIGHT * n_rows / (2.0 * (n_rows - 1))) / spread, 0.0)
    mean_a[...], mean_b[...] = mean[0:1, :], mean[1:2, :]
    pull_a[...], pull_b[...] = pull[0:1, :], pull[1:2, :]

    def product(part, k):
        zq = plus(z, k)
        acc = jnp.zeros((pair, chunk), F32)
        for f in range(4):
            for cc in range(2):
                for yy in range(2):
                    lhs = zi[f, cc, yy, zq].reshape(pair, chunk)
                    acc = acc + lax.dot_general(
                        lhs, wt[f, cc, yy, part], (((1,), (1,)), ((), ())), preferred_element_type=F32
                    )
        return acc

    def send_part(slot, value, to):
        part_out[slot] = value.astype(BF16)
        return copy(part_out.at[slot], part_in.at[slot], dev(x_=to))

    r, l = {}, {}
    r[0] = send_part(0, product(x2, 2), xr)
    l[0] = send_part(1, product(x2, 0), xl)
    r[1] = send_part(2, product(x2, 1), xr)
    l[1] = send_part(3, product(x2, 3), xl)
    for part in (xr, xl):
        gram(zl, c, oyl, part)
        gram(zl, oc, oyl, part)
    r[2] = send_part(4, product(xr, 0), xr)
    l[2] = send_part(5, product(xl, 2), xl)
    r[3] = send_part(6, product(xr, 3), xr)
    l[3] = send_part(7, product(xl, 1), xl)
    acc = product(xr, 2)
    r[0].wait_recv()
    r[4] = send_part(8, acc + part_in[0].astype(F32), xr)
    acc = product(xl, 0)
    l[0].wait_recv()
    l[4] = send_part(9, acc + part_in[1].astype(F32), xl)
    acc = product(xr, 1)
    r[1].wait_recv()
    r[5] = send_part(10, acc + part_in[2].astype(F32), xr)
    acc = product(xl, 3)
    l[1].wait_recv()
    l[5] = send_part(11, acc + part_in[3].astype(F32), xl)
    gram(zl, c, oyl, x)
    gram(zl, oc, oyl, x)

    back = []

    def give(k, total):
        zq = plus(z, k)
        rows_out[zq] = total.astype(BF16).reshape(2, local_rows, chunk)
        back.append(copy(rows_out.at[zq, oyh], rows_in.at[yh, z], dev(yh_=oyh, z_=zq)))
        if k == 0:
            rows_in[yh, z] = rows_out[z, yh]
        else:
            back.append(copy(rows_out.at[zq, yh], rows_in.at[yh, z], dev(z_=zq)))

    acc = product(x, 2)
    l[2].wait_recv()
    acc = acc + part_in[5].astype(F32)
    r[4].wait_recv()
    give(2, acc + part_in[8].astype(F32))
    acc = product(x, 0)
    r[2].wait_recv()
    acc = acc + part_in[4].astype(F32)
    l[4].wait_recv()
    give(0, acc + part_in[9].astype(F32))
    acc = product(x, 1)
    l[3].wait_recv()
    acc = acc + part_in[7].astype(F32)
    r[5].wait_recv()
    give(1, acc + part_in[10].astype(F32))
    acc = product(x, 3)
    r[3].wait_recv()
    acc = acc + part_in[6].astype(F32)
    l[5].wait_recv()
    give(3, acc + part_in[11].astype(F32))
    for cp in back:
        cp.wait_recv()
    for v in range(2):
        for f in range(4):
            cov[v, :, f * chunk : (f + 1) * chunk] = rows_in[v, f]
    for cp in sent:
        cp.wait_send()


def on_device(z_a, z_b):
    rows, cols = z_a.shape
    chunk = cols // 4
    vmem = pl.BlockSpec(memory_space=pltpu.VMEM)
    hbm = pl.BlockSpec(memory_space=pl.ANY)
    cov, mean_a, mean_b, pull_a, pull_b = pl.pallas_call(
        kernel,
        out_shape=[jax.ShapeDtypeStruct((2, rows, cols), BF16), *[jax.ShapeDtypeStruct((1, cols), F32)] * 4],
        in_specs=[hbm, hbm],
        out_specs=[vmem] * 5,
        scratch_shapes=[
            pltpu.VMEM((rows, cols), F32),
            pltpu.VMEM((rows, cols), F32),
            pltpu.VMEM((8, 2, cols), F32),
            pltpu.VMEM((8, 2, cols), F32),
            pltpu.VMEM((4, 2, 2, 4, 2, rows, chunk), BF16),
            pltpu.VMEM((4, rows, chunk), BF16),
            pltpu.VMEM((4, 4, chunk, 2 * rows), BF16),
            pltpu.VMEM((4, 2, 2, 4, chunk, chunk), BF16),
            pltpu.VMEM((12, 2 * rows, chunk), BF16),
            pltpu.VMEM((12, 2 * rows, chunk), BF16),
            pltpu.VMEM((4, 2, rows, chunk), BF16),
            pltpu.VMEM((2, 4, rows, chunk), BF16),
            pltpu.SemaphoreType.DMA((2,)),
            pltpu.SemaphoreType.DMA((N_COPIES,)),
            pltpu.SemaphoreType.DMA((N_COPIES,)),
        ],
        compiler_params=pltpu.CompilerParams(collective_id=0, has_side_effects=True, vmem_limit_bytes=56 * 1024 * 1024),
        name="vicreg",
    )(z_a, z_b)
    difference = INVARIANCE_WEIGHT * (z_a - z_b)
    dz_a = difference + pull_a * (z_a - mean_a) + cov[0].astype(F32)
    dz_b = pull_b * (z_b - mean_b) - difference + cov[1].astype(F32)
    return dz_a, dz_b


def solution(mesh):
    specs = (P("dp", "mp"), P("dp", "mp"))
    return jax.shard_map(on_device, mesh=mesh, in_specs=specs, out_specs=specs, check_vma=False)
```

```python
import jax
import jax.numpy as jnp
from jax import lax
from jax.experimental import pallas as pl
from jax.experimental.pallas import tpu as pltpu
from jax.sharding import PartitionSpec as P

INVARIANCE_WEIGHT = 25.0
VARIANCE_WEIGHT = 25.0
DEVIATION_FLOOR = 0.0001
HUBER_EDGE = 0.05

MESH = pl.DeviceIdType.MESH
F32 = jnp.float32
BF16 = jnp.bfloat16
N_COPIES = 128


def kernel(za_hbm, zb_hbm, cov, mean_a, mean_b, pull_a, pull_b, za, zb, sums, squares, zi, stage, jt, wt, part_out, part_in, own, rows_out, rows_in, ls, ss, rs):
    dp = lax.axis_index("dp")
    mp = lax.axis_index("mp")
    yh, z = dp // 4, dp % 4
    x, yl, c = mp // 4, (mp // 2) % 2, mp % 2
    local_rows, cols = za.shape
    chunk = cols // 4
    n_rows = local_rows * 8
    pair = 2 * local_rows

    def dev(yh_=None, z_=None, x_=None, yl_=None, c_=None):
        yh_ = yh if yh_ is None else yh_
        z_ = z if z_ is None else z_
        x_ = x if x_ is None else x_
        yl_ = yl if yl_ is None else yl_
        c_ = c if c_ is None else c_
        return (yh_ * 4 + z_, x_ * 4 + yl_ * 2 + c_)

    def plus(v, k):
        return (v + (k % 4)) % 4

    sent = []

    def copy(src, dst, device):
        i = len(sent)
        cp = pltpu.make_async_remote_copy(
            src_ref=src, dst_ref=dst, send_sem=ss.at[i], recv_sem=rs.at[i], device_id=device, device_id_type=MESH
        )
        cp.start()
        sent.append(cp)
        return cp

    zl, zr, z2 = plus(z, -1), plus(z, 1), plus(z, 2)
    xl, xr, x2 = plus(x, -1), plus(x, 1), plus(x, 2)
    oyh, oyl, oc = 1 - yh, 1 - yl, 1 - c
    dp_peers = [(a, b) for a in range(2) for b in range(4) if a or b]

    def peer(a, b):
        return oyh if a else yh, plus(z, b)

    partners = [dev(yh_=peer(a, b)[0], z_=peer(a, b)[1]) for a, b in dp_peers]
    partners += [dev(yl_=oyl), dev(yh_=oyh, yl_=oyl), dev(x_=xl), dev(x_=xr), dev(c_=oc)]
    barrier = pltpu.get_barrier_semaphore()
    for partner in partners:
        pl.semaphore_signal(barrier, inc=1, device_id=partner, device_id_type=MESH)

    loads = [pltpu.make_async_copy(za_hbm, za, ls.at[0]), pltpu.make_async_copy(zb_hbm, zb, ls.at[1])]
    for load in loads:
        load.start()

    for v, ref in enumerate((za, zb)):
        loads[v].wait()
        sums[dp, v : v + 1, :] = jnp.sum(ref[...], axis=0, keepdims=True)
    pl.semaphore_wait(barrier, len(partners))
    def to_peers(ref):
        return [copy(ref, ref, dev(yh_=peer(a, b)[0], z_=peer(a, b)[1])) for a, b in dp_peers]

    for cp in to_peers(sums.at[dp]):
        cp.wait_recv()

    totals = jnp.zeros((2, cols), F32)
    for d in range(8):
        totals = totals + sums[d]
    mean = totals * (1.0 / n_rows)

    first = yh == 0
    for f in range(4):
        cut = slice(f * chunk, (f + 1) * chunk)
        ca = (za[:, cut] - mean[0:1, cut]).astype(BF16)
        cb = (zb[:, cut] - mean[1:2, cut]).astype(BF16)
        zi[f, c, yl, z, yh] = jnp.where(first, ca, cb)
        stage[f] = jnp.where(first, cb, ca)

    right_f = [plus(z, k) for k in (1, 2, 3, 0)]
    left_f = [plus(z, k) for k in (-1, 2, 0, 1)]
    from_left_f = [plus(z, k) for k in (0, 1, 2, 3)]
    from_right_f = [plus(z, k) for k in (0, 3, 1, 2)]

    def mine(f, to):
        return copy(zi.at[f, c, yl, z, yh], zi.at[f, c, yl, z, yh], dev(z_=to))

    def others(f, to):
        return copy(zi.at[f, c, yl, z, oyh], zi.at[f, c, yl, z, oyh], dev(z_=to))

    y1, y02 = {}, {}
    for k in (1, 3, 0, 2):
        f = plus(z, k)
        y1[k] = copy(stage.at[f], zi.at[f, c, yl, z, yh], dev(yh_=oyh))
    ra, rb, la, lb = {}, {}, {}, {}
    for s in range(4):
        ra[s] = mine(right_f[s], zr)
        la[s] = mine(left_f[s], zl)
    for k in (1, 3, 2, 0):
        f = plus(z, k)
        here = zi.at[f, c, yl, z, yh]
        y02[k] = [copy(here, here, dev(yl_=oyl)), copy(stage.at[f], here, dev(yh_=oyh, yl_=oyl))]

    for v, ref in enumerate((za, zb)):
        centered = ref[...] - mean[v : v + 1, :]
        squares[dp, v : v + 1, :] = jnp.sum(centered * centered, axis=0, keepdims=True)
    square_copies = to_peers(squares.at[dp])

    half = chunk // 2
    slab, slab_fwd = {}, []

    def slab_send(q):
        zq = plus(z, q)
        jt[zq, x] = zi[z, c, yl, zq].reshape(pair, chunk).T
        slab[q] = [copy(jt.at[zq, x], jt.at[zq, x], dev(x_=xr)), copy(jt.at[zq, x], jt.at[zq, x], dev(x_=xl))]

    def slab_forward(q):
        zq = plus(z, q)
        for cp in slab[q]:
            cp.wait_recv()
        lo, hi = pl.ds(0, half), pl.ds(half, half)
        slab_fwd.append(copy(jt.at[zq, xl, lo], jt.at[zq, xl, lo], dev(x_=xr)))
        slab_fwd.append(copy(jt.at[zq, xr, hi], jt.at[zq, xr, hi], dev(x_=xl)))

    def forward_right(f):
        ref = zi.at[f, c, yl, zl, yh]
        return copy(ref, ref, dev(z_=zr))

    def forward_left(f):
        ref = zi.at[f, c, yl, zr, oyh]
        return copy(ref, ref, dev(z_=zl))

    fr, fl = {}, {}
    shared = {}

    def share(key, ref):
        shared[key] = copy(ref, ref, dev(c_=oc))

    y1[1].wait_recv()
    rb[0] = others(right_f[0], zr)
    ra[1].wait_recv()
    fr[0] = forward_right(from_left_f[1])
    y1[3].wait_recv()
    lb[0] = others(left_f[0], zl)
    y1[0].wait_recv()
    slab_send(0)
    y1[2].wait_recv()
    rb[1] = others(right_f[1], zr)
    lb[1] = others(left_f[1], zl)
    lb[2] = others(left_f[2], zl)
    ra[2].wait_recv()
    fr[1] = forward_right(from_left_f[2])
    ra[0].wait_recv()
    rb[0].wait_recv()
    slab_send(-1)
    la[0].wait_recv()
    lb[0].wait_recv()
    slab_send(1)
    lb[1].wait_recv()
    fl[0] = forward_left(from_right_f[1])
    lb[3] = others(left_f[3], zl)
    ra[3].wait_recv()
    fr[2] = forward_right(from_left_f[3])
    fl[1] = forward_left(from_right_f[0])
    fr[3] = forward_right(from_left_f[0])
    rb[2] = others(right_f[2], zr)
    rb[3] = others(right_f[3], zr)
    lb[2].wait_recv()
    fl[2] = forward_left(from_right_f[2])
    slab_forward(0)
    for s in range(1, 4):
        la[s].wait_recv()
    rb[1].wait_recv()

    across = {}

    def opposite(q):
        fr[q].wait_recv()
        fl[q].wait_recv()
        f = plus(z, q)
        across[q] = copy(zi.at[f, c, yl, z2], zi.at[f, c, yl, z2], dev(yl_=oyl))

    opposite(0)
    slab_send(2)
    share(("same", 0), zi.at[z, c, yl])

    rc, lc = {}, {}
    right_c = [plus(z, k) for k in (1, 2, 3, 0)]
    left_c = [plus(z, k) for k in (3, 0, 1, 2)]

    def direct(q):
        rc[q] = copy(zi.at[right_c[q], c, oyl, z], zi.at[right_c[q], c, oyl, z], dev(z_=zr))
        lc[q] = copy(zi.at[left_c[q], c, oyl, z], zi.at[left_c[q], c, oyl, z], dev(z_=zl))

    scale = 2.0 * n_rows / (n_rows - 1.0)
    slope = scale / (n_rows - 1.0)
    edge = HUBER_EDGE * scale

    def gram(f, cc, yy, part):
        g = jnp.zeros((chunk, chunk), F32)
        for q in range(4):
            g = g + jnp.dot(jt[q, part], zi[f, cc, yy, q].reshape(pair, chunk), preferred_element_type=F32)
        wt[f, cc, yy, part] = jnp.clip(g * slope, -edge, edge).astype(BF16)

    def gram_part(cc, part):
        for q in range(4):
            gram(plus(z, q), cc, yl, part)

    def gram_block(f):
        for cc in (c, oc):
            for part in range(4):
                gram(f, cc, oyl, part)

    lb[3].wait_recv()
    fl[3] = forward_left(from_right_f[3])
    for k in (1, 3):
        for cp in y02[k]:
            cp.wait_recv()
        share(("own", k), zi.at[plus(z, k), c, oyl, z])
    direct(0)
    slab_forward(-1)
    slab_forward(1)
    for k in (2, 0):
        for cp in y02[k]:
            cp.wait_recv()
        share(("own", k), zi.at[plus(z, k), c, oyl, z])
    direct(1)
    opposite(1)
    rb[2].wait_recv()
    rb[3].wait_recv()
    share(("same", 1), zi.at[plus(z, 1), c, yl])
    shared["same", 0].wait_recv()
    gram(z, c, yl, x)
    gram(z, oc, yl, x)
    gram(zr, c, yl, x)
    opposite(2)
    share(("same", 2), zi.at[plus(z, 2), c, yl])
    slab_forward(2)
    direct(2)
    opposite(3)
    share(("same", 3), zi.at[plus(z, 3), c, yl])
    direct(3)

    def arrive(q):
        f = plus(z, q)
        rc[q].wait_recv()
        share(("left", q), zi.at[f, c, oyl, zl])
        lc[q].wait_recv()
        share(("right", q), zi.at[f, c, oyl, zr])
        across[q].wait_recv()
        share(("across", q), zi.at[f, c, oyl, z2])

    def sibling(q):
        for name in ("own", "left", "right", "across"):
            shared[name, q].wait_recv()

    gram(z2, c, yl, x)
    gram(zl, c, yl, x)
    gram_part(c, xl)
    gram_part(c, xr)
    arrive(0)
    for q in range(1, 4):
        shared["same", q].wait_recv()
    for q in range(1, 4):
        gram(plus(z, q), oc, yl, x)
    gram_part(oc, xl)
    gram_part(oc, xr)
    row_id = lax.broadcasted_iota(jnp.int32, (chunk, chunk), 0)
    col_id = lax.broadcasted_iota(jnp.int32, (chunk, chunk), 1)
    wt[z, c, yl, x] = jnp.where(row_id == col_id, jnp.zeros((), BF16), wt[z, c, yl, x])
    arrive(1)
    sibling(0)
    for cp in slab_fwd:
        cp.wait_recv()
    gram_part(c, x2)
    gram_part(oc, x2)
    gram_block(z)
    arrive(2)
    sibling(1)
    gram_block(zr)
    arrive(3)
    sibling(2)
    gram_block(z2)
    sibling(3)
    gram(zl, c, oyl, x2)
    gram(zl, oc, oyl, x2)

    def products(part_a, k_a, part_b, k_b):
        a = b = jnp.zeros((pair, chunk), F32)
        for f in range(4):
            for cc in range(2):
                for yy in range(2):
                    a = a + lax.dot_general(
                        zi[f, cc, yy, plus(z, k_a)].reshape(pair, chunk),
                        wt[f, cc, yy, part_a],
                        (((1,), (1,)), ((), ())),
                        preferred_element_type=F32,
                    )
                    b = b + lax.dot_general(
                        zi[f, cc, yy, plus(z, k_b)].reshape(pair, chunk),
                        wt[f, cc, yy, part_b],
                        (((1,), (1,)), ((), ())),
                        preferred_element_type=F32,
                    )
        return a, b

    def send_parts(slot, a, b):
        part_out[slot] = a.astype(BF16)
        part_out[slot + 1] = b.astype(BF16)
        right = copy(part_out.at[slot], part_in.at[slot], dev(x_=xr))
        left = copy(part_out.at[slot + 1], part_in.at[slot + 1], dev(x_=xl))
        return right, left

    r, l = {}, {}
    r[0], l[0] = send_parts(0, *products(x2, 2, x2, 0))
    r[1], l[1] = send_parts(2, *products(x2, 1, x2, 3))
    for part in (xr, xl):
        gram(zl, c, oyl, part)
        gram(zl, oc, oyl, part)
    r[2], l[2] = send_parts(4, *products(xr, 0, xl, 2))
    r[3], l[3] = send_parts(6, *products(xr, 3, xl, 1))
    a, b = products(xr, 2, xl, 0)
    r[0].wait_recv()
    l[0].wait_recv()
    r[4], l[4] = send_parts(8, a + part_in[0].astype(F32), b + part_in[1].astype(F32))
    a, b = products(xr, 1, xl, 3)
    r[1].wait_recv()
    l[1].wait_recv()
    r[5], l[5] = send_parts(10, a + part_in[2].astype(F32), b + part_in[3].astype(F32))
    gram(zl, c, oyl, x)
    gram(zl, oc, oyl, x)

    for cp in square_copies:
        cp.wait_recv()
    variance = jnp.zeros((2, cols), F32)
    for d in range(8):
        variance = variance + squares[d]
    spread = jnp.sqrt(variance / (n_rows - 1) + DEVIATION_FLOOR)
    pull = jnp.where(spread < 1.0, -(VARIANCE_WEIGHT * n_rows / (2.0 * (n_rows - 1))) / spread, 0.0)
    mean_a[...], mean_b[...] = mean[0:1, :], mean[1:2, :]
    pull_a[...], pull_b[...] = pull[0:1, :], pull[1:2, :]

    back = []

    def give(k, total):
        zq = plus(z, k)
        rows_out[zq] = total.astype(BF16).reshape(2, local_rows, chunk)
        back.append(copy(rows_out.at[zq, oyh], rows_in.at[yh, z], dev(yh_=oyh, z_=zq)))
        if k == 0:
            rows_in[yh, z] = rows_out[z, yh]
        else:
            back.append(copy(rows_out.at[zq, yh], rows_in.at[yh, z], dev(z_=zq)))

    a, b = products(x, 2, x, 0)
    own[0], own[1] = a, b
    a, b = products(x, 1, x, 3)
    own[2], own[3] = a, b
    l[2].wait_recv()
    r[4].wait_recv()
    give(2, own[0] + (part_in[5].astype(F32) + part_in[8].astype(F32)))
    r[2].wait_recv()
    l[4].wait_recv()
    give(0, own[1] + (part_in[4].astype(F32) + part_in[9].astype(F32)))
    l[3].wait_recv()
    r[5].wait_recv()
    give(1, own[2] + (part_in[7].astype(F32) + part_in[10].astype(F32)))
    r[3].wait_recv()
    l[5].wait_recv()
    give(3, own[3] + (part_in[6].astype(F32) + part_in[11].astype(F32)))
    for cp in back:
        cp.wait_recv()
    for v in range(2):
        for f in range(4):
            cov[v, :, f * chunk : (f + 1) * chunk] = rows_in[v, f]
    for cp in sent:
        cp.wait_send()


def on_device(z_a, z_b):
    rows, cols = z_a.shape
    chunk = cols // 4
    vmem = pl.BlockSpec(memory_space=pltpu.VMEM)
    hbm = pl.BlockSpec(memory_space=pl.ANY)
    cov, mean_a, mean_b, pull_a, pull_b = pl.pallas_call(
        kernel,
        out_shape=[jax.ShapeDtypeStruct((2, rows, cols), BF16), *[jax.ShapeDtypeStruct((1, cols), F32)] * 4],
        in_specs=[hbm, hbm],
        out_specs=[vmem] * 5,
        scratch_shapes=[
            pltpu.VMEM((rows, cols), F32),
            pltpu.VMEM((rows, cols), F32),
            pltpu.VMEM((8, 2, cols), F32),
            pltpu.VMEM((8, 2, cols), F32),
            pltpu.VMEM((4, 2, 2, 4, 2, rows, chunk), BF16),
            pltpu.VMEM((4, rows, chunk), BF16),
            pltpu.VMEM((4, 4, chunk, 2 * rows), BF16),
            pltpu.VMEM((4, 2, 2, 4, chunk, chunk), BF16),
            pltpu.VMEM((12, 2 * rows, chunk), BF16),
            pltpu.VMEM((12, 2 * rows, chunk), BF16),
            pltpu.VMEM((4, 2 * rows, chunk), F32),
            pltpu.VMEM((4, 2, rows, chunk), BF16),
            pltpu.VMEM((2, 4, rows, chunk), BF16),
            pltpu.SemaphoreType.DMA((2,)),
            pltpu.SemaphoreType.DMA((N_COPIES,)),
            pltpu.SemaphoreType.DMA((N_COPIES,)),
        ],
        compiler_params=pltpu.CompilerParams(collective_id=0, has_side_effects=True, vmem_limit_bytes=56 * 1024 * 1024),
        name="vicreg",
    )(z_a, z_b)
    difference = INVARIANCE_WEIGHT * (z_a - z_b)
    dz_a = difference + pull_a * (z_a - mean_a) + cov[0].astype(F32)
    dz_b = pull_b * (z_b - mean_b) - difference + cov[1].astype(F32)
    return dz_a, dz_b


def solution(mesh):
    specs = (P("dp", "mp"), P("dp", "mp"))
    return jax.shard_map(on_device, mesh=mesh, in_specs=specs, out_specs=specs, check_vma=False)
```

```python
import jax
import jax.numpy as jnp
from jax import lax
from jax.experimental import pallas as pl
from jax.experimental.pallas import tpu as pltpu
from jax.sharding import PartitionSpec as P

INVARIANCE_WEIGHT = 25.0
VARIANCE_WEIGHT = 25.0
DEVIATION_FLOOR = 0.0001
HUBER_EDGE = 0.05

MESH = pl.DeviceIdType.MESH
F32 = jnp.float32
BF16 = jnp.bfloat16
N_COPIES = 128


def kernel(za_hbm, zb_hbm, cov, mean_a, mean_b, pull_a, pull_b, za, zb, sums, squares, zi, stage, jt, wt, part_out, part_in, own, rows_out, rows_in, ls, ss, rs):
    dp = lax.axis_index("dp")
    mp = lax.axis_index("mp")
    yh, z = dp // 4, dp % 4
    x, yl, c = mp // 4, (mp // 2) % 2, mp % 2
    local_rows, cols = za.shape
    chunk = cols // 4
    n_rows = local_rows * 8
    pair = 2 * local_rows

    def dev(yh_=None, z_=None, x_=None, yl_=None, c_=None):
        yh_ = yh if yh_ is None else yh_
        z_ = z if z_ is None else z_
        x_ = x if x_ is None else x_
        yl_ = yl if yl_ is None else yl_
        c_ = c if c_ is None else c_
        return (yh_ * 4 + z_, x_ * 4 + yl_ * 2 + c_)

    def plus(v, k):
        return (v + (k % 4)) % 4

    sent = []

    def copy(src, dst, device):
        i = len(sent)
        cp = pltpu.make_async_remote_copy(
            src_ref=src, dst_ref=dst, send_sem=ss.at[i], recv_sem=rs.at[i], device_id=device, device_id_type=MESH
        )
        cp.start()
        sent.append(cp)
        return cp

    zl, zr, z2 = plus(z, -1), plus(z, 1), plus(z, 2)
    xl, xr, x2 = plus(x, -1), plus(x, 1), plus(x, 2)
    oyh, oyl, oc = 1 - yh, 1 - yl, 1 - c
    dp_peers = [(a, b) for a in range(2) for b in range(4) if a or b]

    def peer(a, b):
        return oyh if a else yh, plus(z, b)

    partners = [dev(yh_=peer(a, b)[0], z_=peer(a, b)[1]) for a, b in dp_peers]
    partners += [dev(yl_=oyl), dev(yh_=oyh, yl_=oyl), dev(x_=xl), dev(x_=xr), dev(c_=oc)]
    barrier = pltpu.get_barrier_semaphore()
    for partner in partners:
        pl.semaphore_signal(barrier, inc=1, device_id=partner, device_id_type=MESH)

    loads = [pltpu.make_async_copy(za_hbm, za, ls.at[0]), pltpu.make_async_copy(zb_hbm, zb, ls.at[1])]
    for load in loads:
        load.start()

    for v, ref in enumerate((za, zb)):
        loads[v].wait()
        sums[dp, v : v + 1, :] = jnp.sum(ref[...], axis=0, keepdims=True)
    pl.semaphore_wait(barrier, len(partners))
    def to_peers(ref):
        return [copy(ref, ref, dev(yh_=peer(a, b)[0], z_=peer(a, b)[1])) for a, b in dp_peers]

    for cp in to_peers(sums.at[dp]):
        cp.wait_recv()

    totals = jnp.zeros((2, cols), F32)
    for d in range(8):
        totals = totals + sums[d]
    mean = totals * (1.0 / n_rows)

    first = yh == 0
    for f in range(4):
        cut = slice(f * chunk, (f + 1) * chunk)
        ca = (za[:, cut] - mean[0:1, cut]).astype(BF16)
        cb = (zb[:, cut] - mean[1:2, cut]).astype(BF16)
        zi[f, c, yl, z, yh] = jnp.where(first, ca, cb)
        stage[f] = jnp.where(first, cb, ca)

    right_f = [plus(z, k) for k in (1, 2, 3, 0)]
    left_f = [plus(z, k) for k in (-1, 2, 0, 1)]
    from_left_f = [plus(z, k) for k in (0, 1, 2, 3)]
    from_right_f = [plus(z, k) for k in (0, 3, 1, 2)]

    def mine(f, to):
        return copy(zi.at[f, c, yl, z, yh], zi.at[f, c, yl, z, yh], dev(z_=to))

    def others(f, to):
        return copy(zi.at[f, c, yl, z, oyh], zi.at[f, c, yl, z, oyh], dev(z_=to))

    y1, y02 = {}, {}
    for k in (0, 1, 3, 2):
        f = plus(z, k)
        y1[k] = copy(stage.at[f], zi.at[f, c, yl, z, yh], dev(yh_=oyh))
    ra, rb, la, lb = {}, {}, {}, {}
    for s in range(4):
        ra[s] = mine(right_f[s], zr)
        la[s] = mine(left_f[s], zl)
    for k in (1, 3, 2, 0):
        f = plus(z, k)
        here = zi.at[f, c, yl, z, yh]
        y02[k] = [copy(here, here, dev(yl_=oyl)), copy(stage.at[f], here, dev(yh_=oyh, yl_=oyl))]

    for v, ref in enumerate((za, zb)):
        centered = ref[...] - mean[v : v + 1, :]
        squares[dp, v : v + 1, :] = jnp.sum(centered * centered, axis=0, keepdims=True)
    square_copies = to_peers(squares.at[dp])

    half = chunk // 2
    slab, slab_fwd = {}, []

    def slab_send(q):
        zq = plus(z, q)
        jt[zq, x] = zi[z, c, yl, zq].reshape(pair, chunk).T
        slab[q] = [copy(jt.at[zq, x], jt.at[zq, x], dev(x_=xr)), copy(jt.at[zq, x], jt.at[zq, x], dev(x_=xl))]

    def slab_forward(q):
        zq = plus(z, q)
        for cp in slab[q]:
            cp.wait_recv()
        lo, hi = pl.ds(0, half), pl.ds(half, half)
        slab_fwd.append(copy(jt.at[zq, xl, lo], jt.at[zq, xl, lo], dev(x_=xr)))
        slab_fwd.append(copy(jt.at[zq, xr, hi], jt.at[zq, xr, hi], dev(x_=xl)))

    def forward_right(f):
        ref = zi.at[f, c, yl, zl, yh]
        return copy(ref, ref, dev(z_=zr))

    def forward_left(f):
        ref = zi.at[f, c, yl, zr, oyh]
        return copy(ref, ref, dev(z_=zl))

    fr, fl = {}, {}
    shared = {}

    def share(key, ref):
        shared[key] = copy(ref, ref, dev(c_=oc))

    y1[0].wait_recv()
    slab_send(0)
    y1[1].wait_recv()
    rb[0] = others(right_f[0], zr)
    ra[1].wait_recv()
    fr[0] = forward_right(from_left_f[1])
    y1[3].wait_recv()
    lb[0] = others(left_f[0], zl)
    y1[2].wait_recv()
    rb[1] = others(right_f[1], zr)
    lb[1] = others(left_f[1], zl)
    lb[2] = others(left_f[2], zl)
    ra[2].wait_recv()
    fr[1] = forward_right(from_left_f[2])
    ra[0].wait_recv()
    rb[0].wait_recv()
    slab_send(-1)
    la[0].wait_recv()
    lb[0].wait_recv()
    slab_send(1)
    lb[1].wait_recv()
    fl[0] = forward_left(from_right_f[1])
    lb[3] = others(left_f[3], zl)
    ra[3].wait_recv()
    fr[2] = forward_right(from_left_f[3])
    fl[1] = forward_left(from_right_f[0])
    fr[3] = forward_right(from_left_f[0])
    rb[2] = others(right_f[2], zr)
    rb[3] = others(right_f[3], zr)
    lb[2].wait_recv()
    fl[2] = forward_left(from_right_f[2])
    slab_forward(0)
    for s in range(1, 4):
        la[s].wait_recv()
    rb[1].wait_recv()

    across = {}

    def opposite(q):
        fr[q].wait_recv()
        fl[q].wait_recv()
        f = plus(z, q)
        across[q] = copy(zi.at[f, c, yl, z2], zi.at[f, c, yl, z2], dev(yl_=oyl))

    opposite(0)
    slab_send(2)
    share(("same", 0), zi.at[z, c, yl])

    rc, lc = {}, {}
    right_c = [plus(z, k) for k in (1, 2, 3, 0)]
    left_c = [plus(z, k) for k in (3, 0, 1, 2)]

    def direct(q):
        rc[q] = copy(zi.at[right_c[q], c, oyl, z], zi.at[right_c[q], c, oyl, z], dev(z_=zr))
        lc[q] = copy(zi.at[left_c[q], c, oyl, z], zi.at[left_c[q], c, oyl, z], dev(z_=zl))

    scale = 2.0 * n_rows / (n_rows - 1.0)
    slope = scale / (n_rows - 1.0)
    edge = HUBER_EDGE * scale

    def gram(f, cc, yy, part):
        g = jnp.zeros((chunk, chunk), F32)
        for q in range(4):
            g = g + jnp.dot(jt[q, part], zi[f, cc, yy, q].reshape(pair, chunk), preferred_element_type=F32)
        wt[f, cc, yy, part] = jnp.clip(g * slope, -edge, edge).astype(BF16)

    def gram_part(cc, part):
        for q in range(4):
            gram(plus(z, q), cc, yl, part)

    lb[3].wait_recv()
    fl[3] = forward_left(from_right_f[3])
    for k in (1, 3):
        for cp in y02[k]:
            cp.wait_recv()
        share(("own", k), zi.at[plus(z, k), c, oyl, z])
    direct(0)
    slab_forward(-1)
    slab_forward(1)
    for k in (2, 0):
        for cp in y02[k]:
            cp.wait_recv()
        share(("own", k), zi.at[plus(z, k), c, oyl, z])
    direct(1)
    opposite(1)
    rb[2].wait_recv()
    rb[3].wait_recv()
    share(("same", 1), zi.at[zr, c, yl])
    shared["same", 0].wait_recv()
    gram(z, c, yl, x)
    gram(z, oc, yl, x)
    gram(zr, c, yl, x)
    opposite(2)
    share(("same", 2), zi.at[z2, c, yl])
    slab_forward(2)
    direct(2)
    opposite(3)
    share(("same", 3), zi.at[zl, c, yl])
    direct(3)

    def arrive(q):
        f = plus(z, q)
        rc[q].wait_recv()
        share(("left", q), zi.at[f, c, oyl, zl])
        lc[q].wait_recv()
        share(("right", q), zi.at[f, c, oyl, zr])
        across[q].wait_recv()
        share(("across", q), zi.at[f, c, oyl, z2])

    def sibling(q):
        for name in ("own", "left", "right", "across"):
            shared[name, q].wait_recv()

    gram(z2, c, yl, x)
    gram(zl, c, yl, x)
    gram_part(c, xl)
    gram_part(c, xr)
    arrive(0)
    for q in range(1, 4):
        shared["same", q].wait_recv()
    for q in range(1, 4):
        gram(plus(z, q), oc, yl, x)
    gram_part(oc, xl)
    gram_part(oc, xr)
    row_id = lax.broadcasted_iota(jnp.int32, (chunk, chunk), 0)
    col_id = lax.broadcasted_iota(jnp.int32, (chunk, chunk), 1)
    wt[z, c, yl, x] = jnp.where(row_id == col_id, jnp.zeros((), BF16), wt[z, c, yl, x])
    arrive(1)
    sibling(0)
    for cp in slab_fwd:
        cp.wait_recv()

    def gram_other(q, parts):
        for part in parts:
            for cc in (c, oc):
                gram(plus(z, q), cc, oyl, part)

    gram_part(c, x2)
    gram_part(oc, x2)
    gram_other(0, (x2, xl, xr))
    arrive(2)
    sibling(1)
    sibling(2)
    gram_other(1, (x2,))
    gram_other(2, (x2,))
    arrive(3)
    gram_other(1, (xl, xr))
    sibling(3)
    gram_other(3, (x2,))

    def products(part_a, k_a, part_b, k_b):
        a = b = jnp.zeros((pair, chunk), F32)
        for f in range(4):
            for cc in range(2):
                for yy in range(2):
                    a = a + lax.dot_general(
                        zi[f, cc, yy, plus(z, k_a)].reshape(pair, chunk),
                        wt[f, cc, yy, part_a],
                        (((1,), (1,)), ((), ())),
                        preferred_element_type=F32,
                    )
                    b = b + lax.dot_general(
                        zi[f, cc, yy, plus(z, k_b)].reshape(pair, chunk),
                        wt[f, cc, yy, part_b],
                        (((1,), (1,)), ((), ())),
                        preferred_element_type=F32,
                    )
        return a, b

    def send_parts(slot, a, b):
        part_out[slot] = a.astype(BF16)
        part_out[slot + 1] = b.astype(BF16)
        right = copy(part_out.at[slot], part_in.at[slot], dev(x_=xr))
        left = copy(part_out.at[slot + 1], part_in.at[slot + 1], dev(x_=xl))
        return right, left

    r, l = {}, {}
    r[0], l[0] = send_parts(0, *products(x2, 2, x2, 0))
    r[1], l[1] = send_parts(2, *products(x2, 1, x2, 3))
    gram_other(2, (xl, xr))
    gram_other(3, (xl, xr))
    r[2], l[2] = send_parts(4, *products(xr, 0, xl, 2))
    r[3], l[3] = send_parts(6, *products(xr, 3, xl, 1))
    a, b = products(xr, 2, xl, 0)
    r[0].wait_recv()
    l[0].wait_recv()
    r[4], l[4] = send_parts(8, a + part_in[0].astype(F32), b + part_in[1].astype(F32))
    a, b = products(xr, 1, xl, 3)
    r[1].wait_recv()
    l[1].wait_recv()
    r[5], l[5] = send_parts(10, a + part_in[2].astype(F32), b + part_in[3].astype(F32))
    for q in range(4):
        gram_other(q, (x,))

    for cp in square_copies:
        cp.wait_recv()
    variance = jnp.zeros((2, cols), F32)
    for d in range(8):
        variance = variance + squares[d]
    spread = jnp.sqrt(variance / (n_rows - 1) + DEVIATION_FLOOR)
    pull = jnp.where(spread < 1.0, -(VARIANCE_WEIGHT * n_rows / (2.0 * (n_rows - 1))) / spread, 0.0)
    mean_a[...], mean_b[...] = mean[0:1, :], mean[1:2, :]
    pull_a[...], pull_b[...] = pull[0:1, :], pull[1:2, :]

    back = []

    def give(k, total):
        zq = plus(z, k)
        rows_out[zq] = total.astype(BF16).reshape(2, local_rows, chunk)
        back.append(copy(rows_out.at[zq, oyh], rows_in.at[yh, z], dev(yh_=oyh, z_=zq)))
        if k == 0:
            rows_in[yh, z] = rows_out[z, yh]
        else:
            back.append(copy(rows_out.at[zq, yh], rows_in.at[yh, z], dev(z_=zq)))

    a, b = products(x, 2, x, 0)
    own[0], own[1] = a, b
    a, b = products(x, 1, x, 3)
    own[2], own[3] = a, b
    l[2].wait_recv()
    r[4].wait_recv()
    give(2, own[0] + (part_in[5].astype(F32) + part_in[8].astype(F32)))
    r[2].wait_recv()
    l[4].wait_recv()
    give(0, own[1] + (part_in[4].astype(F32) + part_in[9].astype(F32)))
    l[3].wait_recv()
    r[5].wait_recv()
    give(1, own[2] + (part_in[7].astype(F32) + part_in[10].astype(F32)))
    r[3].wait_recv()
    l[5].wait_recv()
    give(3, own[3] + (part_in[6].astype(F32) + part_in[11].astype(F32)))
    for cp in back:
        cp.wait_recv()
    for v in range(2):
        for f in range(4):
            cov[v, :, f * chunk : (f + 1) * chunk] = rows_in[v, f]
    for cp in sent:
        cp.wait_send()


def on_device(z_a, z_b):
    rows, cols = z_a.shape
    chunk = cols // 4
    vmem = pl.BlockSpec(memory_space=pltpu.VMEM)
    hbm = pl.BlockSpec(memory_space=pl.ANY)
    cov, mean_a, mean_b, pull_a, pull_b = pl.pallas_call(
        kernel,
        out_shape=[jax.ShapeDtypeStruct((2, rows, cols), BF16), *[jax.ShapeDtypeStruct((1, cols), F32)] * 4],
        in_specs=[hbm, hbm],
        out_specs=[vmem] * 5,
        scratch_shapes=[
            pltpu.VMEM((rows, cols), F32),
            pltpu.VMEM((rows, cols), F32),
            pltpu.VMEM((8, 2, cols), F32),
            pltpu.VMEM((8, 2, cols), F32),
            pltpu.VMEM((4, 2, 2, 4, 2, rows, chunk), BF16),
            pltpu.VMEM((4, rows, chunk), BF16),
            pltpu.VMEM((4, 4, chunk, 2 * rows), BF16),
            pltpu.VMEM((4, 2, 2, 4, chunk, chunk), BF16),
            pltpu.VMEM((12, 2 * rows, chunk), BF16),
            pltpu.VMEM((12, 2 * rows, chunk), BF16),
            pltpu.VMEM((4, 2 * rows, chunk), F32),
            pltpu.VMEM((4, 2, rows, chunk), BF16),
            pltpu.VMEM((2, 4, rows, chunk), BF16),
            pltpu.SemaphoreType.DMA((2,)),
            pltpu.SemaphoreType.DMA((N_COPIES,)),
            pltpu.SemaphoreType.DMA((N_COPIES,)),
        ],
        compiler_params=pltpu.CompilerParams(collective_id=0, has_side_effects=True, vmem_limit_bytes=56 * 1024 * 1024),
        name="vicreg",
    )(z_a, z_b)
    difference = INVARIANCE_WEIGHT * (z_a - z_b)
    dz_a = difference + pull_a * (z_a - mean_a) + cov[0].astype(F32)
    dz_b = pull_b * (z_b - mean_b) - difference + cov[1].astype(F32)
    return dz_a, dz_b


def solution(mesh):
    specs = (P("dp", "mp"), P("dp", "mp"))
    return jax.shard_map(on_device, mesh=mesh, in_specs=specs, out_specs=specs, check_vma=False)
```

```python
import jax
import jax.numpy as jnp
from jax import lax
from jax.experimental import pallas as pl
from jax.experimental.pallas import tpu as pltpu
from jax.sharding import PartitionSpec as P

INVARIANCE_WEIGHT = 25.0
VARIANCE_WEIGHT = 25.0
DEVIATION_FLOOR = 0.0001
HUBER_EDGE = 0.05

MESH = pl.DeviceIdType.MESH
F32 = jnp.float32
BF16 = jnp.bfloat16
N_COPIES = 136


def kernel(za_hbm, zb_hbm, cov, mean_a, mean_b, pull_a, pull_b, za, zb, sums, squares, zi, stage, jt, wt, part_out, part_in, own, rows_out, rows_in, ls, ss, rs):
    dp = lax.axis_index("dp")
    mp = lax.axis_index("mp")
    yh, z = dp // 4, dp % 4
    x, yl, c = mp // 4, (mp // 2) % 2, mp % 2
    local_rows, cols = za.shape
    chunk = cols // 4
    n_rows = local_rows * 8
    pair = 2 * local_rows

    def dev(yh_=None, z_=None, x_=None, yl_=None, c_=None):
        yh_ = yh if yh_ is None else yh_
        z_ = z if z_ is None else z_
        x_ = x if x_ is None else x_
        yl_ = yl if yl_ is None else yl_
        c_ = c if c_ is None else c_
        return (yh_ * 4 + z_, x_ * 4 + yl_ * 2 + c_)

    def plus(v, k):
        return (v + (k % 4)) % 4

    sent = []

    def copy(src, dst, device):
        i = len(sent)
        cp = pltpu.make_async_remote_copy(
            src_ref=src, dst_ref=dst, send_sem=ss.at[i], recv_sem=rs.at[i], device_id=device, device_id_type=MESH
        )
        cp.start()
        sent.append(cp)
        return cp

    zl, zr, z2 = plus(z, -1), plus(z, 1), plus(z, 2)
    xl, xr, x2 = plus(x, -1), plus(x, 1), plus(x, 2)
    oyh, oyl, oc = 1 - yh, 1 - yl, 1 - c
    dp_peers = [(a, b) for a in range(2) for b in range(4) if a or b]

    def peer(a, b):
        return oyh if a else yh, plus(z, b)

    partners = [dev(yh_=peer(a, b)[0], z_=peer(a, b)[1]) for a, b in dp_peers]
    partners += [dev(yl_=oyl), dev(yh_=oyh, yl_=oyl), dev(x_=xl), dev(x_=xr), dev(c_=oc)]
    barrier = pltpu.get_barrier_semaphore()
    for partner in partners:
        pl.semaphore_signal(barrier, inc=1, device_id=partner, device_id_type=MESH)

    loads = [pltpu.make_async_copy(za_hbm, za, ls.at[0]), pltpu.make_async_copy(zb_hbm, zb, ls.at[1])]
    for load in loads:
        load.start()

    for v, ref in enumerate((za, zb)):
        loads[v].wait()
        sums[dp, v : v + 1, :] = jnp.sum(ref[...], axis=0, keepdims=True)
    pl.semaphore_wait(barrier, len(partners))
    def to_peers(ref):
        return [copy(ref, ref, dev(yh_=peer(a, b)[0], z_=peer(a, b)[1])) for a, b in dp_peers]

    for cp in to_peers(sums.at[dp]):
        cp.wait_recv()

    totals = jnp.zeros((2, cols), F32)
    for d in range(8):
        totals = totals + sums[d]
    mean = totals * (1.0 / n_rows)

    first = yh == 0
    for f in range(4):
        cut = slice(f * chunk, (f + 1) * chunk)
        ca = (za[:, cut] - mean[0:1, cut]).astype(BF16)
        cb = (zb[:, cut] - mean[1:2, cut]).astype(BF16)
        zi[f, c, yl, z, yh] = jnp.where(first, ca, cb)
        stage[f] = jnp.where(first, cb, ca)

    right_f = [plus(z, k) for k in (1, 2, 3, 0)]
    left_f = [plus(z, k) for k in (-1, 2, 0, 1)]
    from_left_f = [plus(z, k) for k in (0, 1, 2, 3)]
    from_right_f = [plus(z, k) for k in (0, 3, 1, 2)]

    def mine(f, to):
        return copy(zi.at[f, c, yl, z, yh], zi.at[f, c, yl, z, yh], dev(z_=to))

    def others(f, to):
        return copy(zi.at[f, c, yl, z, oyh], zi.at[f, c, yl, z, oyh], dev(z_=to))

    y1, y02 = {}, {}
    for k in (0, 1, 3, 2):
        f = plus(z, k)
        y1[k] = copy(stage.at[f], zi.at[f, c, yl, z, yh], dev(yh_=oyh))
    ra, rb, la, lb = {}, {}, {}, {}
    for s in range(4):
        ra[s] = mine(right_f[s], zr)
        la[s] = mine(left_f[s], zl)
    for k in (1, 3, 2, 0):
        f = plus(z, k)
        here = zi.at[f, c, yl, z, yh]
        y02[k] = [copy(here, here, dev(yl_=oyl)), copy(stage.at[f], here, dev(yh_=oyh, yl_=oyl))]

    for v, ref in enumerate((za, zb)):
        centered = ref[...] - mean[v : v + 1, :]
        squares[dp, v : v + 1, :] = jnp.sum(centered * centered, axis=0, keepdims=True)
    square_copies = to_peers(squares.at[dp])

    half = chunk // 2
    slab, slab_fwd = {}, []

    def slab_send(q):
        zq = plus(z, q)
        jt[zq, x] = zi[z, c, yl, zq].reshape(pair, chunk).T
        slab[q] = [copy(jt.at[zq, x], jt.at[zq, x], dev(x_=xr)), copy(jt.at[zq, x], jt.at[zq, x], dev(x_=xl))]

    def slab_forward(q):
        zq = plus(z, q)
        for cp in slab[q]:
            cp.wait_recv()
        lo, hi = pl.ds(0, half), pl.ds(half, half)
        slab_fwd.append(copy(jt.at[zq, xl, lo], jt.at[zq, xl, lo], dev(x_=xr)))
        slab_fwd.append(copy(jt.at[zq, xr, hi], jt.at[zq, xr, hi], dev(x_=xl)))

    def forward_right(f):
        ref = zi.at[f, c, yl, zl, yh]
        return copy(ref, ref, dev(z_=zr))

    def forward_left(f):
        ref = zi.at[f, c, yl, zr, oyh]
        return copy(ref, ref, dev(z_=zl))

    fr, fl = {}, {}
    shared = {}

    def share(key, ref):
        shared[key] = copy(ref, ref, dev(c_=oc))

    y1[0].wait_recv()
    slab_send(0)
    y1[1].wait_recv()
    rb[0] = others(right_f[0], zr)
    ra[1].wait_recv()
    fr[0] = forward_right(from_left_f[1])
    y1[3].wait_recv()
    lb[0] = others(left_f[0], zl)
    y1[2].wait_recv()
    rb[1] = others(right_f[1], zr)
    lb[1] = others(left_f[1], zl)
    lb[2] = others(left_f[2], zl)
    ra[2].wait_recv()
    fr[1] = forward_right(from_left_f[2])

    def to_other(ref):
        return copy(ref, ref, dev(yl_=oyl))

    ra[0].wait_recv()
    rb[0].wait_recv()
    slab_send(-1)
    near_left = to_other(zi.at[z, c, yl, zl])
    la[0].wait_recv()
    lb[0].wait_recv()
    slab_send(1)
    near_right = to_other(zi.at[z, c, yl, zr])
    across = {q: [] for q in range(4)}

    def opposite_mine(q):
        fr[q].wait_recv()
        across[q].append(to_other(zi.at[plus(z, q), c, yl, z2, yh]))

    def opposite_others(q):
        fl[q].wait_recv()
        across[q].append(to_other(zi.at[plus(z, q), c, yl, z2, oyh]))
        share(("same", q), zi.at[plus(z, q), c, yl])

    lb[1].wait_recv()
    fl[0] = forward_left(from_right_f[1])
    lb[3] = others(left_f[3], zl)
    ra[3].wait_recv()
    fr[2] = forward_right(from_left_f[3])
    fl[1] = forward_left(from_right_f[0])
    fr[3] = forward_right(from_left_f[0])
    rb[2] = others(right_f[2], zr)
    rb[3] = others(right_f[3], zr)
    opposite_mine(0)
    lb[2].wait_recv()
    fl[2] = forward_left(from_right_f[2])
    slab_forward(0)
    for s in range(1, 4):
        la[s].wait_recv()
    rb[1].wait_recv()
    opposite_mine(1)
    opposite_others(0)
    slab_send(2)
    lb[3].wait_recv()
    fl[3] = forward_left(from_right_f[3])
    opposite_mine(2)
    opposite_mine(3)

    rc, lc = {}, {}
    right_c = [plus(z, k) for k in (1, 2, 3, 0)]
    left_c = [plus(z, k) for k in (3, 0, 1, 2)]

    def direct(q):
        rc[q] = copy(zi.at[right_c[q], c, oyl, z], zi.at[right_c[q], c, oyl, z], dev(z_=zr))
        lc[q] = copy(zi.at[left_c[q], c, oyl, z], zi.at[left_c[q], c, oyl, z], dev(z_=zl))

    scale = 2.0 * n_rows / (n_rows - 1.0)
    slope = scale / (n_rows - 1.0)
    edge = HUBER_EDGE * scale

    def gram(f, cc, yy, part):
        g = jnp.zeros((chunk, chunk), F32)
        for q in range(4):
            g = g + jnp.dot(jt[q, part], zi[f, cc, yy, q].reshape(pair, chunk), preferred_element_type=F32)
        wt[f, cc, yy, part] = jnp.clip(g * slope, -edge, edge).astype(BF16)

    def gram_part(cc, part):
        for q in range(4):
            gram(plus(z, q), cc, yl, part)

    for k in (2, 0, 3, 1):
        for cp in y02[k]:
            cp.wait_recv()
        share(("own", k), zi.at[plus(z, k), c, oyl, z])
    direct(1)
    slab_forward(-1)
    slab_forward(1)
    rb[2].wait_recv()
    rb[3].wait_recv()
    opposite_others(1)
    direct(2)
    shared["same", 0].wait_recv()
    gram(z, c, yl, x)
    gram(z, oc, yl, x)
    gram(zr, c, yl, x)
    slab_forward(2)
    opposite_others(2)
    direct(3)
    opposite_others(3)

    def arrive(q):
        f = plus(z, q)
        (rc[q] if q else near_left).wait_recv()
        share(("left", q), zi.at[f, c, oyl, zl])
        (lc[q] if q else near_right).wait_recv()
        share(("right", q), zi.at[f, c, oyl, zr])
        for cp in across[q]:
            cp.wait_recv()
        share(("across", q), zi.at[f, c, oyl, z2])

    def sibling(q):
        for name in ("own", "left", "right", "across"):
            shared[name, q].wait_recv()

    gram(z2, c, yl, x)
    gram(zl, c, yl, x)
    gram_part(c, xl)
    gram_part(c, xr)
    arrive(0)
    for q in range(1, 4):
        shared["same", q].wait_recv()
    for q in range(1, 4):
        gram(plus(z, q), oc, yl, x)
    gram_part(oc, xl)
    gram_part(oc, xr)
    row_id = lax.broadcasted_iota(jnp.int32, (chunk, chunk), 0)
    col_id = lax.broadcasted_iota(jnp.int32, (chunk, chunk), 1)
    wt[z, c, yl, x] = jnp.where(row_id == col_id, jnp.zeros((), BF16), wt[z, c, yl, x])
    arrive(1)
    sibling(0)
    for cp in slab_fwd:
        cp.wait_recv()

    def gram_other(q, parts):
        for part in parts:
            for cc in (c, oc):
                gram(plus(z, q), cc, oyl, part)

    gram_part(c, x2)
    gram_part(oc, x2)
    gram_other(0, (x2,))
    arrive(2)
    sibling(1)
    sibling(2)
    gram_other(1, (x2,))
    gram_other(2, (x2,))

    blocks = [(plus(z, q), cc, yy) for q in range(4) for yy in (yl, oyl) for cc in (0, 1)]

    def products(tiles, over, start=None):
        accs = [jnp.zeros((pair, chunk), F32) for _ in tiles] if start is None else start
        for f, cc, yy in over:
            for i, (part, k) in enumerate(tiles):
                accs[i] = accs[i] + lax.dot_general(
                    zi[f, cc, yy, plus(z, k)].reshape(pair, chunk),
                    wt[f, cc, yy, part],
                    (((1,), (1,)), ((), ())),
                    preferred_element_type=F32,
                )
        return accs

    def keep(slot, value):
        part_out[slot] = value.astype(BF16).reshape(2, local_rows, chunk)

    def send_parts(slot):
        right = copy(part_out.at[slot], part_in.at[slot], dev(x_=xr))
        left = copy(part_out.at[slot + 1], part_in.at[slot + 1], dev(x_=xl))
        return right, left

    def send_halves(slot):
        return [
            [copy(part_out.at[i, p], part_in.at[i, p], dev(x_=to)) for p in (oyh, yh)]
            for i, to in ((slot, xr), (slot + 1, xl))
        ]

    def taken(slot):
        return part_in[slot].astype(F32).reshape(pair, chunk)

    turn = [(x2, 2), (x2, 0), (x2, 1), (x2, 3)]
    for i, acc in enumerate(products(turn, blocks[:14])):
        own[i] = acc
    arrive(3)
    sibling(3)
    gram_other(3, (x2,))
    for i, acc in enumerate(products(turn, blocks[14:], [own[i] for i in range(4)])):
        keep(i, acc)
    r, l = {}, {}
    r[0], l[0] = send_parts(0)
    r[1], l[1] = send_parts(2)
    for q in range(4):
        gram_other(q, (xl, xr))
    a, b = products([(xr, 0), (xl, 2)], blocks)
    keep(4, a)
    keep(5, b)
    r[2], l[2] = send_parts(4)
    a, b = products([(xr, 3), (xl, 1)], blocks)
    keep(6, a)
    keep(7, b)
    r[3], l[3] = send_parts(6)
    a, b = products([(xr, 2), (xl, 0)], blocks)
    r[0].wait_recv()
    l[0].wait_recv()
    keep(8, a + taken(0))
    keep(9, b + taken(1))
    r[4], l[4] = send_halves(8)
    a, b = products([(xr, 1), (xl, 3)], blocks)
    r[1].wait_recv()
    l[1].wait_recv()
    keep(10, a + taken(2))
    keep(11, b + taken(3))
    r[5], l[5] = send_halves(10)
    for q in range(4):
        gram_other(q, (x,))

    for cp in square_copies:
        cp.wait_recv()
    variance = jnp.zeros((2, cols), F32)
    for d in range(8):
        variance = variance + squares[d]
    spread = jnp.sqrt(variance / (n_rows - 1) + DEVIATION_FLOOR)
    pull = jnp.where(spread < 1.0, -(VARIANCE_WEIGHT * n_rows / (2.0 * (n_rows - 1))) / spread, 0.0)
    mean_a[...], mean_b[...] = mean[0:1, :], mean[1:2, :]
    pull_a[...], pull_b[...] = pull[0:1, :], pull[1:2, :]

    for k in (2, 1):
        a, b = products([(x, k), (x, (k + 2) % 4)], blocks)
        own[k] = a
        own[(k + 2) % 4] = b
    back = []

    def give(k, which, straight, summed, far):
        zq = plus(z, k)
        p = (oyh, yh)[which]
        far[which].wait_recv()
        rows = pl.ds(pl.multiple_of(p * local_rows, local_rows), local_rows)
        total = own[k, rows, :] + (part_in[straight, p].astype(F32) + part_in[summed, p].astype(F32))
        rows_out[zq, p] = total.astype(BF16)
        if k or not which:
            back.append(copy(rows_out.at[zq, p], rows_in.at[yh, z], dev(yh_=p, z_=zq)))
        else:
            rows_in[yh, z] = rows_out[z, yh]

    l[2].wait_recv()
    r[2].wait_recv()
    for which in (0, 1):
        give(2, which, 5, 8, r[4])
        give(0, which, 4, 9, l[4])
    l[3].wait_recv()
    r[3].wait_recv()
    for which in (0, 1):
        give(1, which, 7, 10, r[5])
        give(3, which, 6, 11, l[5])
    for cp in back:
        cp.wait_recv()
    for v in range(2):
        for f in range(4):
            cov[v, :, f * chunk : (f + 1) * chunk] = rows_in[v, f]
    for cp in sent:
        cp.wait_send()


def on_device(z_a, z_b):
    rows, cols = z_a.shape
    chunk = cols // 4
    vmem = pl.BlockSpec(memory_space=pltpu.VMEM)
    hbm = pl.BlockSpec(memory_space=pl.ANY)
    cov, mean_a, mean_b, pull_a, pull_b = pl.pallas_call(
        kernel,
        out_shape=[jax.ShapeDtypeStruct((2, rows, cols), BF16), *[jax.ShapeDtypeStruct((1, cols), F32)] * 4],
        in_specs=[hbm, hbm],
        out_specs=[vmem] * 5,
        scratch_shapes=[
            pltpu.VMEM((rows, cols), F32),
            pltpu.VMEM((rows, cols), F32),
            pltpu.VMEM((8, 2, cols), F32),
            pltpu.VMEM((8, 2, cols), F32),
            pltpu.VMEM((4, 2, 2, 4, 2, rows, chunk), BF16),
            pltpu.VMEM((4, rows, chunk), BF16),
            pltpu.VMEM((4, 4, chunk, 2 * rows), BF16),
            pltpu.VMEM((4, 2, 2, 4, chunk, chunk), BF16),
            pltpu.VMEM((12, 2, rows, chunk), BF16),
            pltpu.VMEM((12, 2, rows, chunk), BF16),
            pltpu.VMEM((4, 2 * rows, chunk), F32),
            pltpu.VMEM((4, 2, rows, chunk), BF16),
            pltpu.VMEM((2, 4, rows, chunk), BF16),
            pltpu.SemaphoreType.DMA((2,)),
            pltpu.SemaphoreType.DMA((N_COPIES,)),
            pltpu.SemaphoreType.DMA((N_COPIES,)),
        ],
        compiler_params=pltpu.CompilerParams(collective_id=0, has_side_effects=True, vmem_limit_bytes=56 * 1024 * 1024),
        name="vicreg",
    )(z_a, z_b)
    difference = INVARIANCE_WEIGHT * (z_a - z_b)
    dz_a = difference + pull_a * (z_a - mean_a) + cov[0].astype(F32)
    dz_b = pull_b * (z_b - mean_b) - difference + cov[1].astype(F32)
    return dz_a, dz_b


def solution(mesh):
    specs = (P("dp", "mp"), P("dp", "mp"))
    return jax.shard_map(on_device, mesh=mesh, in_specs=specs, out_specs=specs, check_vma=False)
```

```python
import jax
import jax.numpy as jnp
from jax import lax
from jax.experimental import pallas as pl
from jax.experimental.pallas import tpu as pltpu
from jax.sharding import PartitionSpec as P

INVARIANCE_WEIGHT = 25.0
VARIANCE_WEIGHT = 25.0
DEVIATION_FLOOR = 0.0001
HUBER_EDGE = 0.05

MESH = pl.DeviceIdType.MESH
F32 = jnp.float32
BF16 = jnp.bfloat16
N_COPIES = 136


def kernel(za_hbm, zb_hbm, cov, mean_a, mean_b, pull_a, pull_b, za, zb, sums, squares, zi, stage, jt, wt, part_out, part_in, own, rows_out, rows_in, ls, ss, rs):
    dp = lax.axis_index("dp")
    mp = lax.axis_index("mp")
    yh, z = dp // 4, dp % 4
    x, yl, c = mp // 4, (mp // 2) % 2, mp % 2
    local_rows, cols = za.shape
    chunk = cols // 4
    n_rows = local_rows * 8
    pair = 2 * local_rows

    def dev(yh_=None, z_=None, x_=None, yl_=None, c_=None):
        yh_ = yh if yh_ is None else yh_
        z_ = z if z_ is None else z_
        x_ = x if x_ is None else x_
        yl_ = yl if yl_ is None else yl_
        c_ = c if c_ is None else c_
        return (yh_ * 4 + z_, x_ * 4 + yl_ * 2 + c_)

    def plus(v, k):
        return (v + (k % 4)) % 4

    sent = []

    def copy(src, dst, device):
        i = len(sent)
        cp = pltpu.make_async_remote_copy(
            src_ref=src, dst_ref=dst, send_sem=ss.at[i], recv_sem=rs.at[i], device_id=device, device_id_type=MESH
        )
        cp.start()
        sent.append(cp)
        return cp

    zl, zr, z2 = plus(z, -1), plus(z, 1), plus(z, 2)
    xl, xr, x2 = plus(x, -1), plus(x, 1), plus(x, 2)
    oyh, oyl, oc = 1 - yh, 1 - yl, 1 - c
    dp_peers = [(a, b) for a in range(2) for b in range(4) if a or b]

    def peer(a, b):
        return oyh if a else yh, plus(z, b)

    partners = [dev(yh_=peer(a, b)[0], z_=peer(a, b)[1]) for a, b in dp_peers]
    partners += [dev(yl_=oyl), dev(yh_=oyh, yl_=oyl), dev(x_=xl), dev(x_=xr), dev(c_=oc)]
    barrier = pltpu.get_barrier_semaphore()
    for partner in partners:
        pl.semaphore_signal(barrier, inc=1, device_id=partner, device_id_type=MESH)

    loads = [pltpu.make_async_copy(za_hbm, za, ls.at[0]), pltpu.make_async_copy(zb_hbm, zb, ls.at[1])]
    for load in loads:
        load.start()

    for v, ref in enumerate((za, zb)):
        loads[v].wait()
        sums[dp, v : v + 1, :] = jnp.sum(ref[...], axis=0, keepdims=True)
    pl.semaphore_wait(barrier, len(partners))
    def to_peers(ref):
        return [copy(ref, ref, dev(yh_=peer(a, b)[0], z_=peer(a, b)[1])) for a, b in dp_peers]

    for cp in to_peers(sums.at[dp]):
        cp.wait_recv()

    totals = jnp.zeros((2, cols), F32)
    for d in range(8):
        totals = totals + sums[d]
    mean = totals * (1.0 / n_rows)

    first = yh == 0
    for f in range(4):
        cut = slice(f * chunk, (f + 1) * chunk)
        ca = (za[:, cut] - mean[0:1, cut]).astype(BF16)
        cb = (zb[:, cut] - mean[1:2, cut]).astype(BF16)
        zi[f, c, yl, z, yh] = jnp.where(first, ca, cb)
        stage[f] = jnp.where(first, cb, ca)

    right_f = [plus(z, k) for k in (1, 2, 3, 0)]
    left_f = [plus(z, k) for k in (-1, 2, 0, 1)]
    from_left_f = [plus(z, k) for k in (0, 1, 2, 3)]
    from_right_f = [plus(z, k) for k in (0, 3, 1, 2)]

    def mine(f, to):
        return copy(zi.at[f, c, yl, z, yh], zi.at[f, c, yl, z, yh], dev(z_=to))

    def others(f, to):
        return copy(zi.at[f, c, yl, z, oyh], zi.at[f, c, yl, z, oyh], dev(z_=to))

    y1, y02 = {}, {}
    for k in (0, 1, 3, 2):
        f = plus(z, k)
        y1[k] = copy(stage.at[f], zi.at[f, c, yl, z, yh], dev(yh_=oyh))
    ra, rb, la, lb = {}, {}, {}, {}
    for s in range(4):
        ra[s] = mine(right_f[s], zr)
        la[s] = mine(left_f[s], zl)
    for k in (1, 3, 2, 0):
        f = plus(z, k)
        here = zi.at[f, c, yl, z, yh]
        y02[k] = [copy(here, here, dev(yl_=oyl)), copy(stage.at[f], here, dev(yh_=oyh, yl_=oyl))]

    for v, ref in enumerate((za, zb)):
        centered = ref[...] - mean[v : v + 1, :]
        squares[dp, v : v + 1, :] = jnp.sum(centered * centered, axis=0, keepdims=True)
    square_copies = to_peers(squares.at[dp])

    half = chunk // 2
    slab, slab_fwd = {}, []

    def slab_send(q):
        zq = plus(z, q)
        jt[zq, x] = zi[z, c, yl, zq].reshape(pair, chunk).T
        slab[q] = [copy(jt.at[zq, x], jt.at[zq, x], dev(x_=xr)), copy(jt.at[zq, x], jt.at[zq, x], dev(x_=xl))]

    def slab_forward(q):
        zq = plus(z, q)
        for cp in slab[q]:
            cp.wait_recv()
        lo, hi = pl.ds(0, half), pl.ds(half, half)
        slab_fwd.append(copy(jt.at[zq, xl, lo], jt.at[zq, xl, lo], dev(x_=xr)))
        slab_fwd.append(copy(jt.at[zq, xr, hi], jt.at[zq, xr, hi], dev(x_=xl)))

    def forward_right(f):
        ref = zi.at[f, c, yl, zl, yh]
        return copy(ref, ref, dev(z_=zr))

    def forward_left(f):
        ref = zi.at[f, c, yl, zr, oyh]
        return copy(ref, ref, dev(z_=zl))

    fr, fl = {}, {}
    shared = {}

    def share(key, ref):
        shared[key] = copy(ref, ref, dev(c_=oc))

    y1[0].wait_recv()
    slab_send(0)
    y1[1].wait_recv()
    rb[0] = others(right_f[0], zr)
    ra[1].wait_recv()
    fr[0] = forward_right(from_left_f[1])
    y1[3].wait_recv()
    lb[0] = others(left_f[0], zl)
    y1[2].wait_recv()
    rb[1] = others(right_f[1], zr)
    lb[1] = others(left_f[1], zl)
    lb[2] = others(left_f[2], zl)
    ra[2].wait_recv()
    fr[1] = forward_right(from_left_f[2])

    def to_other(ref):
        return copy(ref, ref, dev(yl_=oyl))

    ra[0].wait_recv()
    rb[0].wait_recv()
    slab_send(-1)
    near_left = to_other(zi.at[z, c, yl, zl])
    la[0].wait_recv()
    lb[0].wait_recv()
    slab_send(1)
    near_right = to_other(zi.at[z, c, yl, zr])
    across = {q: [] for q in range(4)}

    def opposite_mine(q):
        fr[q].wait_recv()
        across[q].append(to_other(zi.at[plus(z, q), c, yl, z2, yh]))

    def opposite_others(q):
        fl[q].wait_recv()
        across[q].append(to_other(zi.at[plus(z, q), c, yl, z2, oyh]))
        share(("same", q), zi.at[plus(z, q), c, yl])

    lb[1].wait_recv()
    fl[0] = forward_left(from_right_f[1])
    lb[3] = others(left_f[3], zl)
    ra[3].wait_recv()
    fr[2] = forward_right(from_left_f[3])
    fl[1] = forward_left(from_right_f[0])
    fr[3] = forward_right(from_left_f[0])
    rb[2] = others(right_f[2], zr)
    rb[3] = others(right_f[3], zr)
    opposite_mine(0)
    lb[2].wait_recv()
    fl[2] = forward_left(from_right_f[2])
    slab_forward(0)
    for s in range(1, 4):
        la[s].wait_recv()
    rb[1].wait_recv()
    opposite_mine(1)
    opposite_others(0)
    slab_send(2)
    lb[3].wait_recv()
    fl[3] = forward_left(from_right_f[3])
    opposite_mine(2)
    opposite_mine(3)

    rc, lc = {}, {}
    right_c = [plus(z, k) for k in (1, 2, 3, 0)]
    left_c = [plus(z, k) for k in (3, 0, 1, 2)]

    def direct(q):
        rc[q] = copy(zi.at[right_c[q], c, oyl, z], zi.at[right_c[q], c, oyl, z], dev(z_=zr))
        lc[q] = copy(zi.at[left_c[q], c, oyl, z], zi.at[left_c[q], c, oyl, z], dev(z_=zl))

    scale = 2.0 * n_rows / (n_rows - 1.0)
    slope = scale / (n_rows - 1.0)
    edge = HUBER_EDGE * scale

    def gram(f, cc, yy, part):
        g = jnp.zeros((chunk, chunk), F32)
        for q in range(4):
            g = g + jnp.dot(jt[q, part], zi[f, cc, yy, q].reshape(pair, chunk), preferred_element_type=F32)
        wt[f, cc, yy, part] = jnp.clip(g * slope, -edge, edge).astype(BF16)

    def gram_part(cc, part):
        for q in range(4):
            gram(plus(z, q), cc, yl, part)

    for k in (2, 0, 3, 1):
        for cp in y02[k]:
            cp.wait_recv()
        share(("own", k), zi.at[plus(z, k), c, oyl, z])
    direct(1)
    slab_forward(-1)
    slab_forward(1)
    rb[2].wait_recv()
    rb[3].wait_recv()
    opposite_others(1)
    direct(2)
    shared["same", 0].wait_recv()
    gram(z, c, yl, x)
    gram(z, oc, yl, x)
    gram(zr, c, yl, x)
    slab_forward(2)
    opposite_others(2)
    direct(3)
    shared["same", 1].wait_recv()
    gram(z2, c, yl, x)
    gram(zr, oc, yl, x)
    for part in (xl, xr):
        gram(z, c, yl, part)
        gram(z, oc, yl, part)
        gram(zr, c, yl, part)
    opposite_others(3)

    def arrive(q):
        f = plus(z, q)
        (rc[q] if q else near_left).wait_recv()
        share(("left", q), zi.at[f, c, oyl, zl])
        (lc[q] if q else near_right).wait_recv()
        share(("right", q), zi.at[f, c, oyl, zr])
        for cp in across[q]:
            cp.wait_recv()
        share(("across", q), zi.at[f, c, oyl, z2])

    def sibling(q):
        for name in ("own", "left", "right", "across"):
            shared[name, q].wait_recv()

    for part in (xl, xr):
        gram(z2, c, yl, part)
        gram(zl, c, yl, part)
    arrive(0)
    arrive(1)
    for q in (2, 3):
        shared["same", q].wait_recv()
    sibling(0)
    for cp in slab_fwd:
        cp.wait_recv()

    def gram_other(q, parts):
        for part in parts:
            for cc in (c, oc):
                gram(plus(z, q), cc, oyl, part)

    gram_part(c, x2)
    gram_part(oc, x2)
    gram_other(0, (x2,))
    arrive(2)
    sibling(1)
    sibling(2)
    gram_other(1, (x2,))
    gram_other(2, (x2,))

    blocks = [(plus(z, q), cc, yy) for q in range(4) for yy in (yl, oyl) for cc in (0, 1)]

    def products(tiles, over, start=None):
        accs = [jnp.zeros((pair, chunk), F32) for _ in tiles] if start is None else start
        for f, cc, yy in over:
            for i, (part, k) in enumerate(tiles):
                accs[i] = accs[i] + lax.dot_general(
                    zi[f, cc, yy, plus(z, k)].reshape(pair, chunk),
                    wt[f, cc, yy, part],
                    (((1,), (1,)), ((), ())),
                    preferred_element_type=F32,
                )
        return accs

    def keep(slot, value):
        part_out[slot] = value.astype(BF16).reshape(2, local_rows, chunk)

    def send_parts(slot):
        right = copy(part_out.at[slot], part_in.at[slot], dev(x_=xr))
        left = copy(part_out.at[slot + 1], part_in.at[slot + 1], dev(x_=xl))
        return right, left

    def send_halves(slot):
        return [
            [copy(part_out.at[i, p], part_in.at[i, p], dev(x_=to)) for p in (oyh, yh)]
            for i, to in ((slot, xr), (slot + 1, xl))
        ]

    def taken(slot):
        return part_in[slot].astype(F32).reshape(pair, chunk)

    turn = [(x2, 2), (x2, 0), (x2, 1), (x2, 3)]
    for i, acc in enumerate(products(turn, blocks[:14])):
        own[i] = acc
    arrive(3)
    sibling(3)
    gram_other(3, (x2,))
    for i, acc in enumerate(products(turn, blocks[14:], [own[i] for i in range(4)])):
        keep(i, acc)
    r, l = {}, {}
    r[0], l[0] = send_parts(0)
    r[1], l[1] = send_parts(2)
    for part in (xl, xr):
        for f in (zr, z2, zl):
            gram(f, oc, yl, part)
    for q in range(4):
        gram_other(q, (xl, xr))
    a, b = products([(xr, 0), (xl, 2)], blocks)
    keep(4, a)
    keep(5, b)
    r[2], l[2] = send_parts(4)
    a, b = products([(xr, 3), (xl, 1)], blocks)
    keep(6, a)
    keep(7, b)
    r[3], l[3] = send_parts(6)
    a, b = products([(xr, 2), (xl, 0)], blocks)
    r[0].wait_recv()
    l[0].wait_recv()
    keep(8, a + taken(0))
    keep(9, b + taken(1))
    r[4], l[4] = send_halves(8)
    a, b = products([(xr, 1), (xl, 3)], blocks)
    r[1].wait_recv()
    l[1].wait_recv()
    keep(10, a + taken(2))
    keep(11, b + taken(3))
    r[5], l[5] = send_halves(10)
    gram(zl, c, yl, x)
    gram(z2, oc, yl, x)
    gram(zl, oc, yl, x)
    for q in range(4):
        gram_other(q, (x,))
    row_id = lax.broadcasted_iota(jnp.int32, (chunk, chunk), 0)
    col_id = lax.broadcasted_iota(jnp.int32, (chunk, chunk), 1)
    wt[z, c, yl, x] = jnp.where(row_id == col_id, jnp.zeros((), BF16), wt[z, c, yl, x])

    for cp in square_copies:
        cp.wait_recv()
    variance = jnp.zeros((2, cols), F32)
    for d in range(8):
        variance = variance + squares[d]
    spread = jnp.sqrt(variance / (n_rows - 1) + DEVIATION_FLOOR)
    pull = jnp.where(spread < 1.0, -(VARIANCE_WEIGHT * n_rows / (2.0 * (n_rows - 1))) / spread, 0.0)
    mean_a[...], mean_b[...] = mean[0:1, :], mean[1:2, :]
    pull_a[...], pull_b[...] = pull[0:1, :], pull[1:2, :]

    for k in (2, 1):
        a, b = products([(x, k), (x, (k + 2) % 4)], blocks)
        own[k] = a
        own[(k + 2) % 4] = b
    back = []

    def give(k, which, straight, summed, far):
        zq = plus(z, k)
        p = (oyh, yh)[which]
        far[which].wait_recv()
        rows = pl.ds(pl.multiple_of(p * local_rows, local_rows), local_rows)
        total = own[k, rows, :] + (part_in[straight, p].astype(F32) + part_in[summed, p].astype(F32))
        rows_out[zq, p] = total.astype(BF16)
        if k or not which:
            back.append(copy(rows_out.at[zq, p], rows_in.at[yh, z], dev(yh_=p, z_=zq)))
        else:
            rows_in[yh, z] = rows_out[z, yh]

    l[2].wait_recv()
    r[2].wait_recv()
    for which in (0, 1):
        give(2, which, 5, 8, r[4])
        give(0, which, 4, 9, l[4])
    l[3].wait_recv()
    r[3].wait_recv()
    for which in (0, 1):
        give(1, which, 7, 10, r[5])
        give(3, which, 6, 11, l[5])
    for cp in back:
        cp.wait_recv()
    for v in range(2):
        for f in range(4):
            cov[v, :, f * chunk : (f + 1) * chunk] = rows_in[v, f]
    for cp in sent:
        cp.wait_send()


def on_device(z_a, z_b):
    rows, cols = z_a.shape
    chunk = cols // 4
    vmem = pl.BlockSpec(memory_space=pltpu.VMEM)
    hbm = pl.BlockSpec(memory_space=pl.ANY)
    cov, mean_a, mean_b, pull_a, pull_b = pl.pallas_call(
        kernel,
        out_shape=[jax.ShapeDtypeStruct((2, rows, cols), BF16), *[jax.ShapeDtypeStruct((1, cols), F32)] * 4],
        in_specs=[hbm, hbm],
        out_specs=[vmem] * 5,
        scratch_shapes=[
            pltpu.VMEM((rows, cols), F32),
            pltpu.VMEM((rows, cols), F32),
            pltpu.VMEM((8, 2, cols), F32),
            pltpu.VMEM((8, 2, cols), F32),
            pltpu.VMEM((4, 2, 2, 4, 2, rows, chunk), BF16),
            pltpu.VMEM((4, rows, chunk), BF16),
            pltpu.VMEM((4, 4, chunk, 2 * rows), BF16),
            pltpu.VMEM((4, 2, 2, 4, chunk, chunk), BF16),
            pltpu.VMEM((12, 2, rows, chunk), BF16),
            pltpu.VMEM((12, 2, rows, chunk), BF16),
            pltpu.VMEM((4, 2 * rows, chunk), F32),
            pltpu.VMEM((4, 2, rows, chunk), BF16),
            pltpu.VMEM((2, 4, rows, chunk), BF16),
            pltpu.SemaphoreType.DMA((2,)),
            pltpu.SemaphoreType.DMA((N_COPIES,)),
            pltpu.SemaphoreType.DMA((N_COPIES,)),
        ],
        compiler_params=pltpu.CompilerParams(collective_id=0, has_side_effects=True, vmem_limit_bytes=56 * 1024 * 1024),
        name="vicreg",
    )(z_a, z_b)
    difference = INVARIANCE_WEIGHT * (z_a - z_b)
    dz_a = difference + pull_a * (z_a - mean_a) + cov[0].astype(F32)
    dz_b = pull_b * (z_b - mean_b) - difference + cov[1].astype(F32)
    return dz_a, dz_b


def solution(mesh):
    specs = (P("dp", "mp"), P("dp", "mp"))
    return jax.shard_map(on_device, mesh=mesh, in_specs=specs, out_specs=specs, check_vma=False)
```

```python
import jax
import jax.numpy as jnp
from jax import lax
from jax.experimental import pallas as pl
from jax.experimental.pallas import tpu as pltpu
from jax.sharding import PartitionSpec as P

INVARIANCE_WEIGHT = 25.0
VARIANCE_WEIGHT = 25.0
DEVIATION_FLOOR = 0.0001
HUBER_EDGE = 0.05

MESH = pl.DeviceIdType.MESH
F32 = jnp.float32
BF16 = jnp.bfloat16
N_COPIES = 136


def kernel(za_hbm, zb_hbm, cov, mean_a, mean_b, pull_a, pull_b, za, zb, sums, squares, zi, stage, jt, wt, part_out, part_in, own, rows_out, rows_in, ls, ss, rs):
    dp = lax.axis_index("dp")
    mp = lax.axis_index("mp")
    yh, z = dp // 4, dp % 4
    x, yl, c = mp // 4, (mp // 2) % 2, mp % 2
    local_rows, cols = za.shape
    chunk = cols // 4
    n_rows = local_rows * 8
    pair = 2 * local_rows

    def dev(yh_=None, z_=None, x_=None, yl_=None, c_=None):
        yh_ = yh if yh_ is None else yh_
        z_ = z if z_ is None else z_
        x_ = x if x_ is None else x_
        yl_ = yl if yl_ is None else yl_
        c_ = c if c_ is None else c_
        return (yh_ * 4 + z_, x_ * 4 + yl_ * 2 + c_)

    def plus(v, k):
        return (v + (k % 4)) % 4

    sent = []

    def copy(src, dst, device):
        i = len(sent)
        cp = pltpu.make_async_remote_copy(
            src_ref=src, dst_ref=dst, send_sem=ss.at[i], recv_sem=rs.at[i], device_id=device, device_id_type=MESH
        )
        cp.start()
        sent.append(cp)
        return cp

    zl, zr, z2 = plus(z, -1), plus(z, 1), plus(z, 2)
    xl, xr, x2 = plus(x, -1), plus(x, 1), plus(x, 2)
    oyh, oyl, oc = 1 - yh, 1 - yl, 1 - c
    dp_peers = [(a, b) for a in range(2) for b in range(4) if a or b]

    def peer(a, b):
        return oyh if a else yh, plus(z, b)

    partners = [dev(yh_=peer(a, b)[0], z_=peer(a, b)[1]) for a, b in dp_peers]
    partners += [dev(yl_=oyl), dev(yh_=oyh, yl_=oyl), dev(x_=xl), dev(x_=xr), dev(c_=oc)]
    barrier = pltpu.get_barrier_semaphore()
    for partner in partners:
        pl.semaphore_signal(barrier, inc=1, device_id=partner, device_id_type=MESH)

    loads = [pltpu.make_async_copy(za_hbm, za, ls.at[0]), pltpu.make_async_copy(zb_hbm, zb, ls.at[1])]
    for load in loads:
        load.start()

    for v, ref in enumerate((za, zb)):
        loads[v].wait()
        sums[dp, v : v + 1, :] = jnp.sum(ref[...], axis=0, keepdims=True)
    pl.semaphore_wait(barrier, len(partners))
    def to_peers(ref):
        return [copy(ref, ref, dev(yh_=peer(a, b)[0], z_=peer(a, b)[1])) for a, b in dp_peers]

    for cp in to_peers(sums.at[dp]):
        cp.wait_recv()

    totals = jnp.zeros((2, cols), F32)
    for d in range(8):
        totals = totals + sums[d]
    mean = totals * (1.0 / n_rows)

    first = yh == 0
    for f in range(4):
        cut = slice(f * chunk, (f + 1) * chunk)
        ca = (za[:, cut] - mean[0:1, cut]).astype(BF16)
        cb = (zb[:, cut] - mean[1:2, cut]).astype(BF16)
        zi[f, c, yl, z, yh] = jnp.where(first, ca, cb)
        stage[f] = jnp.where(first, cb, ca)

    right_f = [plus(z, k) for k in (1, 2, 3, 0)]
    left_f = [plus(z, k) for k in (-1, 2, 0, 1)]
    from_left_f = [plus(z, k) for k in (0, 1, 2, 3)]
    from_right_f = [plus(z, k) for k in (0, 3, 1, 2)]

    def mine(f, to):
        return copy(zi.at[f, c, yl, z, yh], zi.at[f, c, yl, z, yh], dev(z_=to))

    def others(f, to):
        return copy(zi.at[f, c, yl, z, oyh], zi.at[f, c, yl, z, oyh], dev(z_=to))

    y1, y02 = {}, {}
    for k in (0, 1, 3, 2):
        f = plus(z, k)
        y1[k] = copy(stage.at[f], zi.at[f, c, yl, z, yh], dev(yh_=oyh))
    ra, rb, la, lb = {}, {}, {}, {}
    for s in range(4):
        ra[s] = mine(right_f[s], zr)
        la[s] = mine(left_f[s], zl)
    for k in (1, 3, 2, 0):
        f = plus(z, k)
        here = zi.at[f, c, yl, z, yh]
        y02[k] = [copy(here, here, dev(yl_=oyl)), copy(stage.at[f], here, dev(yh_=oyh, yl_=oyl))]

    for v, ref in enumerate((za, zb)):
        centered = ref[...] - mean[v : v + 1, :]
        squares[dp, v : v + 1, :] = jnp.sum(centered * centered, axis=0, keepdims=True)
    square_copies = to_peers(squares.at[dp])

    half = chunk // 2
    slab, slab_fwd = {}, []

    def slab_send(q):
        zq = plus(z, q)
        jt[zq, x] = zi[z, c, yl, zq].reshape(pair, chunk).T
        slab[q] = [copy(jt.at[zq, x], jt.at[zq, x], dev(x_=xr)), copy(jt.at[zq, x], jt.at[zq, x], dev(x_=xl))]

    def slab_forward(q):
        zq = plus(z, q)
        for cp in slab[q]:
            cp.wait_recv()
        lo, hi = pl.ds(0, half), pl.ds(half, half)
        slab_fwd.append(copy(jt.at[zq, xl, lo], jt.at[zq, xl, lo], dev(x_=xr)))
        slab_fwd.append(copy(jt.at[zq, xr, hi], jt.at[zq, xr, hi], dev(x_=xl)))

    def forward_right(f):
        ref = zi.at[f, c, yl, zl, yh]
        return copy(ref, ref, dev(z_=zr))

    def forward_left(f):
        ref = zi.at[f, c, yl, zr, oyh]
        return copy(ref, ref, dev(z_=zl))

    fr, fl = {}, {}
    shared = {}

    def share(key, ref):
        shared[key] = copy(ref, ref, dev(c_=oc))

    y1[0].wait_recv()
    slab_send(0)
    y1[1].wait_recv()
    rb[0] = others(right_f[0], zr)
    ra[1].wait_recv()
    fr[0] = forward_right(from_left_f[1])
    y1[3].wait_recv()
    lb[0] = others(left_f[0], zl)
    y1[2].wait_recv()
    rb[1] = others(right_f[1], zr)
    lb[1] = others(left_f[1], zl)
    lb[2] = others(left_f[2], zl)
    ra[2].wait_recv()
    fr[1] = forward_right(from_left_f[2])

    def to_other(ref):
        return copy(ref, ref, dev(yl_=oyl))

    ra[0].wait_recv()
    rb[0].wait_recv()
    slab_send(-1)
    near_left = to_other(zi.at[z, c, yl, zl])
    la[0].wait_recv()
    lb[0].wait_recv()
    slab_send(1)
    near_right = to_other(zi.at[z, c, yl, zr])
    across = {q: [] for q in range(4)}

    def opposite_mine(q):
        fr[q].wait_recv()
        across[q].append(to_other(zi.at[plus(z, q), c, yl, z2, yh]))

    def opposite_others(q):
        fl[q].wait_recv()
        across[q].append(to_other(zi.at[plus(z, q), c, yl, z2, oyh]))
        share(("same", q), zi.at[plus(z, q), c, yl])

    lb[1].wait_recv()
    fl[0] = forward_left(from_right_f[1])
    lb[3] = others(left_f[3], zl)
    ra[3].wait_recv()
    fr[2] = forward_right(from_left_f[3])
    fl[1] = forward_left(from_right_f[0])
    fr[3] = forward_right(from_left_f[0])
    rb[2] = others(right_f[2], zr)
    rb[3] = others(right_f[3], zr)
    opposite_mine(0)
    lb[2].wait_recv()
    fl[2] = forward_left(from_right_f[2])
    slab_forward(0)
    for s in range(1, 4):
        la[s].wait_recv()
    rb[1].wait_recv()
    opposite_mine(1)
    opposite_others(0)
    slab_send(2)
    lb[3].wait_recv()
    fl[3] = forward_left(from_right_f[3])
    opposite_mine(2)
    opposite_mine(3)

    rc, lc = {}, {}
    right_c = [plus(z, k) for k in (1, 2, 3, 0)]
    left_c = [plus(z, k) for k in (3, 0, 1, 2)]

    def direct(q):
        rc[q] = copy(zi.at[right_c[q], c, oyl, z], zi.at[right_c[q], c, oyl, z], dev(z_=zr))
        lc[q] = copy(zi.at[left_c[q], c, oyl, z], zi.at[left_c[q], c, oyl, z], dev(z_=zl))

    scale = 2.0 * n_rows / (n_rows - 1.0)
    slope = scale / (n_rows - 1.0)
    edge = HUBER_EDGE * scale

    def gram(f, cc, yy, part):
        g = jnp.zeros((chunk, chunk), F32)
        for q in range(4):
            g = g + jnp.dot(jt[q, part], zi[f, cc, yy, q].reshape(pair, chunk), preferred_element_type=F32)
        wt[f, cc, yy, part] = jnp.clip(g * slope, -edge, edge).astype(BF16)

    def gram_part(cc, part):
        for q in range(4):
            gram(plus(z, q), cc, yl, part)

    for k in (2, 0, 3, 1):
        for cp in y02[k]:
            cp.wait_recv()
        share(("own", k), zi.at[plus(z, k), c, oyl, z])
    direct(1)
    slab_forward(-1)
    slab_forward(1)
    rb[2].wait_recv()
    rb[3].wait_recv()
    opposite_others(1)
    direct(2)
    shared["same", 0].wait_recv()
    gram(z, c, yl, x)
    gram(z, oc, yl, x)
    gram(zr, c, yl, x)
    slab_forward(2)
    opposite_others(2)
    direct(3)
    opposite_others(3)

    def arrive(q):
        f = plus(z, q)
        (rc[q] if q else near_left).wait_recv()
        share(("left", q), zi.at[f, c, oyl, zl])
        (lc[q] if q else near_right).wait_recv()
        share(("right", q), zi.at[f, c, oyl, zr])
        for cp in across[q]:
            cp.wait_recv()
        share(("across", q), zi.at[f, c, oyl, z2])

    def sibling(q):
        for name in ("own", "left", "right", "across"):
            shared[name, q].wait_recv()

    gram(z2, c, yl, x)
    gram(zl, c, yl, x)
    gram_part(c, xl)
    gram_part(c, xr)
    arrive(0)
    for q in range(1, 4):
        shared["same", q].wait_recv()
    for q in range(1, 4):
        gram(plus(z, q), oc, yl, x)
    gram_part(oc, xl)
    gram_part(oc, xr)
    row_id = lax.broadcasted_iota(jnp.int32, (chunk, chunk), 0)
    col_id = lax.broadcasted_iota(jnp.int32, (chunk, chunk), 1)
    wt[z, c, yl, x] = jnp.where(row_id == col_id, jnp.zeros((), BF16), wt[z, c, yl, x])
    arrive(1)
    sibling(0)
    for cp in slab_fwd:
        cp.wait_recv()

    def gram_other(q, parts):
        for part in parts:
            for cc in (c, oc):
                gram(plus(z, q), cc, oyl, part)

    gram_part(c, x2)
    gram_part(oc, x2)
    gram_other(0, (x2,))
    arrive(2)
    sibling(1)
    sibling(2)
    gram_other(1, (x2,))
    gram_other(2, (x2,))

    blocks = [(plus(z, q), cc, yy) for q in range(4) for yy in (yl, oyl) for cc in (0, 1)]

    def products(tiles, over, start=None):
        accs = [jnp.zeros((pair, chunk), F32) for _ in tiles] if start is None else start
        for f, cc, yy in over:
            for i, (part, k) in enumerate(tiles):
                accs[i] = accs[i] + lax.dot_general(
                    zi[f, cc, yy, plus(z, k)].reshape(pair, chunk),
                    wt[f, cc, yy, part],
                    (((1,), (1,)), ((), ())),
                    preferred_element_type=F32,
                )
        return accs

    def keep(slot, value):
        part_out[slot] = value.astype(BF16).reshape(2, local_rows, chunk)

    def send_parts(slot):
        right = copy(part_out.at[slot], part_in.at[slot], dev(x_=xr))
        left = copy(part_out.at[slot + 1], part_in.at[slot + 1], dev(x_=xl))
        return right, left

    def send_halves(slot):
        return [
            [copy(part_out.at[i, p], part_in.at[i, p], dev(x_=to)) for p in (oyh, yh)]
            for i, to in ((slot, xr), (slot + 1, xl))
        ]

    def taken(slot):
        return part_in[slot].astype(F32).reshape(pair, chunk)

    turn = [(x2, 2), (x2, 0)]
    for i, acc in enumerate(products(turn, blocks[:14])):
        own[i] = acc
    arrive(3)
    sibling(3)
    gram_other(3, (x2,))
    for i, acc in enumerate(products(turn, blocks[14:], [own[i] for i in range(2)])):
        keep(i, acc)
    r, l = {}, {}
    r[0], l[0] = send_parts(0)
    a, b = products([(x2, 1), (x2, 3)], blocks)
    keep(2, a)
    keep(3, b)
    r[1], l[1] = send_parts(2)
    for q in range(4):
        gram_other(q, (xl, xr))
    a, b = products([(xr, 0), (xl, 2)], blocks)
    keep(4, a)
    keep(5, b)
    r[2], l[2] = send_parts(4)
    a, b = products([(xr, 3), (xl, 1)], blocks)
    keep(6, a)
    keep(7, b)
    r[3], l[3] = send_parts(6)
    a, b = products([(xr, 2), (xl, 0)], blocks)
    r[0].wait_recv()
    l[0].wait_recv()
    keep(8, a + taken(0))
    keep(9, b + taken(1))
    r[4], l[4] = send_halves(8)
    a, b = products([(xr, 1), (xl, 3)], blocks)
    r[1].wait_recv()
    l[1].wait_recv()
    keep(10, a + taken(2))
    keep(11, b + taken(3))
    r[5], l[5] = send_halves(10)
    for q in range(4):
        gram_other(q, (x,))

    for cp in square_copies:
        cp.wait_recv()
    variance = jnp.zeros((2, cols), F32)
    for d in range(8):
        variance = variance + squares[d]
    spread = jnp.sqrt(variance / (n_rows - 1) + DEVIATION_FLOOR)
    pull = jnp.where(spread < 1.0, -(VARIANCE_WEIGHT * n_rows / (2.0 * (n_rows - 1))) / spread, 0.0)
    mean_a[...], mean_b[...] = mean[0:1, :], mean[1:2, :]
    pull_a[...], pull_b[...] = pull[0:1, :], pull[1:2, :]

    for k in (2, 1):
        a, b = products([(x, k), (x, (k + 2) % 4)], blocks)
        own[k] = a
        own[(k + 2) % 4] = b
    back = []

    def give(k, which, straight, summed, far):
        zq = plus(z, k)
        p = (oyh, yh)[which]
        far[which].wait_recv()
        rows = pl.ds(pl.multiple_of(p * local_rows, local_rows), local_rows)
        total = own[k, rows, :] + (part_in[straight, p].astype(F32) + part_in[summed, p].astype(F32))
        rows_out[zq, p] = total.astype(BF16)
        if k or not which:
            back.append(copy(rows_out.at[zq, p], rows_in.at[yh, z], dev(yh_=p, z_=zq)))
        else:
            rows_in[yh, z] = rows_out[z, yh]

    l[2].wait_recv()
    r[2].wait_recv()
    for which in (0, 1):
        give(2, which, 5, 8, r[4])
        give(0, which, 4, 9, l[4])
    l[3].wait_recv()
    r[3].wait_recv()
    for which in (0, 1):
        give(1, which, 7, 10, r[5])
        give(3, which, 6, 11, l[5])
    for cp in back:
        cp.wait_recv()
    for v in range(2):
        for f in range(4):
            cov[v, :, f * chunk : (f + 1) * chunk] = rows_in[v, f]
    for cp in sent:
        cp.wait_send()


def on_device(z_a, z_b):
    rows, cols = z_a.shape
    chunk = cols // 4
    vmem = pl.BlockSpec(memory_space=pltpu.VMEM)
    hbm = pl.BlockSpec(memory_space=pl.ANY)
    cov, mean_a, mean_b, pull_a, pull_b = pl.pallas_call(
        kernel,
        out_shape=[jax.ShapeDtypeStruct((2, rows, cols), BF16), *[jax.ShapeDtypeStruct((1, cols), F32)] * 4],
        in_specs=[hbm, hbm],
        out_specs=[vmem] * 5,
        scratch_shapes=[
            pltpu.VMEM((rows, cols), F32),
            pltpu.VMEM((rows, cols), F32),
            pltpu.VMEM((8, 2, cols), F32),
            pltpu.VMEM((8, 2, cols), F32),
            pltpu.VMEM((4, 2, 2, 4, 2, rows, chunk), BF16),
            pltpu.VMEM((4, rows, chunk), BF16),
            pltpu.VMEM((4, 4, chunk, 2 * rows), BF16),
            pltpu.VMEM((4, 2, 2, 4, chunk, chunk), BF16),
            pltpu.VMEM((12, 2, rows, chunk), BF16),
            pltpu.VMEM((12, 2, rows, chunk), BF16),
            pltpu.VMEM((4, 2 * rows, chunk), F32),
            pltpu.VMEM((4, 2, rows, chunk), BF16),
            pltpu.VMEM((2, 4, rows, chunk), BF16),
            pltpu.SemaphoreType.DMA((2,)),
            pltpu.SemaphoreType.DMA((N_COPIES,)),
            pltpu.SemaphoreType.DMA((N_COPIES,)),
        ],
        compiler_params=pltpu.CompilerParams(collective_id=0, has_side_effects=True, vmem_limit_bytes=56 * 1024 * 1024),
        name="vicreg",
    )(z_a, z_b)
    difference = INVARIANCE_WEIGHT * (z_a - z_b)
    dz_a = difference + pull_a * (z_a - mean_a) + cov[0].astype(F32)
    dz_b = pull_b * (z_b - mean_b) - difference + cov[1].astype(F32)
    return dz_a, dz_b


def solution(mesh):
    specs = (P("dp", "mp"), P("dp", "mp"))
    return jax.shard_map(on_device, mesh=mesh, in_specs=specs, out_specs=specs, check_vma=False)
```

```python
import jax
import jax.numpy as jnp
from jax import lax
from jax.experimental import pallas as pl
from jax.experimental.pallas import tpu as pltpu
from jax.sharding import PartitionSpec as P

INVARIANCE_WEIGHT = 25.0
VARIANCE_WEIGHT = 25.0
DEVIATION_FLOOR = 0.0001
HUBER_EDGE = 0.05

MESH = pl.DeviceIdType.MESH
F32 = jnp.float32
BF16 = jnp.bfloat16
N_COPIES = 152


def kernel(za_hbm, zb_hbm, cov, mean_a, mean_b, pull_a, pull_b, za, zb, sums, squares, zi, stage, jt, wt, part_out, part_in, own, rows_out, rows_in, ls, ss, rs):
    dp = lax.axis_index("dp")
    mp = lax.axis_index("mp")
    yh, z = dp // 4, dp % 4
    x, yl, c = mp // 4, (mp // 2) % 2, mp % 2
    local_rows, cols = za.shape
    chunk = cols // 4
    n_rows = local_rows * 8
    pair = 2 * local_rows

    def dev(yh_=None, z_=None, x_=None, yl_=None, c_=None):
        yh_ = yh if yh_ is None else yh_
        z_ = z if z_ is None else z_
        x_ = x if x_ is None else x_
        yl_ = yl if yl_ is None else yl_
        c_ = c if c_ is None else c_
        return (yh_ * 4 + z_, x_ * 4 + yl_ * 2 + c_)

    def plus(v, k):
        return (v + (k % 4)) % 4

    sent = []

    def copy(src, dst, device):
        i = len(sent)
        cp = pltpu.make_async_remote_copy(
            src_ref=src, dst_ref=dst, send_sem=ss.at[i], recv_sem=rs.at[i], device_id=device, device_id_type=MESH
        )
        cp.start()
        sent.append(cp)
        return cp

    zl, zr, z2 = plus(z, -1), plus(z, 1), plus(z, 2)
    xl, xr, x2 = plus(x, -1), plus(x, 1), plus(x, 2)
    oyh, oyl, oc = 1 - yh, 1 - yl, 1 - c
    dp_peers = [(a, b) for a in range(2) for b in range(4) if a or b]

    def peer(a, b):
        return oyh if a else yh, plus(z, b)

    partners = [dev(yh_=peer(a, b)[0], z_=peer(a, b)[1]) for a, b in dp_peers]
    partners += [dev(yl_=oyl), dev(yh_=oyh, yl_=oyl), dev(x_=xl), dev(x_=xr), dev(c_=oc)]
    barrier = pltpu.get_barrier_semaphore()
    for partner in partners:
        pl.semaphore_signal(barrier, inc=1, device_id=partner, device_id_type=MESH)

    loads = [pltpu.make_async_copy(za_hbm, za, ls.at[0]), pltpu.make_async_copy(zb_hbm, zb, ls.at[1])]
    for load in loads:
        load.start()

    for v, ref in enumerate((za, zb)):
        loads[v].wait()
        sums[dp, v : v + 1, :] = jnp.sum(ref[...], axis=0, keepdims=True)
    pl.semaphore_wait(barrier, len(partners))
    def to_peers(ref):
        return [copy(ref, ref, dev(yh_=peer(a, b)[0], z_=peer(a, b)[1])) for a, b in dp_peers]

    for cp in to_peers(sums.at[dp]):
        cp.wait_recv()

    totals = jnp.zeros((2, cols), F32)
    for d in range(8):
        totals = totals + sums[d]
    mean = totals * (1.0 / n_rows)

    first = yh == 0
    for f in range(4):
        cut = slice(f * chunk, (f + 1) * chunk)
        ca = (za[:, cut] - mean[0:1, cut]).astype(BF16)
        cb = (zb[:, cut] - mean[1:2, cut]).astype(BF16)
        zi[f, c, yl, z, yh] = jnp.where(first, ca, cb)
        stage[f] = jnp.where(first, cb, ca)

    right_f = [plus(z, k) for k in (1, 2, 3, 0)]
    left_f = [plus(z, k) for k in (-1, 2, 0, 1)]
    from_left_f = [plus(z, k) for k in (0, 1, 2, 3)]
    from_right_f = [plus(z, k) for k in (0, 3, 1, 2)]

    def mine(f, to):
        return copy(zi.at[f, c, yl, z, yh], zi.at[f, c, yl, z, yh], dev(z_=to))

    def others(f, to):
        return copy(zi.at[f, c, yl, z, oyh], zi.at[f, c, yl, z, oyh], dev(z_=to))

    y1, y02 = {}, {}
    for k in (0, 1, 3, 2):
        f = plus(z, k)
        y1[k] = copy(stage.at[f], zi.at[f, c, yl, z, yh], dev(yh_=oyh))
    ra, rb, la, lb = {}, {}, {}, {}
    for s in range(4):
        ra[s] = mine(right_f[s], zr)
        la[s] = mine(left_f[s], zl)
    for k in (1, 3, 2, 0):
        f = plus(z, k)
        here = zi.at[f, c, yl, z, yh]
        y02[k] = [copy(here, here, dev(yl_=oyl)), copy(stage.at[f], here, dev(yh_=oyh, yl_=oyl))]

    for v, ref in enumerate((za, zb)):
        centered = ref[...] - mean[v : v + 1, :]
        squares[dp, v : v + 1, :] = jnp.sum(centered * centered, axis=0, keepdims=True)
    square_copies = to_peers(squares.at[dp])

    half = chunk // 2
    slab, slab_fwd = {}, []

    def slab_send(q):
        zq = plus(z, q)
        jt[zq, x] = zi[z, c, yl, zq].reshape(pair, chunk).T
        slab[q] = [copy(jt.at[zq, x], jt.at[zq, x], dev(x_=xr)), copy(jt.at[zq, x], jt.at[zq, x], dev(x_=xl))]

    def slab_forward(q):
        zq = plus(z, q)
        for cp in slab[q]:
            cp.wait_recv()
        lo, hi = pl.ds(0, half), pl.ds(half, half)
        slab_fwd.append(copy(jt.at[zq, xl, lo], jt.at[zq, xl, lo], dev(x_=xr)))
        slab_fwd.append(copy(jt.at[zq, xr, hi], jt.at[zq, xr, hi], dev(x_=xl)))

    def forward_right(f):
        ref = zi.at[f, c, yl, zl, yh]
        return copy(ref, ref, dev(z_=zr))

    def forward_left(f):
        ref = zi.at[f, c, yl, zr, oyh]
        return copy(ref, ref, dev(z_=zl))

    fr, fl = {}, {}
    shared = {}

    def share(key, ref):
        shared[key] = copy(ref, ref, dev(c_=oc))

    y1[0].wait_recv()
    slab_send(0)
    y1[1].wait_recv()
    rb[0] = others(right_f[0], zr)
    ra[1].wait_recv()
    fr[0] = forward_right(from_left_f[1])
    y1[3].wait_recv()
    lb[0] = others(left_f[0], zl)
    y1[2].wait_recv()
    rb[1] = others(right_f[1], zr)
    lb[1] = others(left_f[1], zl)
    lb[2] = others(left_f[2], zl)
    ra[2].wait_recv()
    fr[1] = forward_right(from_left_f[2])

    def to_other(ref):
        return copy(ref, ref, dev(yl_=oyl))

    def share_rows(q, zq):
        share(("same", q, len([key for key in shared if key[:2] == ("same", q)])), zi.at[plus(z, q), c, yl, zq])

    def same(q):
        for i in range(4):
            shared["same", q, i].wait_recv()

    for q in range(4):
        share_rows(q, z)

    ra[0].wait_recv()
    rb[0].wait_recv()
    slab_send(-1)
    near_left = to_other(zi.at[z, c, yl, zl])
    share_rows(0, zl)
    la[0].wait_recv()
    lb[0].wait_recv()
    slab_send(1)
    near_right = to_other(zi.at[z, c, yl, zr])
    share_rows(0, zr)
    across = {q: [] for q in range(4)}

    def opposite_mine(q):
        fr[q].wait_recv()
        across[q].append(to_other(zi.at[plus(z, q), c, yl, z2, yh]))

    def opposite_others(q):
        fl[q].wait_recv()
        across[q].append(to_other(zi.at[plus(z, q), c, yl, z2, oyh]))
        share_rows(q, z2)

    lb[1].wait_recv()
    fl[0] = forward_left(from_right_f[1])
    lb[3] = others(left_f[3], zl)
    ra[3].wait_recv()
    fr[2] = forward_right(from_left_f[3])
    fl[1] = forward_left(from_right_f[0])
    fr[3] = forward_right(from_left_f[0])
    rb[2] = others(right_f[2], zr)
    rb[3] = others(right_f[3], zr)
    opposite_mine(0)
    lb[2].wait_recv()
    fl[2] = forward_left(from_right_f[2])
    slab_forward(0)
    for s in range(1, 4):
        la[s].wait_recv()
    rb[1].wait_recv()
    opposite_mine(1)
    share_rows(1, zl)
    share_rows(3, zr)
    share_rows(1, zr)
    opposite_others(0)
    slab_send(2)
    lb[3].wait_recv()
    fl[3] = forward_left(from_right_f[3])
    share_rows(2, zr)
    opposite_mine(2)
    opposite_mine(3)

    rc, lc = {}, {}
    right_c = [plus(z, k) for k in (1, 2, 3, 0)]
    left_c = [plus(z, k) for k in (3, 0, 1, 2)]

    def direct(q):
        rc[q] = copy(zi.at[right_c[q], c, oyl, z], zi.at[right_c[q], c, oyl, z], dev(z_=zr))
        lc[q] = copy(zi.at[left_c[q], c, oyl, z], zi.at[left_c[q], c, oyl, z], dev(z_=zl))

    scale = 2.0 * n_rows / (n_rows - 1.0)
    slope = scale / (n_rows - 1.0)
    edge = HUBER_EDGE * scale

    def gram(f, cc, yy, part):
        g = jnp.zeros((chunk, chunk), F32)
        for q in range(4):
            g = g + jnp.dot(jt[q, part], zi[f, cc, yy, q].reshape(pair, chunk), preferred_element_type=F32)
        wt[f, cc, yy, part] = jnp.clip(g * slope, -edge, edge).astype(BF16)

    def gram_part(cc, part):
        for q in range(4):
            gram(plus(z, q), cc, yl, part)

    for k in (2, 0, 3, 1):
        for cp in y02[k]:
            cp.wait_recv()
        share(("own", k), zi.at[plus(z, k), c, oyl, z])
    direct(1)
    slab_forward(-1)
    slab_forward(1)
    rb[2].wait_recv()
    rb[3].wait_recv()
    share_rows(2, zl)
    share_rows(3, zl)
    opposite_others(1)
    direct(2)
    same(0)
    gram(z, c, yl, x)
    gram(z, oc, yl, x)
    gram(zr, c, yl, x)
    slab_forward(2)
    opposite_others(2)
    direct(3)
    opposite_others(3)

    def arrive(q):
        f = plus(z, q)
        (rc[q] if q else near_left).wait_recv()
        share(("left", q), zi.at[f, c, oyl, zl])
        (lc[q] if q else near_right).wait_recv()
        share(("right", q), zi.at[f, c, oyl, zr])
        for cp in across[q]:
            cp.wait_recv()
        share(("across", q), zi.at[f, c, oyl, z2])

    def sibling(q):
        for name in ("own", "left", "right", "across"):
            shared[name, q].wait_recv()

    gram_part(c, xl)
    gram_part(c, xr)
    arrive(0)
    for q in range(1, 4):
        same(q)
    gram_part(oc, xl)
    gram_part(oc, xr)
    arrive(1)
    sibling(0)
    for cp in slab_fwd:
        cp.wait_recv()

    def gram_other(q, parts):
        for part in parts:
            for cc in (c, oc):
                gram(plus(z, q), cc, oyl, part)

    gram_part(c, x2)
    gram_part(oc, x2)
    gram_other(0, (x2,))
    arrive(2)
    sibling(1)
    sibling(2)
    gram_other(1, (x2,))
    gram_other(2, (x2,))

    blocks = [(plus(z, q), cc, yy) for q in range(4) for yy in (yl, oyl) for cc in (0, 1)]

    def products(tiles, over, start=None):
        accs = [jnp.zeros((pair, chunk), F32) for _ in tiles] if start is None else start
        for f, cc, yy in over:
            for i, (part, k) in enumerate(tiles):
                accs[i] = accs[i] + lax.dot_general(
                    zi[f, cc, yy, plus(z, k)].reshape(pair, chunk),
                    wt[f, cc, yy, part],
                    (((1,), (1,)), ((), ())),
                    preferred_element_type=F32,
                )
        return accs

    def keep(slot, value):
        part_out[slot] = value.astype(BF16).reshape(2, local_rows, chunk)

    def send_parts(slot):
        right = copy(part_out.at[slot], part_in.at[slot], dev(x_=xr))
        left = copy(part_out.at[slot + 1], part_in.at[slot + 1], dev(x_=xl))
        return right, left

    def send_halves(slot):
        return [
            [copy(part_out.at[i, p], part_in.at[i, p], dev(x_=to)) for p in (oyh, yh)]
            for i, to in ((slot, xr), (slot + 1, xl))
        ]

    def taken(slot):
        return part_in[slot].astype(F32).reshape(pair, chunk)

    turn = [(x2, 2), (x2, 0)]
    for i, acc in enumerate(products(turn, blocks[:14])):
        own[i] = acc
    arrive(3)
    sibling(3)
    gram_other(3, (x2,))
    for i, acc in enumerate(products(turn, blocks[14:], [own[i] for i in range(2)])):
        keep(i, acc)
    r, l = {}, {}
    r[0], l[0] = send_parts(0)
    a, b = products([(x2, 1), (x2, 3)], blocks)
    keep(2, a)
    keep(3, b)
    r[1], l[1] = send_parts(2)
    for q in range(4):
        gram_other(q, (xl, xr))
    a, b = products([(xr, 0), (xl, 2)], blocks)
    keep(4, a)
    keep(5, b)
    r[2], l[2] = send_parts(4)
    a, b = products([(xr, 3), (xl, 1)], blocks)
    keep(6, a)
    keep(7, b)
    r[3], l[3] = send_parts(6)
    a, b = products([(xr, 2), (xl, 0)], blocks)
    r[0].wait_recv()
    l[0].wait_recv()
    keep(8, a + taken(0))
    keep(9, b + taken(1))
    r[4], l[4] = send_halves(8)
    a, b = products([(xr, 1), (xl, 3)], blocks)
    r[1].wait_recv()
    l[1].wait_recv()
    keep(10, a + taken(2))
    keep(11, b + taken(3))
    r[5], l[5] = send_halves(10)
    gram(z2, c, yl, x)
    gram(zl, c, yl, x)
    for q in range(1, 4):
        gram(plus(z, q), oc, yl, x)
    for q in range(4):
        gram_other(q, (x,))
    row_id = lax.broadcasted_iota(jnp.int32, (chunk, chunk), 0)
    col_id = lax.broadcasted_iota(jnp.int32, (chunk, chunk), 1)
    wt[z, c, yl, x] = jnp.where(row_id == col_id, jnp.zeros((), BF16), wt[z, c, yl, x])

    for cp in square_copies:
        cp.wait_recv()
    variance = jnp.zeros((2, cols), F32)
    for d in range(8):
        variance = variance + squares[d]
    spread = jnp.sqrt(variance / (n_rows - 1) + DEVIATION_FLOOR)
    pull = jnp.where(spread < 1.0, -(VARIANCE_WEIGHT * n_rows / (2.0 * (n_rows - 1))) / spread, 0.0)
    mean_a[...], mean_b[...] = mean[0:1, :], mean[1:2, :]
    pull_a[...], pull_b[...] = pull[0:1, :], pull[1:2, :]

    for k in (2, 1):
        a, b = products([(x, k), (x, (k + 2) % 4)], blocks)
        own[k] = a
        own[(k + 2) % 4] = b
    back = []

    def give(k, which, straight, summed, far):
        zq = plus(z, k)
        p = (oyh, yh)[which]
        far[which].wait_recv()
        rows = pl.ds(pl.multiple_of(p * local_rows, local_rows), local_rows)
        total = own[k, rows, :] + (part_in[straight, p].astype(F32) + part_in[summed, p].astype(F32))
        rows_out[zq, p] = total.astype(BF16)
        if k or not which:
            back.append(copy(rows_out.at[zq, p], rows_in.at[yh, z], dev(yh_=p, z_=zq)))
        else:
            rows_in[yh, z] = rows_out[z, yh]

    l[2].wait_recv()
    r[2].wait_recv()
    for which in (0, 1):
        give(2, which, 5, 8, r[4])
        give(0, which, 4, 9, l[4])
    l[3].wait_recv()
    r[3].wait_recv()
    for which in (0, 1):
        give(1, which, 7, 10, r[5])
        give(3, which, 6, 11, l[5])
    for cp in back:
        cp.wait_recv()
    for v in range(2):
        for f in range(4):
            cov[v, :, f * chunk : (f + 1) * chunk] = rows_in[v, f]
    for cp in sent:
        cp.wait_send()


def on_device(z_a, z_b):
    rows, cols = z_a.shape
    chunk = cols // 4
    vmem = pl.BlockSpec(memory_space=pltpu.VMEM)
    hbm = pl.BlockSpec(memory_space=pl.ANY)
    cov, mean_a, mean_b, pull_a, pull_b = pl.pallas_call(
        kernel,
        out_shape=[jax.ShapeDtypeStruct((2, rows, cols), BF16), *[jax.ShapeDtypeStruct((1, cols), F32)] * 4],
        in_specs=[hbm, hbm],
        out_specs=[vmem] * 5,
        scratch_shapes=[
            pltpu.VMEM((rows, cols), F32),
            pltpu.VMEM((rows, cols), F32),
            pltpu.VMEM((8, 2, cols), F32),
            pltpu.VMEM((8, 2, cols), F32),
            pltpu.VMEM((4, 2, 2, 4, 2, rows, chunk), BF16),
            pltpu.VMEM((4, rows, chunk), BF16),
            pltpu.VMEM((4, 4, chunk, 2 * rows), BF16),
            pltpu.VMEM((4, 2, 2, 4, chunk, chunk), BF16),
            pltpu.VMEM((12, 2, rows, chunk), BF16),
            pltpu.VMEM((12, 2, rows, chunk), BF16),
            pltpu.VMEM((4, 2 * rows, chunk), F32),
            pltpu.VMEM((4, 2, rows, chunk), BF16),
            pltpu.VMEM((2, 4, rows, chunk), BF16),
            pltpu.SemaphoreType.DMA((2,)),
            pltpu.SemaphoreType.DMA((N_COPIES,)),
            pltpu.SemaphoreType.DMA((N_COPIES,)),
        ],
        compiler_params=pltpu.CompilerParams(collective_id=0, has_side_effects=True, vmem_limit_bytes=56 * 1024 * 1024),
        name="vicreg",
    )(z_a, z_b)
    difference = INVARIANCE_WEIGHT * (z_a - z_b)
    dz_a = difference + pull_a * (z_a - mean_a) + cov[0].astype(F32)
    dz_b = pull_b * (z_b - mean_b) - difference + cov[1].astype(F32)
    return dz_a, dz_b


def solution(mesh):
    specs = (P("dp", "mp"), P("dp", "mp"))
    return jax.shard_map(on_device, mesh=mesh, in_specs=specs, out_specs=specs, check_vma=False)
```

```python
import jax
import jax.numpy as jnp
from jax import lax
from jax.experimental import pallas as pl
from jax.experimental.pallas import tpu as pltpu
from jax.sharding import PartitionSpec as P

INVARIANCE_WEIGHT = 25.0
VARIANCE_WEIGHT = 25.0
DEVIATION_FLOOR = 0.0001
HUBER_EDGE = 0.05

MESH = pl.DeviceIdType.MESH
F32 = jnp.float32
BF16 = jnp.bfloat16
N_COPIES = 152


def kernel(za_hbm, zb_hbm, cov, mean_a, mean_b, pull_a, pull_b, za, zb, sums, squares, zi, stage, jt, wt, part_out, part_in, own, rows_out, rows_in, ls, ss, rs):
    dp = lax.axis_index("dp")
    mp = lax.axis_index("mp")
    yh, z = dp // 4, dp % 4
    x, yl, c = mp // 4, (mp // 2) % 2, mp % 2
    local_rows, cols = za.shape
    chunk = cols // 4
    n_rows = local_rows * 8
    pair = 2 * local_rows

    def dev(yh_=None, z_=None, x_=None, yl_=None, c_=None):
        yh_ = yh if yh_ is None else yh_
        z_ = z if z_ is None else z_
        x_ = x if x_ is None else x_
        yl_ = yl if yl_ is None else yl_
        c_ = c if c_ is None else c_
        return (yh_ * 4 + z_, x_ * 4 + yl_ * 2 + c_)

    def plus(v, k):
        return (v + (k % 4)) % 4

    sent = []

    def copy(src, dst, device):
        i = len(sent)
        cp = pltpu.make_async_remote_copy(
            src_ref=src, dst_ref=dst, send_sem=ss.at[i], recv_sem=rs.at[i], device_id=device, device_id_type=MESH
        )
        cp.start()
        sent.append(cp)
        return cp

    zl, zr, z2 = plus(z, -1), plus(z, 1), plus(z, 2)
    xl, xr, x2 = plus(x, -1), plus(x, 1), plus(x, 2)
    oyh, oyl, oc = 1 - yh, 1 - yl, 1 - c
    dp_peers = [(a, b) for a in range(2) for b in range(4) if a or b]

    def peer(a, b):
        return oyh if a else yh, plus(z, b)

    partners = [dev(yh_=peer(a, b)[0], z_=peer(a, b)[1]) for a, b in dp_peers]
    partners += [dev(yl_=oyl), dev(yh_=oyh, yl_=oyl), dev(x_=xl), dev(x_=xr), dev(c_=oc)]
    barrier = pltpu.get_barrier_semaphore()
    for partner in partners:
        pl.semaphore_signal(barrier, inc=1, device_id=partner, device_id_type=MESH)

    loads = [pltpu.make_async_copy(za_hbm, za, ls.at[0]), pltpu.make_async_copy(zb_hbm, zb, ls.at[1])]
    for load in loads:
        load.start()

    for v, ref in enumerate((za, zb)):
        loads[v].wait()
        sums[dp, v : v + 1, :] = jnp.sum(ref[...], axis=0, keepdims=True)
    pl.semaphore_wait(barrier, len(partners))
    def to_peers(ref):
        return [copy(ref, ref, dev(yh_=peer(a, b)[0], z_=peer(a, b)[1])) for a, b in dp_peers]

    for cp in to_peers(sums.at[dp]):
        cp.wait_recv()

    totals = jnp.zeros((2, cols), F32)
    for d in range(8):
        totals = totals + sums[d]
    mean = totals * (1.0 / n_rows)

    first = yh == 0
    for f in range(4):
        cut = slice(f * chunk, (f + 1) * chunk)
        ca = (za[:, cut] - mean[0:1, cut]).astype(BF16)
        cb = (zb[:, cut] - mean[1:2, cut]).astype(BF16)
        zi[f, c, yl, z, yh] = jnp.where(first, ca, cb)
        stage[f] = jnp.where(first, cb, ca)

    right_f = [plus(z, k) for k in (1, 2, 3, 0)]
    left_f = [plus(z, k) for k in (-1, 2, 0, 1)]
    from_left_f = [plus(z, k) for k in (0, 1, 2, 3)]
    from_right_f = [plus(z, k) for k in (0, 3, 1, 2)]

    def mine(f, to):
        return copy(zi.at[f, c, yl, z, yh], zi.at[f, c, yl, z, yh], dev(z_=to))

    def others(f, to):
        return copy(zi.at[f, c, yl, z, oyh], zi.at[f, c, yl, z, oyh], dev(z_=to))

    y1, y02 = {}, {}
    for k in (0, 1, 3, 2):
        f = plus(z, k)
        y1[k] = copy(stage.at[f], zi.at[f, c, yl, z, yh], dev(yh_=oyh))
    ra, rb, la, lb = {}, {}, {}, {}
    for s in range(4):
        ra[s] = mine(right_f[s], zr)
        la[s] = mine(left_f[s], zl)
    for k in (1, 3, 2, 0):
        f = plus(z, k)
        here = zi.at[f, c, yl, z, yh]
        y02[k] = [copy(here, here, dev(yl_=oyl)), copy(stage.at[f], here, dev(yh_=oyh, yl_=oyl))]

    for v, ref in enumerate((za, zb)):
        centered = ref[...] - mean[v : v + 1, :]
        squares[dp, v : v + 1, :] = jnp.sum(centered * centered, axis=0, keepdims=True)
    square_copies = to_peers(squares.at[dp])

    half = chunk // 2
    slab, slab_fwd = {}, []

    def slab_send(q):
        zq = plus(z, q)
        jt[zq, x] = zi[z, c, yl, zq].reshape(pair, chunk).T
        slab[q] = [copy(jt.at[zq, x], jt.at[zq, x], dev(x_=xr)), copy(jt.at[zq, x], jt.at[zq, x], dev(x_=xl))]

    def slab_forward(q):
        zq = plus(z, q)
        for cp in slab[q]:
            cp.wait_recv()
        lo, hi = pl.ds(0, half), pl.ds(half, half)
        slab_fwd.append(copy(jt.at[zq, xl, lo], jt.at[zq, xl, lo], dev(x_=xr)))
        slab_fwd.append(copy(jt.at[zq, xr, hi], jt.at[zq, xr, hi], dev(x_=xl)))

    def forward_right(f):
        ref = zi.at[f, c, yl, zl, yh]
        return copy(ref, ref, dev(z_=zr))

    def forward_left(f):
        ref = zi.at[f, c, yl, zr, oyh]
        return copy(ref, ref, dev(z_=zl))

    fr, fl = {}, {}
    shared = {}

    def share(key, ref):
        shared[key] = copy(ref, ref, dev(c_=oc))

    y1[0].wait_recv()
    slab_send(0)
    y1[1].wait_recv()
    rb[0] = others(right_f[0], zr)
    ra[1].wait_recv()
    fr[0] = forward_right(from_left_f[1])
    y1[3].wait_recv()
    lb[0] = others(left_f[0], zl)
    y1[2].wait_recv()
    rb[1] = others(right_f[1], zr)
    lb[1] = others(left_f[1], zl)
    lb[2] = others(left_f[2], zl)
    ra[2].wait_recv()
    fr[1] = forward_right(from_left_f[2])

    def to_other(ref):
        return copy(ref, ref, dev(yl_=oyl))

    def share_rows(q, zq):
        share(("same", q, len([key for key in shared if key[:2] == ("same", q)])), zi.at[plus(z, q), c, yl, zq])

    def same(q):
        for i in range(4):
            shared["same", q, i].wait_recv()

    for q in range(4):
        share_rows(q, z)

    ra[0].wait_recv()
    rb[0].wait_recv()
    slab_send(-1)
    near_left = to_other(zi.at[z, c, yl, zl])
    share_rows(0, zl)
    la[0].wait_recv()
    lb[0].wait_recv()
    slab_send(1)
    near_right = to_other(zi.at[z, c, yl, zr])
    share_rows(0, zr)
    across = {q: [] for q in range(4)}

    def opposite_mine(q):
        fr[q].wait_recv()
        across[q].append(to_other(zi.at[plus(z, q), c, yl, z2, yh]))

    def opposite_others(q):
        fl[q].wait_recv()
        across[q].append(to_other(zi.at[plus(z, q), c, yl, z2, oyh]))
        share_rows(q, z2)

    lb[1].wait_recv()
    fl[0] = forward_left(from_right_f[1])
    lb[3] = others(left_f[3], zl)
    ra[3].wait_recv()
    fr[2] = forward_right(from_left_f[3])
    fl[1] = forward_left(from_right_f[0])
    fr[3] = forward_right(from_left_f[0])
    rb[2] = others(right_f[2], zr)
    rb[3] = others(right_f[3], zr)
    opposite_mine(0)
    lb[2].wait_recv()
    fl[2] = forward_left(from_right_f[2])
    slab_forward(0)
    for s in range(1, 4):
        la[s].wait_recv()
    rb[1].wait_recv()
    opposite_mine(1)
    share_rows(1, zl)
    share_rows(3, zr)
    share_rows(1, zr)
    opposite_others(0)
    slab_send(2)
    lb[3].wait_recv()
    fl[3] = forward_left(from_right_f[3])
    share_rows(2, zr)
    opposite_mine(2)
    opposite_mine(3)

    rc, lc = {}, {}
    right_c = [plus(z, k) for k in (1, 2, 3, 0)]
    left_c = [plus(z, k) for k in (3, 0, 1, 2)]

    def direct(q):
        rc[q] = copy(zi.at[right_c[q], c, oyl, z], zi.at[right_c[q], c, oyl, z], dev(z_=zr))
        lc[q] = copy(zi.at[left_c[q], c, oyl, z], zi.at[left_c[q], c, oyl, z], dev(z_=zl))

    scale = 2.0 * n_rows / (n_rows - 1.0)
    slope = scale / (n_rows - 1.0)
    edge = HUBER_EDGE * scale

    def gram(f, cc, yy, part):
        g = jnp.zeros((chunk, chunk), F32)
        for q in range(4):
            g = g + jnp.dot(jt[q, part], zi[f, cc, yy, q].reshape(pair, chunk), preferred_element_type=F32)
        wt[f, cc, yy, part] = jnp.clip(g * slope, -edge, edge).astype(BF16)

    def gram_part(cc, part):
        for q in range(4):
            gram(plus(z, q), cc, yl, part)

    for k in (2, 0, 3, 1):
        for cp in y02[k]:
            cp.wait_recv()
        share(("own", k), zi.at[plus(z, k), c, oyl, z])
    direct(1)
    slab_forward(-1)
    slab_forward(1)
    rb[2].wait_recv()
    rb[3].wait_recv()
    share_rows(2, zl)
    share_rows(3, zl)
    opposite_others(1)
    direct(2)
    same(0)
    gram(z, c, yl, x)
    gram(z, oc, yl, x)
    gram(zr, c, yl, x)
    slab_forward(2)
    opposite_others(2)
    direct(3)
    opposite_others(3)

    def arrive(q):
        f = plus(z, q)
        (rc[q] if q else near_left).wait_recv()
        share(("left", q), zi.at[f, c, oyl, zl])
        (lc[q] if q else near_right).wait_recv()
        share(("right", q), zi.at[f, c, oyl, zr])
        for cp in across[q]:
            cp.wait_recv()
        share(("across", q), zi.at[f, c, oyl, z2])

    def sibling(q):
        for name in ("own", "left", "right", "across"):
            shared[name, q].wait_recv()

    gram(z2, c, yl, x)
    gram(zl, c, yl, x)
    gram_part(c, xl)
    gram_part(c, xr)
    arrive(0)
    for q in range(1, 4):
        same(q)
    for q in range(1, 4):
        gram(plus(z, q), oc, yl, x)
    gram_part(oc, xl)
    gram_part(oc, xr)
    row_id = lax.broadcasted_iota(jnp.int32, (chunk, chunk), 0)
    col_id = lax.broadcasted_iota(jnp.int32, (chunk, chunk), 1)
    wt[z, c, yl, x] = jnp.where(row_id == col_id, jnp.zeros((), BF16), wt[z, c, yl, x])
    arrive(1)
    sibling(0)
    for cp in slab_fwd:
        cp.wait_recv()

    def gram_other(q, parts):
        for part in parts:
            for cc in (c, oc):
                gram(plus(z, q), cc, oyl, part)

    gram_part(c, x2)
    gram_part(oc, x2)
    gram_other(0, (x2,))
    arrive(2)
    sibling(1)
    sibling(2)
    gram_other(1, (x2,))
    gram_other(2, (x2,))

    blocks = [(plus(z, q), cc, yy) for q in range(4) for yy in (yl, oyl) for cc in (0, 1)]

    def products(tiles, over, start=None):
        accs = [jnp.zeros((pair, chunk), F32) for _ in tiles] if start is None else start
        for f, cc, yy in over:
            for i, (part, k) in enumerate(tiles):
                accs[i] = accs[i] + lax.dot_general(
                    zi[f, cc, yy, plus(z, k)].reshape(pair, chunk),
                    wt[f, cc, yy, part],
                    (((1,), (1,)), ((), ())),
                    preferred_element_type=F32,
                )
        return accs

    def keep(slot, value):
        part_out[slot] = value.astype(BF16).reshape(2, local_rows, chunk)

    def send_parts(slot):
        right = copy(part_out.at[slot], part_in.at[slot], dev(x_=xr))
        left = copy(part_out.at[slot + 1], part_in.at[slot + 1], dev(x_=xl))
        return right, left

    def send_halves(slot):
        return [
            [copy(part_out.at[i, p], part_in.at[i, p], dev(x_=to)) for p in (oyh, yh)]
            for i, to in ((slot, xr), (slot + 1, xl))
        ]

    def taken(slot):
        return part_in[slot].astype(F32).reshape(pair, chunk)

    turn = [(x2, 2), (x2, 0)]
    for i, acc in enumerate(products(turn, blocks[:14])):
        own[i] = acc
    arrive(3)
    sibling(3)
    gram_other(3, (x2,))
    for i, acc in enumerate(products(turn, blocks[14:], [own[i] for i in range(2)])):
        keep(i, acc)
    r, l = {}, {}
    r[0], l[0] = send_parts(0)
    a, b = products([(x2, 1), (x2, 3)], blocks)
    keep(2, a)
    keep(3, b)
    r[1], l[1] = send_parts(2)
    for q in range(4):
        gram_other(q, (xl, xr))
    a, b = products([(xr, 0), (xl, 2)], blocks)
    keep(4, a)
    keep(5, b)
    r[2], l[2] = send_parts(4)
    a, b = products([(xr, 3), (xl, 1)], blocks)
    keep(6, a)
    keep(7, b)
    r[3], l[3] = send_parts(6)
    a, b = products([(xr, 2), (xl, 0)], blocks)
    r[0].wait_recv()
    l[0].wait_recv()
    keep(8, a + taken(0))
    keep(9, b + taken(1))
    r[4], l[4] = send_halves(8)
    a, b = products([(xr, 1), (xl, 3)], blocks)
    r[1].wait_recv()
    l[1].wait_recv()
    keep(10, a + taken(2))
    keep(11, b + taken(3))
    r[5], l[5] = send_halves(10)
    for q in range(4):
        gram_other(q, (x,))

    for cp in square_copies:
        cp.wait_recv()
    variance = jnp.zeros((2, cols), F32)
    for d in range(8):
        variance = variance + squares[d]
    spread = jnp.sqrt(variance / (n_rows - 1) + DEVIATION_FLOOR)
    pull = jnp.where(spread < 1.0, -(VARIANCE_WEIGHT * n_rows / (2.0 * (n_rows - 1))) / spread, 0.0)
    mean_a[...], mean_b[...] = mean[0:1, :], mean[1:2, :]
    pull_a[...], pull_b[...] = pull[0:1, :], pull[1:2, :]

    for k in (2, 1):
        a, b = products([(x, k), (x, (k + 2) % 4)], blocks)
        own[k] = a
        own[(k + 2) % 4] = b
    back = []

    def give(k, which, straight, summed, far):
        zq = plus(z, k)
        p = (oyh, yh)[which]
        far[which].wait_recv()
        rows = pl.ds(pl.multiple_of(p * local_rows, local_rows), local_rows)
        total = own[k, rows, :] + (part_in[straight, p].astype(F32) + part_in[summed, p].astype(F32))
        rows_out[zq, p] = total.astype(BF16)
        if k or not which:
            back.append(copy(rows_out.at[zq, p], rows_in.at[yh, z], dev(yh_=p, z_=zq)))
        else:
            rows_in[yh, z] = rows_out[z, yh]

    l[2].wait_recv()
    r[2].wait_recv()
    for which in (0, 1):
        give(2, which, 5, 8, r[4])
        give(0, which, 4, 9, l[4])
    l[3].wait_recv()
    r[3].wait_recv()
    for which in (0, 1):
        give(1, which, 7, 10, r[5])
        give(3, which, 6, 11, l[5])
    for cp in back:
        cp.wait_recv()
    for v in range(2):
        for f in range(4):
            cov[v, :, f * chunk : (f + 1) * chunk] = rows_in[v, f]
    for cp in sent:
        cp.wait_send()


def on_device(z_a, z_b):
    rows, cols = z_a.shape
    chunk = cols // 4
    vmem = pl.BlockSpec(memory_space=pltpu.VMEM)
    hbm = pl.BlockSpec(memory_space=pl.ANY)
    cov, mean_a, mean_b, pull_a, pull_b = pl.pallas_call(
        kernel,
        out_shape=[jax.ShapeDtypeStruct((2, rows, cols), BF16), *[jax.ShapeDtypeStruct((1, cols), F32)] * 4],
        in_specs=[hbm, hbm],
        out_specs=[vmem] * 5,
        scratch_shapes=[
            pltpu.VMEM((rows, cols), F32),
            pltpu.VMEM((rows, cols), F32),
            pltpu.VMEM((8, 2, cols), F32),
            pltpu.VMEM((8, 2, cols), F32),
            pltpu.VMEM((4, 2, 2, 4, 2, rows, chunk), BF16),
            pltpu.VMEM((4, rows, chunk), BF16),
            pltpu.VMEM((4, 4, chunk, 2 * rows), BF16),
            pltpu.VMEM((4, 2, 2, 4, chunk, chunk), BF16),
            pltpu.VMEM((12, 2, rows, chunk), BF16),
            pltpu.VMEM((12, 2, rows, chunk), BF16),
            pltpu.VMEM((4, 2 * rows, chunk), F32),
            pltpu.VMEM((4, 2, rows, chunk), BF16),
            pltpu.VMEM((2, 4, rows, chunk), BF16),
            pltpu.SemaphoreType.DMA((2,)),
            pltpu.SemaphoreType.DMA((N_COPIES,)),
            pltpu.SemaphoreType.DMA((N_COPIES,)),
        ],
        compiler_params=pltpu.CompilerParams(collective_id=0, has_side_effects=True, vmem_limit_bytes=56 * 1024 * 1024),
        name="vicreg",
    )(z_a, z_b)
    difference = INVARIANCE_WEIGHT * (z_a - z_b)
    dz_a = difference + pull_a * (z_a - mean_a) + cov[0].astype(F32)
    dz_b = pull_b * (z_b - mean_b) - difference + cov[1].astype(F32)
    return dz_a, dz_b


def solution(mesh):
    specs = (P("dp", "mp"), P("dp", "mp"))
    return jax.shard_map(on_device, mesh=mesh, in_specs=specs, out_specs=specs, check_vma=False)
```

```python
import jax
import jax.numpy as jnp
from jax import lax
from jax.experimental import pallas as pl
from jax.experimental.pallas import tpu as pltpu
from jax.sharding import PartitionSpec as P

INVARIANCE_WEIGHT = 25.0
VARIANCE_WEIGHT = 25.0
DEVIATION_FLOOR = 0.0001
HUBER_EDGE = 0.05

MESH = pl.DeviceIdType.MESH
F32 = jnp.float32
BF16 = jnp.bfloat16
N_COPIES = 136


def kernel(za_hbm, zb_hbm, cov, mean_a, mean_b, pull_a, pull_b, za, zb, coefs, sums, squares, zi, stage, jt, wt, part_out, part_in, own, rows_out, rows_in, ls, ss, rs):
    dp = lax.axis_index("dp")
    mp = lax.axis_index("mp")
    yh, z = dp // 4, dp % 4
    x, yl, c = mp // 4, (mp // 2) % 2, mp % 2
    local_rows, cols = za.shape
    chunk = cols // 4
    n_rows = local_rows * 8
    pair = 2 * local_rows

    def dev(yh_=None, z_=None, x_=None, yl_=None, c_=None):
        yh_ = yh if yh_ is None else yh_
        z_ = z if z_ is None else z_
        x_ = x if x_ is None else x_
        yl_ = yl if yl_ is None else yl_
        c_ = c if c_ is None else c_
        return (yh_ * 4 + z_, x_ * 4 + yl_ * 2 + c_)

    def plus(v, k):
        return (v + (k % 4)) % 4

    sent = []

    def copy(src, dst, device):
        i = len(sent)
        cp = pltpu.make_async_remote_copy(
            src_ref=src, dst_ref=dst, send_sem=ss.at[i], recv_sem=rs.at[i], device_id=device, device_id_type=MESH
        )
        cp.start()
        sent.append(cp)
        return cp

    zl, zr, z2 = plus(z, -1), plus(z, 1), plus(z, 2)
    xl, xr, x2 = plus(x, -1), plus(x, 1), plus(x, 2)
    oyh, oyl, oc = 1 - yh, 1 - yl, 1 - c
    dp_peers = [(a, b) for a in range(2) for b in range(4) if a or b]

    def peer(a, b):
        return oyh if a else yh, plus(z, b)

    partners = [dev(yh_=peer(a, b)[0], z_=peer(a, b)[1]) for a, b in dp_peers]
    partners += [dev(yl_=oyl), dev(yh_=oyh, yl_=oyl), dev(x_=xl), dev(x_=xr), dev(c_=oc)]
    barrier = pltpu.get_barrier_semaphore()
    for partner in partners:
        pl.semaphore_signal(barrier, inc=1, device_id=partner, device_id_type=MESH)

    loads = [pltpu.make_async_copy(za_hbm, za, ls.at[0]), pltpu.make_async_copy(zb_hbm, zb, ls.at[1])]
    for load in loads:
        load.start()

    for v, ref in enumerate((za, zb)):
        loads[v].wait()
        sums[dp, v : v + 1, :] = jnp.sum(ref[...], axis=0, keepdims=True)
    pl.semaphore_wait(barrier, len(partners))
    def to_peers(ref):
        return [copy(ref, ref, dev(yh_=peer(a, b)[0], z_=peer(a, b)[1])) for a, b in dp_peers]

    for cp in to_peers(sums.at[dp]):
        cp.wait_recv()

    totals = jnp.zeros((2, cols), F32)
    for d in range(8):
        totals = totals + sums[d]
    mean = totals * (1.0 / n_rows)

    first = yh == 0
    for f in range(4):
        cut = slice(f * chunk, (f + 1) * chunk)
        ca = (za[:, cut] - mean[0:1, cut]).astype(BF16)
        cb = (zb[:, cut] - mean[1:2, cut]).astype(BF16)
        zi[f, c, yl, z, yh] = jnp.where(first, ca, cb)
        stage[f] = jnp.where(first, cb, ca)

    right_f = [plus(z, k) for k in (1, 2, 3, 0)]
    left_f = [plus(z, k) for k in (-1, 2, 0, 1)]
    from_left_f = [plus(z, k) for k in (0, 1, 2, 3)]
    from_right_f = [plus(z, k) for k in (0, 3, 1, 2)]

    def mine(f, to):
        return copy(zi.at[f, c, yl, z, yh], zi.at[f, c, yl, z, yh], dev(z_=to))

    def others(f, to):
        return copy(zi.at[f, c, yl, z, oyh], zi.at[f, c, yl, z, oyh], dev(z_=to))

    y1, y02 = {}, {}
    for k in (0, 1, 3, 2):
        f = plus(z, k)
        y1[k] = copy(stage.at[f], zi.at[f, c, yl, z, yh], dev(yh_=oyh))
    ra, rb, la, lb = {}, {}, {}, {}
    for s in range(4):
        ra[s] = mine(right_f[s], zr)
        la[s] = mine(left_f[s], zl)
    for k in (1, 3, 2, 0):
        f = plus(z, k)
        here = zi.at[f, c, yl, z, yh]
        y02[k] = [copy(here, here, dev(yl_=oyl)), copy(stage.at[f], here, dev(yh_=oyh, yl_=oyl))]

    for v, ref in enumerate((za, zb)):
        centered = ref[...] - mean[v : v + 1, :]
        squares[dp, v : v + 1, :] = jnp.sum(centered * centered, axis=0, keepdims=True)
    square_copies = to_peers(squares.at[dp])

    half = chunk // 2
    slab, slab_fwd = {}, []

    def slab_send(q):
        zq = plus(z, q)
        jt[zq, x] = zi[z, c, yl, zq].reshape(pair, chunk).T
        slab[q] = [copy(jt.at[zq, x], jt.at[zq, x], dev(x_=xr)), copy(jt.at[zq, x], jt.at[zq, x], dev(x_=xl))]

    def slab_forward(q):
        zq = plus(z, q)
        for cp in slab[q]:
            cp.wait_recv()
        lo, hi = pl.ds(0, half), pl.ds(half, half)
        slab_fwd.append(copy(jt.at[zq, xl, lo], jt.at[zq, xl, lo], dev(x_=xr)))
        slab_fwd.append(copy(jt.at[zq, xr, hi], jt.at[zq, xr, hi], dev(x_=xl)))

    def forward_right(f):
        ref = zi.at[f, c, yl, zl, yh]
        return copy(ref, ref, dev(z_=zr))

    def forward_left(f):
        ref = zi.at[f, c, yl, zr, oyh]
        return copy(ref, ref, dev(z_=zl))

    fr, fl = {}, {}
    shared = {}

    def share(key, ref):
        shared[key] = copy(ref, ref, dev(c_=oc))

    y1[0].wait_recv()
    slab_send(0)
    y1[1].wait_recv()
    rb[0] = others(right_f[0], zr)
    ra[1].wait_recv()
    fr[0] = forward_right(from_left_f[1])
    y1[3].wait_recv()
    lb[0] = others(left_f[0], zl)
    y1[2].wait_recv()
    rb[1] = others(right_f[1], zr)
    lb[1] = others(left_f[1], zl)
    lb[2] = others(left_f[2], zl)
    ra[2].wait_recv()
    fr[1] = forward_right(from_left_f[2])

    def to_other(ref):
        return copy(ref, ref, dev(yl_=oyl))

    ra[0].wait_recv()
    rb[0].wait_recv()
    slab_send(-1)
    near_left = to_other(zi.at[z, c, yl, zl])
    la[0].wait_recv()
    lb[0].wait_recv()
    slab_send(1)
    near_right = to_other(zi.at[z, c, yl, zr])
    across = {q: [] for q in range(4)}

    def opposite_mine(q):
        fr[q].wait_recv()
        across[q].append(to_other(zi.at[plus(z, q), c, yl, z2, yh]))

    def opposite_others(q):
        fl[q].wait_recv()
        across[q].append(to_other(zi.at[plus(z, q), c, yl, z2, oyh]))
        share(("same", q), zi.at[plus(z, q), c, yl])

    lb[1].wait_recv()
    fl[0] = forward_left(from_right_f[1])
    lb[3] = others(left_f[3], zl)
    ra[3].wait_recv()
    fr[2] = forward_right(from_left_f[3])
    fl[1] = forward_left(from_right_f[0])
    fr[3] = forward_right(from_left_f[0])
    rb[2] = others(right_f[2], zr)
    rb[3] = others(right_f[3], zr)
    opposite_mine(0)
    lb[2].wait_recv()
    fl[2] = forward_left(from_right_f[2])
    slab_forward(0)
    for s in range(1, 4):
        la[s].wait_recv()
    rb[1].wait_recv()
    opposite_mine(1)
    opposite_others(0)
    slab_send(2)
    lb[3].wait_recv()
    fl[3] = forward_left(from_right_f[3])
    opposite_mine(2)
    opposite_mine(3)

    rc, lc = {}, {}
    right_c = [plus(z, k) for k in (1, 2, 3, 0)]
    left_c = [plus(z, k) for k in (3, 0, 1, 2)]

    def direct(q):
        rc[q] = copy(zi.at[right_c[q], c, oyl, z], zi.at[right_c[q], c, oyl, z], dev(z_=zr))
        lc[q] = copy(zi.at[left_c[q], c, oyl, z], zi.at[left_c[q], c, oyl, z], dev(z_=zl))

    scale = 2.0 * n_rows / (n_rows - 1.0)
    slope = scale / (n_rows - 1.0)
    edge = HUBER_EDGE * scale

    def gram(f, cc, yy, part):
        g = jnp.zeros((chunk, chunk), F32)
        for q in range(4):
            g = g + jnp.dot(jt[q, part], zi[f, cc, yy, q].reshape(pair, chunk), preferred_element_type=F32)
        wt[f, cc, yy, part] = jnp.clip(g * slope, -edge, edge).astype(BF16)

    def gram_part(cc, part):
        for q in range(4):
            gram(plus(z, q), cc, yl, part)

    for k in (2, 0, 3, 1):
        for cp in y02[k]:
            cp.wait_recv()
        share(("own", k), zi.at[plus(z, k), c, oyl, z])
    direct(1)
    slab_forward(-1)
    slab_forward(1)
    rb[2].wait_recv()
    rb[3].wait_recv()
    opposite_others(1)
    direct(2)
    shared["same", 0].wait_recv()
    gram(z, c, yl, x)
    gram(z, oc, yl, x)
    gram(zr, c, yl, x)
    slab_forward(2)
    opposite_others(2)
    direct(3)
    opposite_others(3)

    def arrive(q):
        f = plus(z, q)
        (rc[q] if q else near_left).wait_recv()
        share(("left", q), zi.at[f, c, oyl, zl])
        (lc[q] if q else near_right).wait_recv()
        share(("right", q), zi.at[f, c, oyl, zr])
        for cp in across[q]:
            cp.wait_recv()
        share(("across", q), zi.at[f, c, oyl, z2])

    def sibling(q):
        for name in ("own", "left", "right", "across"):
            shared[name, q].wait_recv()

    gram(z2, c, yl, x)
    gram(zl, c, yl, x)
    gram_part(c, xl)
    gram_part(c, xr)
    arrive(0)
    for q in range(1, 4):
        shared["same", q].wait_recv()
    for q in range(1, 4):
        gram(plus(z, q), oc, yl, x)
    gram_part(oc, xl)
    gram_part(oc, xr)
    row_id = lax.broadcasted_iota(jnp.int32, (chunk, chunk), 0)
    col_id = lax.broadcasted_iota(jnp.int32, (chunk, chunk), 1)
    wt[z, c, yl, x] = jnp.where(row_id == col_id, jnp.zeros((), BF16), wt[z, c, yl, x])
    arrive(1)
    sibling(0)
    for cp in slab_fwd:
        cp.wait_recv()

    def gram_other(q, parts):
        for part in parts:
            for cc in (c, oc):
                gram(plus(z, q), cc, oyl, part)

    gram_part(c, x2)
    gram_part(oc, x2)
    gram_other(0, (x2,))
    arrive(2)
    sibling(1)
    sibling(2)
    gram_other(1, (x2,))
    gram_other(2, (x2,))

    blocks = [(plus(z, q), cc, yy) for q in range(4) for yy in (yl, oyl) for cc in (0, 1)]

    def products(tiles, over, start=None):
        accs = [jnp.zeros((pair, chunk), F32) for _ in tiles] if start is None else start
        for f, cc, yy in over:
            for i, (part, k) in enumerate(tiles):
                accs[i] = accs[i] + lax.dot_general(
                    zi[f, cc, yy, plus(z, k)].reshape(pair, chunk),
                    wt[f, cc, yy, part],
                    (((1,), (1,)), ((), ())),
                    preferred_element_type=F32,
                )
        return accs

    def keep(slot, value):
        part_out[slot] = value.astype(BF16).reshape(2, local_rows, chunk)

    def send_parts(slot):
        right = copy(part_out.at[slot], part_in.at[slot], dev(x_=xr))
        left = copy(part_out.at[slot + 1], part_in.at[slot + 1], dev(x_=xl))
        return right, left

    def send_halves(slot):
        return [
            [copy(part_out.at[i, p], part_in.at[i, p], dev(x_=to)) for p in (oyh, yh)]
            for i, to in ((slot, xr), (slot + 1, xl))
        ]

    def taken(slot):
        return part_in[slot].astype(F32).reshape(pair, chunk)

    turn = [(x2, 2), (x2, 0)]
    for i, acc in enumerate(products(turn, blocks[:14])):
        own[i] = acc
    arrive(3)
    sibling(3)
    gram_other(3, (x2,))
    for i, acc in enumerate(products(turn, blocks[14:], [own[i] for i in range(2)])):
        keep(i, acc)
    r, l = {}, {}
    r[0], l[0] = send_parts(0)
    a, b = products([(x2, 1), (x2, 3)], blocks)
    keep(2, a)
    keep(3, b)
    r[1], l[1] = send_parts(2)
    for q in range(4):
        gram_other(q, (xl, xr))
    a, b = products([(xr, 0), (xl, 2)], blocks)
    keep(4, a)
    keep(5, b)
    r[2], l[2] = send_parts(4)
    a, b = products([(xr, 3), (xl, 1)], blocks)
    keep(6, a)
    keep(7, b)
    r[3], l[3] = send_parts(6)
    a, b = products([(xr, 2), (xl, 0)], blocks)
    r[0].wait_recv()
    l[0].wait_recv()
    keep(8, a + taken(0))
    keep(9, b + taken(1))
    r[4], l[4] = send_halves(8)
    a, b = products([(xr, 1), (xl, 3)], blocks)
    r[1].wait_recv()
    l[1].wait_recv()
    keep(10, a + taken(2))
    keep(11, b + taken(3))
    r[5], l[5] = send_halves(10)
    for q in range(4):
        gram_other(q, (x,))

    for cp in square_copies:
        cp.wait_recv()
    variance = jnp.zeros((2, cols), F32)
    for d in range(8):
        variance = variance + squares[d]
    spread = jnp.sqrt(variance / (n_rows - 1) + DEVIATION_FLOOR)
    pull = jnp.where(spread < 1.0, -(VARIANCE_WEIGHT * n_rows / (2.0 * (n_rows - 1))) / spread, 0.0)
    written = []

    def write(src, dst):
        cp = pltpu.make_async_copy(src, dst, ls.at[2 + len(written)])
        cp.start()
        written.append(cp)

    for i, (value, ref) in enumerate(
        ((mean[0:1, :], mean_a), (mean[1:2, :], mean_b), (pull[0:1, :], pull_a), (pull[1:2, :], pull_b))
    ):
        coefs[i] = value
        write(coefs.at[i], ref)

    for k in (2, 1):
        a, b = products([(x, k), (x, (k + 2) % 4)], blocks)
        own[k] = a
        own[(k + 2) % 4] = b
    back = []

    def give(k, which, straight, summed, far):
        zq = plus(z, k)
        p = (oyh, yh)[which]
        far[which].wait_recv()
        rows = pl.ds(pl.multiple_of(p * local_rows, local_rows), local_rows)
        total = own[k, rows, :] + (part_in[straight, p].astype(F32) + part_in[summed, p].astype(F32))
        rows_out[zq, p] = total.astype(BF16)
        if k or not which:
            back.append((copy(rows_out.at[zq, p], rows_in.at[yh, z], dev(yh_=p, z_=zq)), p, plus(z, -k)))
        else:
            rows_in[yh, z] = rows_out[z, yh]

    l[2].wait_recv()
    r[2].wait_recv()
    for which in (0, 1):
        give(2, which, 5, 8, r[4])
        give(0, which, 4, 9, l[4])
    l[3].wait_recv()
    r[3].wait_recv()
    for which in (0, 1):
        give(1, which, 7, 10, r[5])
        give(3, which, 6, 11, l[5])
    def write_rows(v, f):
        write(rows_in.at[v, f], cov.at[v, :, pl.ds(pl.multiple_of(f * chunk, chunk), chunk)])

    write_rows(yh, z)
    for cp, v, f in back:
        cp.wait_recv()
        write_rows(v, f)
    for cp in written:
        cp.wait()
    for cp in sent:
        cp.wait_send()


def on_device(z_a, z_b):
    rows, cols = z_a.shape
    chunk = cols // 4
    hbm = pl.BlockSpec(memory_space=pl.ANY)
    cov, mean_a, mean_b, pull_a, pull_b = pl.pallas_call(
        kernel,
        out_shape=[jax.ShapeDtypeStruct((2, rows, cols), BF16), *[jax.ShapeDtypeStruct((1, cols), F32)] * 4],
        in_specs=[hbm, hbm],
        out_specs=[hbm] * 5,
        scratch_shapes=[
            pltpu.VMEM((rows, cols), F32),
            pltpu.VMEM((rows, cols), F32),
            pltpu.VMEM((4, 1, cols), F32),
            pltpu.VMEM((8, 2, cols), F32),
            pltpu.VMEM((8, 2, cols), F32),
            pltpu.VMEM((4, 2, 2, 4, 2, rows, chunk), BF16),
            pltpu.VMEM((4, rows, chunk), BF16),
            pltpu.VMEM((4, 4, chunk, 2 * rows), BF16),
            pltpu.VMEM((4, 2, 2, 4, chunk, chunk), BF16),
            pltpu.VMEM((12, 2, rows, chunk), BF16),
            pltpu.VMEM((12, 2, rows, chunk), BF16),
            pltpu.VMEM((4, 2 * rows, chunk), F32),
            pltpu.VMEM((4, 2, rows, chunk), BF16),
            pltpu.VMEM((2, 4, rows, chunk), BF16),
            pltpu.SemaphoreType.DMA((14,)),
            pltpu.SemaphoreType.DMA((N_COPIES,)),
            pltpu.SemaphoreType.DMA((N_COPIES,)),
        ],
        compiler_params=pltpu.CompilerParams(collective_id=0, has_side_effects=True, vmem_limit_bytes=56 * 1024 * 1024),
        name="vicreg",
    )(z_a, z_b)
    difference = INVARIANCE_WEIGHT * (z_a - z_b)
    dz_a = difference + pull_a * (z_a - mean_a) + cov[0].astype(F32)
    dz_b = pull_b * (z_b - mean_b) - difference + cov[1].astype(F32)
    return dz_a, dz_b


def solution(mesh):
    specs = (P("dp", "mp"), P("dp", "mp"))
    return jax.shard_map(on_device, mesh=mesh, in_specs=specs, out_specs=specs, check_vma=False)
```

```python
import jax
import jax.numpy as jnp
from jax import lax
from jax.experimental import pallas as pl
from jax.experimental.pallas import tpu as pltpu
from jax.sharding import PartitionSpec as P

INVARIANCE_WEIGHT = 25.0
VARIANCE_WEIGHT = 25.0
DEVIATION_FLOOR = 0.0001
HUBER_EDGE = 0.05

MESH = pl.DeviceIdType.MESH
F32 = jnp.float32
BF16 = jnp.bfloat16
N_COPIES = 136


def kernel(za_hbm, zb_hbm, cov, mean_a, mean_b, pull_a, pull_b, za, zb, sums, squares, zi, stage, jt, wt, part_out, part_in, own, rows_out, rows_in, ls, ss, rs):
    dp = lax.axis_index("dp")
    mp = lax.axis_index("mp")
    yh, z = dp // 4, dp % 4
    x, yl, c = mp // 4, (mp // 2) % 2, mp % 2
    local_rows, cols = za.shape
    chunk = cols // 4
    n_rows = local_rows * 8
    pair = 2 * local_rows

    def dev(yh_=None, z_=None, x_=None, yl_=None, c_=None):
        yh_ = yh if yh_ is None else yh_
        z_ = z if z_ is None else z_
        x_ = x if x_ is None else x_
        yl_ = yl if yl_ is None else yl_
        c_ = c if c_ is None else c_
        return (yh_ * 4 + z_, x_ * 4 + yl_ * 2 + c_)

    def plus(v, k):
        return (v + (k % 4)) % 4

    sent = []

    def copy(src, dst, device):
        i = len(sent)
        cp = pltpu.make_async_remote_copy(
            src_ref=src, dst_ref=dst, send_sem=ss.at[i], recv_sem=rs.at[i], device_id=device, device_id_type=MESH
        )
        cp.start()
        sent.append(cp)
        return cp

    zl, zr, z2 = plus(z, -1), plus(z, 1), plus(z, 2)
    xl, xr, x2 = plus(x, -1), plus(x, 1), plus(x, 2)
    oyh, oyl, oc = 1 - yh, 1 - yl, 1 - c
    dp_peers = [(a, b) for a in range(2) for b in range(4) if a or b]

    def peer(a, b):
        return oyh if a else yh, plus(z, b)

    partners = [dev(yh_=peer(a, b)[0], z_=peer(a, b)[1]) for a, b in dp_peers]
    partners += [dev(yl_=oyl), dev(yh_=oyh, yl_=oyl), dev(x_=xl), dev(x_=xr), dev(c_=oc)]
    barrier = pltpu.get_barrier_semaphore()
    for partner in partners:
        pl.semaphore_signal(barrier, inc=1, device_id=partner, device_id_type=MESH)

    loads = [pltpu.make_async_copy(za_hbm, za, ls.at[0]), pltpu.make_async_copy(zb_hbm, zb, ls.at[1])]
    for load in loads:
        load.start()

    for v, ref in enumerate((za, zb)):
        loads[v].wait()
        sums[dp, v : v + 1, :] = jnp.sum(ref[...], axis=0, keepdims=True)
    pl.semaphore_wait(barrier, len(partners))
    def to_peers(ref):
        return [copy(ref, ref, dev(yh_=peer(a, b)[0], z_=peer(a, b)[1])) for a, b in dp_peers]

    for cp in to_peers(sums.at[dp]):
        cp.wait_recv()

    totals = jnp.zeros((2, cols), F32)
    for d in range(8):
        totals = totals + sums[d]
    mean = totals * (1.0 / n_rows)

    first = yh == 0
    for f in range(4):
        cut = slice(f * chunk, (f + 1) * chunk)
        ca = (za[:, cut] - mean[0:1, cut]).astype(BF16)
        cb = (zb[:, cut] - mean[1:2, cut]).astype(BF16)
        zi[f, c, yl, z, yh] = jnp.where(first, ca, cb)
        stage[f] = jnp.where(first, cb, ca)

    right_f = [plus(z, k) for k in (1, 2, 3, 0)]
    left_f = [plus(z, k) for k in (-1, 2, 0, 1)]
    from_left_f = [plus(z, k) for k in (0, 1, 2, 3)]
    from_right_f = [plus(z, k) for k in (0, 3, 1, 2)]

    def mine(f, to):
        return copy(zi.at[f, c, yl, z, yh], zi.at[f, c, yl, z, yh], dev(z_=to))

    def others(f, to):
        return copy(zi.at[f, c, yl, z, oyh], zi.at[f, c, yl, z, oyh], dev(z_=to))

    y1, y02 = {}, {}
    for k in (0, 1, 3, 2):
        f = plus(z, k)
        y1[k] = copy(stage.at[f], zi.at[f, c, yl, z, yh], dev(yh_=oyh))
    ra, rb, la, lb = {}, {}, {}, {}
    for s in range(4):
        ra[s] = mine(right_f[s], zr)
        la[s] = mine(left_f[s], zl)
    for k in (1, 3, 2, 0):
        f = plus(z, k)
        here = zi.at[f, c, yl, z, yh]
        y02[k] = [copy(here, here, dev(yl_=oyl)), copy(stage.at[f], here, dev(yh_=oyh, yl_=oyl))]

    for v, ref in enumerate((za, zb)):
        centered = ref[...] - mean[v : v + 1, :]
        squares[dp, v : v + 1, :] = jnp.sum(centered * centered, axis=0, keepdims=True)
    square_copies = to_peers(squares.at[dp])

    half = chunk // 2
    slab, slab_fwd = {}, []

    def slab_send(q):
        zq = plus(z, q)
        jt[zq, x] = zi[z, c, yl, zq].reshape(pair, chunk).T
        slab[q] = [copy(jt.at[zq, x], jt.at[zq, x], dev(x_=xr)), copy(jt.at[zq, x], jt.at[zq, x], dev(x_=xl))]

    def slab_forward(q):
        zq = plus(z, q)
        for cp in slab[q]:
            cp.wait_recv()
        lo, hi = pl.ds(0, half), pl.ds(half, half)
        slab_fwd.append(copy(jt.at[zq, xl, lo], jt.at[zq, xl, lo], dev(x_=xr)))
        slab_fwd.append(copy(jt.at[zq, xr, hi], jt.at[zq, xr, hi], dev(x_=xl)))

    def forward_right(f):
        ref = zi.at[f, c, yl, zl, yh]
        return copy(ref, ref, dev(z_=zr))

    def forward_left(f):
        ref = zi.at[f, c, yl, zr, oyh]
        return copy(ref, ref, dev(z_=zl))

    fr, fl = {}, {}
    shared = {}

    def share(key, ref):
        shared[key] = copy(ref, ref, dev(c_=oc))

    y1[0].wait_recv()
    slab_send(0)
    y1[1].wait_recv()
    rb[0] = others(right_f[0], zr)
    ra[1].wait_recv()
    fr[0] = forward_right(from_left_f[1])
    y1[3].wait_recv()
    lb[0] = others(left_f[0], zl)
    y1[2].wait_recv()
    rb[1] = others(right_f[1], zr)
    lb[1] = others(left_f[1], zl)
    lb[2] = others(left_f[2], zl)
    ra[2].wait_recv()
    fr[1] = forward_right(from_left_f[2])

    def to_other(ref):
        return copy(ref, ref, dev(yl_=oyl))

    ra[0].wait_recv()
    rb[0].wait_recv()
    slab_send(-1)
    near_left = to_other(zi.at[z, c, yl, zl])
    la[0].wait_recv()
    lb[0].wait_recv()
    slab_send(1)
    near_right = to_other(zi.at[z, c, yl, zr])
    across = {q: [] for q in range(4)}

    def opposite_mine(q):
        fr[q].wait_recv()
        across[q].append(to_other(zi.at[plus(z, q), c, yl, z2, yh]))

    def opposite_others(q):
        fl[q].wait_recv()
        across[q].append(to_other(zi.at[plus(z, q), c, yl, z2, oyh]))
        share(("same", q), zi.at[plus(z, q), c, yl])

    lb[1].wait_recv()
    fl[0] = forward_left(from_right_f[1])
    lb[3] = others(left_f[3], zl)
    ra[3].wait_recv()
    fr[2] = forward_right(from_left_f[3])
    fl[1] = forward_left(from_right_f[0])
    fr[3] = forward_right(from_left_f[0])
    rb[2] = others(right_f[2], zr)
    rb[3] = others(right_f[3], zr)
    opposite_mine(0)
    lb[2].wait_recv()
    fl[2] = forward_left(from_right_f[2])
    slab_forward(0)
    for s in range(1, 4):
        la[s].wait_recv()
    rb[1].wait_recv()
    opposite_mine(1)
    opposite_others(0)
    slab_send(2)
    lb[3].wait_recv()
    fl[3] = forward_left(from_right_f[3])
    opposite_mine(2)
    opposite_mine(3)

    rc, lc = {}, {}
    right_c = [plus(z, k) for k in (1, 2, 3, 0)]
    left_c = [plus(z, k) for k in (3, 0, 1, 2)]

    def direct(q):
        rc[q] = copy(zi.at[right_c[q], c, oyl, z], zi.at[right_c[q], c, oyl, z], dev(z_=zr))
        lc[q] = copy(zi.at[left_c[q], c, oyl, z], zi.at[left_c[q], c, oyl, z], dev(z_=zl))

    scale = 2.0 * n_rows / (n_rows - 1.0)
    slope = scale / (n_rows - 1.0)
    edge = HUBER_EDGE * scale

    def gram(f, cc, yy, part):
        g = jnp.zeros((chunk, chunk), F32)
        for q in range(4):
            g = g + jnp.dot(jt[q, part], zi[f, cc, yy, q].reshape(pair, chunk), preferred_element_type=F32)
        wt[f, cc, yy, part] = jnp.clip(g * slope, -edge, edge).astype(BF16)

    def gram_part(cc, part):
        for q in range(4):
            gram(plus(z, q), cc, yl, part)

    for k in (2, 0, 3, 1):
        for cp in y02[k]:
            cp.wait_recv()
        share(("own", k), zi.at[plus(z, k), c, oyl, z])
    direct(1)
    slab_forward(-1)
    slab_forward(1)
    rb[2].wait_recv()
    rb[3].wait_recv()
    opposite_others(1)
    direct(2)
    shared["same", 0].wait_recv()
    gram(z, c, yl, x)
    gram(z, oc, yl, x)
    gram(zr, c, yl, x)
    slab_forward(2)
    opposite_others(2)
    direct(3)
    opposite_others(3)

    def arrive(q):
        f = plus(z, q)
        (rc[q] if q else near_left).wait_recv()
        share(("left", q), zi.at[f, c, oyl, zl])
        (lc[q] if q else near_right).wait_recv()
        share(("right", q), zi.at[f, c, oyl, zr])
        for cp in across[q]:
            cp.wait_recv()
        share(("across", q), zi.at[f, c, oyl, z2])

    def sibling(q):
        for name in ("own", "left", "right", "across"):
            shared[name, q].wait_recv()

    gram(z2, c, yl, x)
    gram(zl, c, yl, x)
    gram_part(c, xl)
    gram_part(c, xr)
    arrive(0)
    for q in range(1, 4):
        shared["same", q].wait_recv()
    for q in range(1, 4):
        gram(plus(z, q), oc, yl, x)
    row_id = lax.broadcasted_iota(jnp.int32, (chunk, chunk), 0)
    col_id = lax.broadcasted_iota(jnp.int32, (chunk, chunk), 1)
    wt[z, c, yl, x] = jnp.where(row_id == col_id, jnp.zeros((), BF16), wt[z, c, yl, x])
    arrive(1)
    sibling(0)
    for cp in slab_fwd:
        cp.wait_recv()

    def gram_other(q, parts):
        for part in parts:
            for cc in (c, oc):
                gram(plus(z, q), cc, oyl, part)

    gram_part(c, x2)
    gram_part(oc, x2)
    gram_other(0, (x2,))
    arrive(2)
    sibling(1)
    sibling(2)
    gram_other(1, (x2,))
    gram_other(2, (x2,))

    blocks = [(plus(z, q), cc, yy) for q in range(4) for yy in (yl, oyl) for cc in (0, 1)]

    def products(tiles, over, start=None):
        accs = [jnp.zeros((pair, chunk), F32) for _ in tiles] if start is None else start
        for f, cc, yy in over:
            for i, (part, k) in enumerate(tiles):
                accs[i] = accs[i] + lax.dot_general(
                    zi[f, cc, yy, plus(z, k)].reshape(pair, chunk),
                    wt[f, cc, yy, part],
                    (((1,), (1,)), ((), ())),
                    preferred_element_type=F32,
                )
        return accs

    def keep(slot, value):
        part_out[slot] = value.astype(BF16).reshape(2, local_rows, chunk)

    def send_parts(slot):
        right = copy(part_out.at[slot], part_in.at[slot], dev(x_=xr))
        left = copy(part_out.at[slot + 1], part_in.at[slot + 1], dev(x_=xl))
        return right, left

    def send_halves(slot):
        return [
            [copy(part_out.at[i, p], part_in.at[i, p], dev(x_=to)) for p in (oyh, yh)]
            for i, to in ((slot, xr), (slot + 1, xl))
        ]

    def taken(slot):
        return part_in[slot].astype(F32).reshape(pair, chunk)

    turn = [(x2, 2), (x2, 0)]
    for i, acc in enumerate(products(turn, blocks[:14])):
        own[i] = acc
    arrive(3)
    sibling(3)
    gram_other(3, (x2,))
    for i, acc in enumerate(products(turn, blocks[14:], [own[i] for i in range(2)])):
        keep(i, acc)
    r, l = {}, {}
    r[0], l[0] = send_parts(0)
    a, b = products([(x2, 1), (x2, 3)], blocks)
    keep(2, a)
    keep(3, b)
    r[1], l[1] = send_parts(2)
    gram_part(oc, xl)
    gram_part(oc, xr)
    for q in range(4):
        gram_other(q, (xl, xr))
    a, b = products([(xr, 0), (xl, 2)], blocks)
    keep(4, a)
    keep(5, b)
    r[2], l[2] = send_parts(4)
    a, b = products([(xr, 3), (xl, 1)], blocks)
    keep(6, a)
    keep(7, b)
    r[3], l[3] = send_parts(6)
    a, b = products([(xr, 2), (xl, 0)], blocks)
    r[0].wait_recv()
    l[0].wait_recv()
    keep(8, a + taken(0))
    keep(9, b + taken(1))
    r[4], l[4] = send_halves(8)
    a, b = products([(xr, 1), (xl, 3)], blocks)
    r[1].wait_recv()
    l[1].wait_recv()
    keep(10, a + taken(2))
    keep(11, b + taken(3))
    r[5], l[5] = send_halves(10)
    for q in range(4):
        gram_other(q, (x,))

    for cp in square_copies:
        cp.wait_recv()
    variance = jnp.zeros((2, cols), F32)
    for d in range(8):
        variance = variance + squares[d]
    spread = jnp.sqrt(variance / (n_rows - 1) + DEVIATION_FLOOR)
    pull = jnp.where(spread < 1.0, -(VARIANCE_WEIGHT * n_rows / (2.0 * (n_rows - 1))) / spread, 0.0)
    mean_a[...], mean_b[...] = mean[0:1, :], mean[1:2, :]
    pull_a[...], pull_b[...] = pull[0:1, :], pull[1:2, :]

    for k in (2, 1):
        a, b = products([(x, k), (x, (k + 2) % 4)], blocks)
        own[k] = a
        own[(k + 2) % 4] = b
    back = []

    def give(k, which, straight, summed, far):
        zq = plus(z, k)
        p = (oyh, yh)[which]
        far[which].wait_recv()
        rows = pl.ds(pl.multiple_of(p * local_rows, local_rows), local_rows)
        total = own[k, rows, :] + (part_in[straight, p].astype(F32) + part_in[summed, p].astype(F32))
        rows_out[zq, p] = total.astype(BF16)
        if k or not which:
            back.append(copy(rows_out.at[zq, p], rows_in.at[yh, z], dev(yh_=p, z_=zq)))
        else:
            rows_in[yh, z] = rows_out[z, yh]

    l[2].wait_recv()
    r[2].wait_recv()
    for which in (0, 1):
        give(2, which, 5, 8, r[4])
        give(0, which, 4, 9, l[4])
    l[3].wait_recv()
    r[3].wait_recv()
    for which in (0, 1):
        give(1, which, 7, 10, r[5])
        give(3, which, 6, 11, l[5])
    for cp in back:
        cp.wait_recv()
    for v in range(2):
        for f in range(4):
            cov[v, :, f * chunk : (f + 1) * chunk] = rows_in[v, f]
    for cp in sent:
        cp.wait_send()


def on_device(z_a, z_b):
    rows, cols = z_a.shape
    chunk = cols // 4
    vmem = pl.BlockSpec(memory_space=pltpu.VMEM)
    hbm = pl.BlockSpec(memory_space=pl.ANY)
    cov, mean_a, mean_b, pull_a, pull_b = pl.pallas_call(
        kernel,
        out_shape=[jax.ShapeDtypeStruct((2, rows, cols), BF16), *[jax.ShapeDtypeStruct((1, cols), F32)] * 4],
        in_specs=[hbm, hbm],
        out_specs=[vmem] * 5,
        scratch_shapes=[
            pltpu.VMEM((rows, cols), F32),
            pltpu.VMEM((rows, cols), F32),
            pltpu.VMEM((8, 2, cols), F32),
            pltpu.VMEM((8, 2, cols), F32),
            pltpu.VMEM((4, 2, 2, 4, 2, rows, chunk), BF16),
            pltpu.VMEM((4, rows, chunk), BF16),
            pltpu.VMEM((4, 4, chunk, 2 * rows), BF16),
            pltpu.VMEM((4, 2, 2, 4, chunk, chunk), BF16),
            pltpu.VMEM((12, 2, rows, chunk), BF16),
            pltpu.VMEM((12, 2, rows, chunk), BF16),
            pltpu.VMEM((4, 2 * rows, chunk), F32),
            pltpu.VMEM((4, 2, rows, chunk), BF16),
            pltpu.VMEM((2, 4, rows, chunk), BF16),
            pltpu.SemaphoreType.DMA((2,)),
            pltpu.SemaphoreType.DMA((N_COPIES,)),
            pltpu.SemaphoreType.DMA((N_COPIES,)),
        ],
        compiler_params=pltpu.CompilerParams(collective_id=0, has_side_effects=True, vmem_limit_bytes=56 * 1024 * 1024),
        name="vicreg",
    )(z_a, z_b)
    difference = INVARIANCE_WEIGHT * (z_a - z_b)
    dz_a = difference + pull_a * (z_a - mean_a) + cov[0].astype(F32)
    dz_b = pull_b * (z_b - mean_b) - difference + cov[1].astype(F32)
    return dz_a, dz_b


def solution(mesh):
    specs = (P("dp", "mp"), P("dp", "mp"))
    return jax.shard_map(on_device, mesh=mesh, in_specs=specs, out_specs=specs, check_vma=False)
```

```python
import jax
import jax.numpy as jnp
from jax import lax
from jax.experimental import pallas as pl
from jax.experimental.pallas import tpu as pltpu
from jax.sharding import PartitionSpec as P

INVARIANCE_WEIGHT = 25.0
VARIANCE_WEIGHT = 25.0
DEVIATION_FLOOR = 0.0001
HUBER_EDGE = 0.05

MESH = pl.DeviceIdType.MESH
F32 = jnp.float32
BF16 = jnp.bfloat16
N_COPIES = 136


def kernel(za_hbm, zb_hbm, cov, mean_a, mean_b, pull_a, pull_b, za, zb, sums, squares, zi, stage, jt, wt, part_out, part_in, own, rows_out, rows_in, ls, ss, rs):
    dp = lax.axis_index("dp")
    mp = lax.axis_index("mp")
    yh, z = dp // 4, dp % 4
    x, yl, c = mp // 4, (mp // 2) % 2, mp % 2
    local_rows, cols = za.shape
    chunk = cols // 4
    n_rows = local_rows * 8
    pair = 2 * local_rows

    def dev(yh_=None, z_=None, x_=None, yl_=None, c_=None):
        yh_ = yh if yh_ is None else yh_
        z_ = z if z_ is None else z_
        x_ = x if x_ is None else x_
        yl_ = yl if yl_ is None else yl_
        c_ = c if c_ is None else c_
        return (yh_ * 4 + z_, x_ * 4 + yl_ * 2 + c_)

    def plus(v, k):
        return (v + (k % 4)) % 4

    sent = []

    def copy(src, dst, device):
        i = len(sent)
        cp = pltpu.make_async_remote_copy(
            src_ref=src, dst_ref=dst, send_sem=ss.at[i], recv_sem=rs.at[i], device_id=device, device_id_type=MESH
        )
        cp.start()
        sent.append(cp)
        return cp

    zl, zr, z2 = plus(z, -1), plus(z, 1), plus(z, 2)
    xl, xr, x2 = plus(x, -1), plus(x, 1), plus(x, 2)
    oyh, oyl, oc = 1 - yh, 1 - yl, 1 - c
    dp_peers = [(a, b) for a in range(2) for b in range(4) if a or b]

    def peer(a, b):
        return oyh if a else yh, plus(z, b)

    partners = [dev(yh_=peer(a, b)[0], z_=peer(a, b)[1]) for a, b in dp_peers]
    partners += [dev(yl_=oyl), dev(yh_=oyh, yl_=oyl), dev(x_=xl), dev(x_=xr), dev(c_=oc)]
    barrier = pltpu.get_barrier_semaphore()
    for partner in partners:
        pl.semaphore_signal(barrier, inc=1, device_id=partner, device_id_type=MESH)

    loads = [pltpu.make_async_copy(za_hbm, za, ls.at[0]), pltpu.make_async_copy(zb_hbm, zb, ls.at[1])]
    for load in loads:
        load.start()

    for v, ref in enumerate((za, zb)):
        loads[v].wait()
        sums[dp, v : v + 1, :] = jnp.sum(ref[...], axis=0, keepdims=True)
    pl.semaphore_wait(barrier, len(partners))
    def to_peers(ref):
        return [copy(ref, ref, dev(yh_=peer(a, b)[0], z_=peer(a, b)[1])) for a, b in dp_peers]

    for cp in to_peers(sums.at[dp]):
        cp.wait_recv()

    totals = jnp.zeros((2, cols), F32)
    for d in range(8):
        totals = totals + sums[d]
    mean = totals * (1.0 / n_rows)

    first = yh == 0
    for f in range(4):
        cut = slice(f * chunk, (f + 1) * chunk)
        ca = (za[:, cut] - mean[0:1, cut]).astype(BF16)
        cb = (zb[:, cut] - mean[1:2, cut]).astype(BF16)
        zi[f, c, yl, z, yh] = jnp.where(first, ca, cb)
        stage[f] = jnp.where(first, cb, ca)

    right_f = [plus(z, k) for k in (1, 2, 3, 0)]
    left_f = [plus(z, k) for k in (-1, 2, 0, 1)]
    from_left_f = [plus(z, k) for k in (0, 1, 2, 3)]
    from_right_f = [plus(z, k) for k in (0, 3, 1, 2)]

    def mine(f, to):
        return copy(zi.at[f, c, yl, z, yh], zi.at[f, c, yl, z, yh], dev(z_=to))

    def others(f, to):
        return copy(zi.at[f, c, yl, z, oyh], zi.at[f, c, yl, z, oyh], dev(z_=to))

    y1, y02 = {}, {}
    for k in (0, 1, 3, 2):
        f = plus(z, k)
        y1[k] = copy(stage.at[f], zi.at[f, c, yl, z, yh], dev(yh_=oyh))
    ra, rb, la, lb = {}, {}, {}, {}
    for s in range(4):
        ra[s] = mine(right_f[s], zr)
        la[s] = mine(left_f[s], zl)
    for k in (1, 3, 2, 0):
        f = plus(z, k)
        here = zi.at[f, c, yl, z, yh]
        y02[k] = [copy(here, here, dev(yl_=oyl)), copy(stage.at[f], here, dev(yh_=oyh, yl_=oyl))]

    for v, ref in enumerate((za, zb)):
        centered = ref[...] - mean[v : v + 1, :]
        squares[dp, v : v + 1, :] = jnp.sum(centered * centered, axis=0, keepdims=True)
    square_copies = to_peers(squares.at[dp])

    half = chunk // 2
    slab, slab_fwd = {}, []

    def slab_send(q):
        zq = plus(z, q)
        jt[zq, x] = zi[z, c, yl, zq].reshape(pair, chunk).T
        slab[q] = [copy(jt.at[zq, x], jt.at[zq, x], dev(x_=xr)), copy(jt.at[zq, x], jt.at[zq, x], dev(x_=xl))]

    def slab_forward(q):
        zq = plus(z, q)
        for cp in slab[q]:
            cp.wait_recv()
        lo, hi = pl.ds(0, half), pl.ds(half, half)
        slab_fwd.append(copy(jt.at[zq, xl, lo], jt.at[zq, xl, lo], dev(x_=xr)))
        slab_fwd.append(copy(jt.at[zq, xr, hi], jt.at[zq, xr, hi], dev(x_=xl)))

    def forward_right(f):
        ref = zi.at[f, c, yl, zl, yh]
        return copy(ref, ref, dev(z_=zr))

    def forward_left(f):
        ref = zi.at[f, c, yl, zr, oyh]
        return copy(ref, ref, dev(z_=zl))

    fr, fl = {}, {}
    shared = {}

    def share(key, ref):
        shared[key] = copy(ref, ref, dev(c_=oc))

    y1[0].wait_recv()
    slab_send(0)
    y1[1].wait_recv()
    rb[0] = others(right_f[0], zr)
    ra[1].wait_recv()
    fr[0] = forward_right(from_left_f[1])
    y1[3].wait_recv()
    lb[0] = others(left_f[0], zl)
    y1[2].wait_recv()
    rb[1] = others(right_f[1], zr)
    lb[1] = others(left_f[1], zl)
    lb[2] = others(left_f[2], zl)
    ra[2].wait_recv()
    fr[1] = forward_right(from_left_f[2])

    def to_other(ref):
        return copy(ref, ref, dev(yl_=oyl))

    ra[0].wait_recv()
    rb[0].wait_recv()
    slab_send(-1)
    near_left = to_other(zi.at[z, c, yl, zl])
    la[0].wait_recv()
    lb[0].wait_recv()
    slab_send(1)
    near_right = to_other(zi.at[z, c, yl, zr])
    across = {q: [] for q in range(4)}

    def opposite_mine(q):
        fr[q].wait_recv()
        across[q].append(to_other(zi.at[plus(z, q), c, yl, z2, yh]))

    def opposite_others(q):
        fl[q].wait_recv()
        across[q].append(to_other(zi.at[plus(z, q), c, yl, z2, oyh]))
        share(("same", q), zi.at[plus(z, q), c, yl])

    lb[1].wait_recv()
    fl[0] = forward_left(from_right_f[1])
    lb[3] = others(left_f[3], zl)
    ra[3].wait_recv()
    fr[2] = forward_right(from_left_f[3])
    fl[1] = forward_left(from_right_f[0])
    fr[3] = forward_right(from_left_f[0])
    rb[2] = others(right_f[2], zr)
    rb[3] = others(right_f[3], zr)
    opposite_mine(0)
    lb[2].wait_recv()
    fl[2] = forward_left(from_right_f[2])
    slab_forward(0)
    for s in range(1, 4):
        la[s].wait_recv()
    rb[1].wait_recv()
    opposite_mine(1)
    opposite_others(0)
    slab_send(2)
    lb[3].wait_recv()
    fl[3] = forward_left(from_right_f[3])
    opposite_mine(2)
    opposite_mine(3)

    rc, lc = {}, {}
    right_c = [plus(z, k) for k in (1, 2, 3, 0)]
    left_c = [plus(z, k) for k in (3, 0, 1, 2)]

    def direct(q):
        rc[q] = copy(zi.at[right_c[q], c, oyl, z], zi.at[right_c[q], c, oyl, z], dev(z_=zr))
        lc[q] = copy(zi.at[left_c[q], c, oyl, z], zi.at[left_c[q], c, oyl, z], dev(z_=zl))

    scale = 2.0 * n_rows / (n_rows - 1.0)
    slope = scale / (n_rows - 1.0)
    edge = HUBER_EDGE * scale

    def gram(f, cc, yy, part):
        g = jnp.zeros((chunk, chunk), F32)
        for q in range(4):
            g = g + jnp.dot(jt[q, part], zi[f, cc, yy, q].reshape(pair, chunk), preferred_element_type=F32)
        wt[f, cc, yy, part] = jnp.clip(g * slope, -edge, edge).astype(BF16)

    def gram_part(cc, part):
        for q in range(4):
            gram(plus(z, q), cc, yl, part)

    for k in (2, 0, 3, 1):
        for cp in y02[k]:
            cp.wait_recv()
        share(("own", k), zi.at[plus(z, k), c, oyl, z])
    direct(1)
    slab_forward(-1)
    slab_forward(1)
    rb[2].wait_recv()
    rb[3].wait_recv()
    opposite_others(1)
    direct(2)
    slab_forward(2)
    opposite_others(2)
    direct(3)
    shared["same", 0].wait_recv()
    gram(z, c, yl, x)
    gram(z, oc, yl, x)
    gram(zr, c, yl, x)
    opposite_others(3)

    def arrive(q):
        f = plus(z, q)
        (rc[q] if q else near_left).wait_recv()
        share(("left", q), zi.at[f, c, oyl, zl])
        (lc[q] if q else near_right).wait_recv()
        share(("right", q), zi.at[f, c, oyl, zr])
        for cp in across[q]:
            cp.wait_recv()
        share(("across", q), zi.at[f, c, oyl, z2])

    def sibling(q):
        for name in ("own", "left", "right", "across"):
            shared[name, q].wait_recv()

    gram(z2, c, yl, x)
    gram(zl, c, yl, x)
    gram_part(c, xl)
    gram_part(c, xr)
    arrive(0)
    for q in range(1, 4):
        shared["same", q].wait_recv()
    for q in range(1, 4):
        gram(plus(z, q), oc, yl, x)
    gram_part(oc, xl)
    gram_part(oc, xr)
    row_id = lax.broadcasted_iota(jnp.int32, (chunk, chunk), 0)
    col_id = lax.broadcasted_iota(jnp.int32, (chunk, chunk), 1)
    wt[z, c, yl, x] = jnp.where(row_id == col_id, jnp.zeros((), BF16), wt[z, c, yl, x])
    arrive(1)
    sibling(0)
    for cp in slab_fwd:
        cp.wait_recv()

    def gram_other(q, parts):
        for part in parts:
            for cc in (c, oc):
                gram(plus(z, q), cc, oyl, part)

    gram_part(c, x2)
    gram_part(oc, x2)
    gram_other(0, (x2,))
    arrive(2)
    sibling(1)
    sibling(2)
    gram_other(1, (x2,))
    gram_other(2, (x2,))

    blocks = [(plus(z, q), cc, yy) for q in range(4) for yy in (yl, oyl) for cc in (0, 1)]

    def products(tiles, over, start=None):
        accs = [jnp.zeros((pair, chunk), F32) for _ in tiles] if start is None else start
        for f, cc, yy in over:
            for i, (part, k) in enumerate(tiles):
                accs[i] = accs[i] + lax.dot_general(
                    zi[f, cc, yy, plus(z, k)].reshape(pair, chunk),
                    wt[f, cc, yy, part],
                    (((1,), (1,)), ((), ())),
                    preferred_element_type=F32,
                )
        return accs

    def keep(slot, value):
        part_out[slot] = value.astype(BF16).reshape(2, local_rows, chunk)

    def send_parts(slot):
        right = copy(part_out.at[slot], part_in.at[slot], dev(x_=xr))
        left = copy(part_out.at[slot + 1], part_in.at[slot + 1], dev(x_=xl))
        return right, left

    def send_halves(slot):
        return [
            [copy(part_out.at[i, p], part_in.at[i, p], dev(x_=to)) for p in (oyh, yh)]
            for i, to in ((slot, xr), (slot + 1, xl))
        ]

    def taken(slot):
        return part_in[slot].astype(F32).reshape(pair, chunk)

    turn = [(x2, 2), (x2, 0)]
    for i, acc in enumerate(products(turn, blocks[:14])):
        own[i] = acc
    arrive(3)
    sibling(3)
    gram_other(3, (x2,))
    for i, acc in enumerate(products(turn, blocks[14:], [own[i] for i in range(2)])):
        keep(i, acc)
    r, l = {}, {}
    r[0], l[0] = send_parts(0)
    a, b = products([(x2, 1), (x2, 3)], blocks)
    keep(2, a)
    keep(3, b)
    r[1], l[1] = send_parts(2)
    for q in range(4):
        gram_other(q, (xl, xr))
    a, b = products([(xr, 0), (xl, 2)], blocks)
    keep(4, a)
    keep(5, b)
    r[2], l[2] = send_parts(4)
    a, b = products([(xr, 3), (xl, 1)], blocks)
    keep(6, a)
    keep(7, b)
    r[3], l[3] = send_parts(6)
    a, b = products([(xr, 2), (xl, 0)], blocks)
    r[0].wait_recv()
    l[0].wait_recv()
    keep(8, a + taken(0))
    keep(9, b + taken(1))
    r[4], l[4] = send_halves(8)
    a, b = products([(xr, 1), (xl, 3)], blocks)
    r[1].wait_recv()
    l[1].wait_recv()
    keep(10, a + taken(2))
    keep(11, b + taken(3))
    r[5], l[5] = send_halves(10)
    for q in range(4):
        gram_other(q, (x,))

    for cp in square_copies:
        cp.wait_recv()
    variance = jnp.zeros((2, cols), F32)
    for d in range(8):
        variance = variance + squares[d]
    spread = jnp.sqrt(variance / (n_rows - 1) + DEVIATION_FLOOR)
    pull = jnp.where(spread < 1.0, -(VARIANCE_WEIGHT * n_rows / (2.0 * (n_rows - 1))) / spread, 0.0)
    mean_a[...], mean_b[...] = mean[0:1, :], mean[1:2, :]
    pull_a[...], pull_b[...] = pull[0:1, :], pull[1:2, :]

    for k in (2, 1):
        a, b = products([(x, k), (x, (k + 2) % 4)], blocks)
        own[k] = a
        own[(k + 2) % 4] = b
    back = []

    def give(k, which, straight, summed, far):
        zq = plus(z, k)
        p = (oyh, yh)[which]
        far[which].wait_recv()
        rows = pl.ds(pl.multiple_of(p * local_rows, local_rows), local_rows)
        total = own[k, rows, :] + (part_in[straight, p].astype(F32) + part_in[summed, p].astype(F32))
        rows_out[zq, p] = total.astype(BF16)
        if k or not which:
            back.append(copy(rows_out.at[zq, p], rows_in.at[yh, z], dev(yh_=p, z_=zq)))
        else:
            rows_in[yh, z] = rows_out[z, yh]

    l[2].wait_recv()
    r[2].wait_recv()
    for which in (0, 1):
        give(2, which, 5, 8, r[4])
        give(0, which, 4, 9, l[4])
    l[3].wait_recv()
    r[3].wait_recv()
    for which in (0, 1):
        give(1, which, 7, 10, r[5])
        give(3, which, 6, 11, l[5])
    for cp in back:
        cp.wait_recv()
    for v in range(2):
        for f in range(4):
            cov[v, :, f * chunk : (f + 1) * chunk] = rows_in[v, f]
    for cp in sent:
        cp.wait_send()


def on_device(z_a, z_b):
    rows, cols = z_a.shape
    chunk = cols // 4
    vmem = pl.BlockSpec(memory_space=pltpu.VMEM)
    hbm = pl.BlockSpec(memory_space=pl.ANY)
    cov, mean_a, mean_b, pull_a, pull_b = pl.pallas_call(
        kernel,
        out_shape=[jax.ShapeDtypeStruct((2, rows, cols), BF16), *[jax.ShapeDtypeStruct((1, cols), F32)] * 4],
        in_specs=[hbm, hbm],
        out_specs=[vmem] * 5,
        scratch_shapes=[
            pltpu.VMEM((rows, cols), F32),
            pltpu.VMEM((rows, cols), F32),
            pltpu.VMEM((8, 2, cols), F32),
            pltpu.VMEM((8, 2, cols), F32),
            pltpu.VMEM((4, 2, 2, 4, 2, rows, chunk), BF16),
            pltpu.VMEM((4, rows, chunk), BF16),
            pltpu.VMEM((4, 4, chunk, 2 * rows), BF16),
            pltpu.VMEM((4, 2, 2, 4, chunk, chunk), BF16),
            pltpu.VMEM((12, 2, rows, chunk), BF16),
            pltpu.VMEM((12, 2, rows, chunk), BF16),
            pltpu.VMEM((4, 2 * rows, chunk), F32),
            pltpu.VMEM((4, 2, rows, chunk), BF16),
            pltpu.VMEM((2, 4, rows, chunk), BF16),
            pltpu.SemaphoreType.DMA((2,)),
            pltpu.SemaphoreType.DMA((N_COPIES,)),
            pltpu.SemaphoreType.DMA((N_COPIES,)),
        ],
        compiler_params=pltpu.CompilerParams(collective_id=0, has_side_effects=True, vmem_limit_bytes=56 * 1024 * 1024),
        name="vicreg",
    )(z_a, z_b)
    difference = INVARIANCE_WEIGHT * (z_a - z_b)
    dz_a = difference + pull_a * (z_a - mean_a) + cov[0].astype(F32)
    dz_b = pull_b * (z_b - mean_b) - difference + cov[1].astype(F32)
    return dz_a, dz_b


def solution(mesh):
    specs = (P("dp", "mp"), P("dp", "mp"))
    return jax.shard_map(on_device, mesh=mesh, in_specs=specs, out_specs=specs, check_vma=False)
```
